32 devices in a mesh: row: 8 (over z, y), col: 4 (over x, core).
Axes of the slice: x: 2, y: 2, z: 4, core: 2. Of those that a mesh axis runs over, the one named last changes fastest.
Arguments:
- feats: bfloat16 [32, 16, 128, 512], P('row', 'col'), may hold values from -20 to 20
- virt_emb: bfloat16 [4, 512], replicated, may hold values from -18 to 18
- w_query: bfloat16 [512, 512], replicated, may hold values from -1 to 1
- w_key: bfloat16 [512, 512], replicated, may hold values from -1 to 1
- w_value: bfloat16 [512, 512], replicated, may hold values from -0.25 to 0.25
- w_out: bfloat16 [512, 512], replicated, may hold values from -0.25 to 0.25
- link_mask: int32 [32, 16, 4], P('row', 'col'), may hold values 0 or 1
- partners: int32 [32, 16, 4], P('row', 'col'), may hold values from 0 to 511, as said below
- virt_ids: int32 [32, 16, 128], P('row', 'col'), may hold values from 0 to 3
Outputs:
- node_out: bfloat16 [32, 16, 128, 512], P('row', 'col')
- virt_out: float32 [4, 512], replicated
The draws below stay inside these ranges and needn't reach their ends.
Inputs may be any that keep to these rules, and one draw needn't show every extreme that they name: For every m, partners[., ., m] is a perfect matching of the blocks: the partner of a block lies on another device, and the partner's entry for m names the block back. Counted over all 4 matchings, the blocks of one device have at most 3 partners on any one device, and exactly 3 on some device.
All inputs are finite; a program needn't handle non-finite values. No bound on the sum of `link_mask` on one device may be relied on, other than what follows from the above.
Results may differ from the reference program's by a relative error of at most 0.0077.
Values may be sent and summed in bfloat16 or wider, within the bound.
No kernel may reach another device: no remote copies, remote signals or barrier semaphores. Data moves between devices by JAX's collectives and lax.ppermute only.
A program may use at most 192 MiB of HBM per device.

```python
import math
import jax
import jax.numpy as jnp
from jax import lax

D = 512
H = 8
HD = 64
BLK = 128
BX = 4
BY = 4
NEXP = 4
NVIRT = 4
GBX = 32
GBY = 16


def virtual_table(key):
    return jax.random.randint(jax.random.fold_in(key, 7), (GBX, GBY, BLK), 0, NVIRT).astype(jnp.int32)


def virtual_base(key):
    return jax.random.normal(jax.random.fold_in(key, 5), (NVIRT, D), jnp.float32)


def query_base(key):
    return jnp.clip(jax.random.normal(jax.random.fold_in(key, 3), (D, D), jnp.float32), -4.0, 4.0) / math.sqrt(D)


def draw_virt_ids(key, part):
    return virtual_table(key)


def draw_virt_emb(key, part):
    base = virtual_base(key)
    return jnp.clip(base, -4.0, 4.0).astype(jnp.bfloat16)


def draw_w_query(key, part):
    return query_base(key).astype(jnp.bfloat16)


def draw_w_key(key, part):
    other = jnp.clip(jax.random.normal(jax.random.fold_in(key, 4), (D, D), jnp.float32), -4.0, 4.0) / math.sqrt(D)
    return other.astype(jnp.bfloat16)


def draw_feats(key, part):
    shape = (GBX, GBY, BLK, D)
    column_scales = 0.3 * jnp.exp(math.log(10.0) * jax.random.uniform(jax.random.fold_in(key, 1), (1, 1, 1, D), jnp.float32))
    return (jnp.clip(jax.random.normal(jax.random.fold_in(key, 2), shape, jnp.float32), -4.0, 4.0) * column_scales).astype(jnp.bfloat16)


def draw_partners(key, part):
    grid_rows = GBX // BX
    grid_cols = GBY // BY
    devices = grid_rows * grid_cols
    nblocks = BX * BY
    slot_count = nblocks * NEXP
    labels = jax.random.permutation(jax.random.fold_in(key, 11), devices).astype(jnp.int32)
    inverse = jnp.zeros((devices,), jnp.int32).at[labels].set(jnp.arange(devices, dtype=jnp.int32))
    masks = 1 + jax.random.permutation(jax.random.fold_in(key, 12), slot_count).astype(jnp.int32) % (devices - 1)
    first = lax.broadcasted_iota(jnp.int32, (GBX, GBY, NEXP), 0)
    second = lax.broadcasted_iota(jnp.int32, (GBX, GBY, NEXP), 1)
    matching = lax.broadcasted_iota(jnp.int32, (GBX, GBY, NEXP), 2)
    device = first // BX * grid_cols + second // BY
    slot_index = matching * nblocks + first % BX * BY + second % BY
    other = inverse[jnp.bitwise_xor(labels[device], masks[slot_index])]
    return ((other // grid_cols * BX + first % BX) * GBY + other % grid_cols * BY + second % BY).astype(jnp.int32)


def place_ends(drawn, stream_key, smallest, top_value):
    longest = drawn.shape.index(max(drawn.shape))
    spots = []
    for shift in (0, 1):
        where = [jax.random.randint(jax.random.fold_in(stream_key, axis), (), 0, length) for axis, length in enumerate(drawn.shape)]
        where[longest] = (where[longest] + shift) % drawn.shape[longest]
        spots.append(tuple(where))
    return drawn.at[spots[0]].set(smallest).at[spots[1]].set(top_value)


def scatter_about(own_key, shape, spread, bound, kind=jnp.bfloat16):
    values = spread * jax.random.normal(own_key, shape, jnp.float32)
    return jnp.clip(values, min=-bound, max=bound).astype(kind)


def setup_inputs(seed: int = 0) -> dict:
    keys = jax.random.split(jax.random.key(seed), 10)
    feats = draw_feats(jax.random.fold_in(keys[9], 71), 0)
    virt_emb = draw_virt_emb(jax.random.fold_in(keys[9], 71), 0)
    w_query = draw_w_query(jax.random.fold_in(keys[9], 71), 0)
    w_key = draw_w_key(jax.random.fold_in(keys[9], 71), 0)
    w_value = scatter_about(keys[4], (D, D), D ** -0.5, 0.25)
    w_out = scatter_about(keys[5], (D, D), D ** -0.5, 0.25)
    link_mask = place_ends((jax.random.randint(keys[6], (GBX, GBY, 4), 0, 4) < 3).astype(jnp.int32), jax.random.fold_in(keys[6], 1), 0, 1)
    partners = draw_partners(jax.random.fold_in(keys[9], 71), 0)
    virt_ids = draw_virt_ids(jax.random.fold_in(keys[9], 71), 0)
    return {"feats": feats, "virt_emb": virt_emb, "w_query": w_query, "w_key": w_key, "w_value": w_value, "w_out": w_out, "link_mask": link_mask, "partners": partners, "virt_ids": virt_ids}


NEG_FILL = -1e+30

def project_rows(matrix, weight):
    return jnp.dot(matrix, weight, preferred_element_type=jnp.float32).astype(jnp.bfloat16)

def reference(feats, virt_emb, w_query, w_key, w_value, w_out, link_mask, partners, virt_ids):
    scale = 1.0 / math.sqrt(HD)
    flat = feats.reshape(GBX * GBY * BLK, D)
    queries = project_rows(flat, w_query).reshape(GBX, GBY, BLK, H, HD)
    key_grid = project_rows(flat, w_key).reshape(GBX, GBY, BLK, H, HD)
    value_grid = project_rows(flat, w_value).reshape(GBX, GBY, BLK, H, HD)
    key_list = key_grid.reshape(GBX * GBY, BLK, H, HD)
    value_list = value_grid.reshape(GBX * GBY, BLK, H, HD)
    virtual_query = project_rows(virt_emb, w_query).astype(jnp.float32).reshape(NVIRT, H, HD)
    virtual_keys = project_rows(virt_emb, w_key).astype(jnp.float32).reshape(NVIRT, H, HD)
    virtual_values = project_rows(virt_emb, w_value).astype(jnp.float32).reshape(NVIRT, H, HD)
    columns = jnp.arange(GBY, dtype=jnp.int32)
    key_count = (5 + NEXP) * BLK

    def neighbours(grid, grid_row):
        here = lax.dynamic_index_in_dim(grid, grid_row, 0, keepdims=False)
        upper = lax.dynamic_index_in_dim(grid, jnp.maximum(grid_row - 1, 0), 0, keepdims=False)
        lower = lax.dynamic_index_in_dim(grid, jnp.minimum(grid_row + 1, GBX - 1), 0, keepdims=False)
        return [here, upper, lower, jnp.roll(here, 1, axis=0), jnp.roll(here, -1, axis=0)]

    def node_row(grid_row):
        links = lax.dynamic_index_in_dim(link_mask, grid_row, 0, keepdims=False) == 1
        chosen = lax.dynamic_index_in_dim(partners, grid_row, 0, keepdims=False)
        live = jnp.concatenate([jnp.ones((GBY, 1), bool), (links[:, 0] & (grid_row > 0))[:, None], (links[:, 1] & (grid_row < GBX - 1))[:, None], (links[:, 2] & (columns > 0))[:, None], (links[:, 3] & (columns < GBY - 1))[:, None], jnp.ones((GBY, NEXP), bool)], axis=1)
        key_sets = jnp.concatenate([jnp.stack(neighbours(key_grid, grid_row), axis=1), key_list[chosen]], axis=1)
        value_sets = jnp.concatenate([jnp.stack(neighbours(value_grid, grid_row), axis=1), value_list[chosen]], axis=1)
        key_flat = key_sets.reshape(GBY, key_count, H, HD).astype(jnp.float32)
        value_flat = value_sets.reshape(GBY, key_count, H, HD).astype(jnp.float32)
        query_row = lax.dynamic_index_in_dim(queries, grid_row, 0, keepdims=False).astype(jnp.float32)
        scores = jnp.einsum('bqhd,bkhd->bhqk', query_row, key_flat) * scale
        key_live = jnp.repeat(live, BLK, axis=1)
        scores = jnp.where(key_live[:, None, None, :], scores, NEG_FILL)
        node_ids = lax.dynamic_index_in_dim(virt_ids, grid_row, 0, keepdims=False)
        virtual_score = jnp.transpose(lax.optimization_barrier(jnp.sum(query_row * virtual_keys[node_ids], axis=-1)), (0, 2, 1)) * scale
        top = jnp.maximum(lax.optimization_barrier(jnp.max(scores, axis=-1)), virtual_score)
        shares = jnp.exp(scores - top[..., None])
        virtual_share = jnp.exp(virtual_score - top)
        total = lax.optimization_barrier(jnp.sum(shares, axis=-1)) + virtual_share
        weights = (shares / total[..., None]).astype(jnp.bfloat16)
        virtual_weight = (virtual_share / total).astype(jnp.bfloat16)
        context = jnp.einsum('bhqk,bkhd->bqhd', weights.astype(jnp.float32), value_flat)
        context = context + jnp.transpose(virtual_weight.astype(jnp.float32), (0, 2, 1))[..., None] * virtual_values[node_ids]
        context = context.astype(jnp.bfloat16).reshape(GBY * BLK, D)
        residual = lax.dynamic_index_in_dim(feats, grid_row, 0, keepdims=False).reshape(GBY * BLK, D).astype(jnp.float32)
        mixed = residual + jnp.dot(context, w_out, preferred_element_type=jnp.float32)
        return mixed.astype(jnp.bfloat16).reshape(GBY, BLK, D)
    node_out = lax.map(node_row, jnp.arange(GBX, dtype=jnp.int32))

    def virtual_row(grid_row):
        node_keys = lax.dynamic_index_in_dim(key_grid, grid_row, 0, keepdims=False).astype(jnp.float32).reshape(GBY * BLK, H, HD)
        return jnp.einsum('vhd,nhd->vhn', virtual_query, node_keys) * scale
    all_scores = lax.map(virtual_row, jnp.arange(GBX, dtype=jnp.int32))
    slots_v = jnp.arange(NVIRT, dtype=jnp.int32)
    membership = virt_ids.reshape(GBX, 1, 1, GBY * BLK) == slots_v[None, :, None, None]
    all_scores = jnp.where(membership, all_scores, NEG_FILL)
    own_score = lax.optimization_barrier(jnp.sum(virtual_query * virtual_keys, axis=-1)) * scale
    top = jnp.maximum(lax.optimization_barrier(jnp.max(all_scores, axis=(0, 3))), own_score)

    def virtual_sums(carry, grid_row):
        total, accum = carry
        row_scores = lax.dynamic_index_in_dim(all_scores, grid_row, 0, keepdims=False)
        row_members = lax.dynamic_index_in_dim(membership, grid_row, 0, keepdims=False)
        shares = jnp.where(row_members, jnp.exp(row_scores - top[..., None]), 0.0)
        row_values = lax.dynamic_index_in_dim(value_grid, grid_row, 0, keepdims=False).astype(jnp.float32).reshape(GBY * BLK, H, HD)
        accum = accum + jnp.einsum('vhn,nhd->vhd', shares, row_values, precision=lax.Precision.HIGHEST)
        return ((total + lax.optimization_barrier(jnp.sum(shares, axis=-1)), accum), None)
    start = (jnp.zeros((NVIRT, H), jnp.float32), jnp.zeros((NVIRT, H, HD), jnp.float32))
    (total, accum), _ = lax.scan(virtual_sums, start, jnp.arange(GBX, dtype=jnp.int32))
    own_share = jnp.exp(own_score - top)
    total = total + own_share
    accum = accum + own_share[..., None] * virtual_values
    virtual_context = (accum / total[..., None]).astype(jnp.bfloat16).reshape(NVIRT, D)
    virt_out = virt_emb.astype(jnp.float32) + jnp.dot(virtual_context, w_out, preferred_element_type=jnp.float32)
    return (node_out, virt_out)
```

```python
import math

import jax
import jax.numpy as jnp
from jax import lax
from jax.experimental import pallas as pl
from jax.experimental.pallas import tpu as pltpu
from jax.sharding import Mesh
from jax.sharding import PartitionSpec as P

D = 512
H = 8
HD = 64
BLK = 128
NEXP = 4
NVIRT = 4

NEG_FILL = -1e30
LAYERS = 4
NEAREST = ((0, 1, 2, 3), (1, 2, 0, 3), (2, 1, 3, 0), (3, 2, 1, 0))
VMEM_LIMIT = 56 * 1024 * 1024
AXES = ("outer", "inner", "col")


def fold_entry(b, s, q_ref, k_ref, vt_ref, m_ref, l_ref, acc_ref):
    low = lax.broadcasted_iota(jnp.int32, (BLK, 2 * HD), 1) < HD
    zero = jnp.zeros((), jnp.bfloat16)
    columns = pl.ds(pl.multiple_of(s * BLK, BLK), BLK)
    scores = []
    tops = []
    for pair in range(H // 2):
        lanes = slice(pair * 2 * HD, (pair + 1) * 2 * HD)
        query = q_ref[b, :, lanes]
        both = jnp.concatenate([jnp.where(low, query, zero), jnp.where(low, zero, query)], axis=0)
        score = lax.dot_general(
            k_ref[s, :, lanes],
            both,
            (((1,), (1,)), ((), ())),
            preferred_element_type=jnp.float32,
        )
        scores.append(score)
        top = jnp.max(score, axis=0, keepdims=True)
        tops += [top[:, :BLK], top[:, BLK:]]
    m_old = m_ref[b]
    m_new = jnp.maximum(m_old, jnp.concatenate(tops, axis=0))
    alpha = jnp.exp(m_old - m_new)
    m_ref[b] = m_new
    sums = []
    for h in range(H):
        score = scores[h // 2][:, (h % 2) * BLK : (h % 2 + 1) * BLK]
        share = jnp.exp(score - m_new[h : h + 1])
        sums.append(jnp.sum(share, axis=0, keepdims=True))
        rows = slice(h * HD, (h + 1) * HD)
        part = jnp.dot(
            vt_ref[rows, columns], share.astype(jnp.bfloat16), preferred_element_type=jnp.float32
        )
        acc_ref[b, rows, :] = acc_ref[b, rows, :] * alpha[h : h + 1] + part
    l_ref[b] = l_ref[b] * alpha + jnp.concatenate(sums, axis=0)


def fold_range(phase, bounds, blocks, slots, q_ref, k_ref, vt_ref, m_ref, l_ref, acc_ref):
    def step(entry, carry):
        fold_entry(blocks[entry], slots[entry], q_ref, k_ref, vt_ref, m_ref, l_ref, acc_ref)
        return carry

    lax.fori_loop(bounds[phase], bounds[phase + 1], step, 0)


def attend_kernel(
    phase, bounds, blocks, slots, q_ref, k_ref, vt_ref, m_in, l_in, acc_in, m_ref, l_ref, acc_ref
):
    pltpu.sync_copy(acc_in, acc_ref)
    m_ref[...] = m_in[...]
    l_ref[...] = l_in[...]
    fold_range(phase, bounds, blocks, slots, q_ref, k_ref, vt_ref, m_ref, l_ref, acc_ref)


def finish_kernel(
    phase,
    bounds,
    blocks,
    slots,
    q_ref,
    k_ref,
    vt_ref,
    m_in,
    l_in,
    acc_in,
    feats_ref,
    w_ref,
    out_ref,
    m_ref,
    l_ref,
    acc_ref,
):
    pltpu.sync_copy(acc_in, acc_ref)
    m_ref[...] = m_in[...]
    l_ref[...] = l_in[...]
    fold_range(phase, bounds, blocks, slots, q_ref, k_ref, vt_ref, m_ref, l_ref, acc_ref)

    def project(b, carry):
        inverse = 1.0 / l_ref[b]
        context = jnp.concatenate(
            [
                acc_ref[b, h * HD : (h + 1) * HD, :] * inverse[h : h + 1]
                for h in range(H)
            ],
            axis=0,
        ).astype(jnp.bfloat16)
        mixed = lax.dot_general(
            context, w_ref[...], (((0,), (0,)), ((), ())), preferred_element_type=jnp.float32
        )
        out_ref[b] = (feats_ref[b].astype(jnp.float32) + mixed).astype(jnp.bfloat16)
        return carry

    lax.fori_loop(0, out_ref.shape[0], project, 0)


VMEM = pl.BlockSpec(memory_space=pltpu.VMEM)
SMEM = pl.BlockSpec(memory_space=pltpu.SMEM)
HBM = pl.BlockSpec(memory_space=pl.ANY)


def attend(phase, entries, expected, q, k, vt, state):
    def kernel(*refs):
        attend_kernel(phase, *refs)

    cost = pl.CostEstimate(
        flops=expected * BLK * BLK * D * 8, bytes_accessed=18 << 20, transcendentals=0
    )
    return pl.pallas_call(
        kernel,
        in_specs=[SMEM] * 3 + [VMEM] * 5 + [HBM],
        out_specs=[VMEM] * 3,
        out_shape=[jax.ShapeDtypeStruct(part.shape, part.dtype) for part in state],
        compiler_params=pltpu.CompilerParams(vmem_limit_bytes=VMEM_LIMIT),
        cost_estimate=cost,
        name=f"attend_{phase}",
    )(*entries, q, k, vt, *state)


def finish(phase, entries, expected, q, k, vt, state, feats, w_out):
    def kernel(*refs):
        finish_kernel(phase, *refs)

    cost = pl.CostEstimate(
        flops=expected * BLK * BLK * D * 8, bytes_accessed=18 << 20, transcendentals=0
    )
    return pl.pallas_call(
        kernel,
        in_specs=[SMEM] * 3 + [VMEM] * 5 + [HBM] + [VMEM] * 2,
        out_specs=VMEM,
        out_shape=jax.ShapeDtypeStruct(feats.shape, feats.dtype),
        scratch_shapes=[pltpu.VMEM(part.shape, part.dtype) for part in state],
        compiler_params=pltpu.CompilerParams(vmem_limit_bytes=VMEM_LIMIT),
        cost_estimate=cost,
        name=f"finish_{phase}",
    )(*entries, q, k, vt, *state, feats, w_out)


def project(rows, weight):
    return jnp.dot(rows, weight, preferred_element_type=jnp.float32).astype(jnp.bfloat16)


def project_transposed(rows, weight):
    return lax.dot_general(
        weight, rows, (((0,), (1,)), ((), ())), preferred_element_type=jnp.float32
    ).astype(jnp.bfloat16)


def per_head(vectors):
    head = jnp.arange(D, dtype=jnp.int32)[None, None, :] // HD
    mine = head == jnp.arange(H, dtype=jnp.int32)[None, :, None]
    return jnp.where(mine, vectors[:, None, :], jnp.zeros((), vectors.dtype)).reshape(NVIRT * H, D)


def pick(index, choices):
    result = choices[-1]
    for place in range(len(choices) - 2, -1, -1):
        result = jnp.where(index == place, choices[place], result)
    return result


def steps_up(first):
    return [(z, z + 1) for z in range(first, LAYERS - 1)]


def steps_down(first):
    return [(LAYERS - 1 - z, LAYERS - 2 - z) for z in range(first, LAYERS - 1)]


def shards(feats, virt_emb, w_query, w_key, w_value, w_out, link_mask, partners, virt_ids):
    blocks_x, blocks_y = (feats.shape[0], feats.shape[1])
    nblocks = blocks_x * blocks_y
    rows_total = nblocks * BLK
    scale = 1.0 / math.sqrt(HD)
    inner = lax.axis_size("inner")
    cols = lax.axis_size("col")
    mesh_rows = LAYERS * inner
    peers = inner * cols
    devices = LAYERS * peers
    layer = lax.axis_index("outer")
    my_row = layer * inner + lax.axis_index("inner")
    my_col = lax.axis_index("col")
    flat = feats.reshape(rows_total, D)
    own = feats.reshape(nblocks, BLK, D)

    slot_count = nblocks * NEXP
    capacity = (slot_count + devices - 2) // (devices - 1)
    grid_cols = blocks_y * cols
    grid_rows = blocks_x * mesh_rows
    partner_ids = jnp.transpose(partners, (2, 0, 1)).reshape(slot_count)
    partner_row = partner_ids // grid_cols
    partner_col = partner_ids % grid_cols
    dest = partner_row // blocks_x * cols + partner_col // blocks_y
    partner_slot = partner_row % blocks_x * blocks_y + partner_col % blocks_y
    order = jnp.arange(slot_count, dtype=jnp.int32)
    own_slot = order % nblocks
    recv_order = order // nblocks * nblocks + partner_slot
    same_dest = dest[:, None] == dest[None, :]
    rank_out = jnp.sum(same_dest & (order[None, :] < order[:, None]), axis=1)
    rank_in = jnp.sum(same_dest & (recv_order[None, :] < recv_order[:, None]), axis=1)
    target = dest * capacity + rank_out
    hits = target[None, :] == jnp.arange(devices * capacity, dtype=jnp.int32)[:, None]
    wanted = jnp.sum(jnp.where(hits, own_slot[None, :], 0), axis=1).astype(jnp.int32)
    wanted = wanted.reshape(LAYERS, peers * capacity)

    around = [wanted] + [
        lax.ppermute(wanted, "outer", [((z + turn) % LAYERS, z) for z in range(LAYERS)])
        for turn in range(1, LAYERS)
    ]

    def table(step):
        turns = [
            around[(NEAREST[z][step] - z) % LAYERS][z] for z in range(LAYERS)
        ]
        return pick(layer, turns)

    def hand_round(source, step):
        sent = jnp.take(source, table(step), axis=0, mode="clip")
        got = lax.all_to_all(
            sent.reshape(peers, capacity * BLK, D), ("inner", "col"), 0, 0, tiled=True
        )
        return got.reshape(peers * capacity * BLK, D)

    up1 = lax.ppermute(own, "outer", steps_up(0))
    down1 = lax.ppermute(own, "outer", steps_down(0))
    up2 = lax.ppermute(up1, "outer", steps_up(1))
    down2 = lax.ppermute(down1, "outer", steps_down(1))
    up3 = lax.ppermute(up2, "outer", steps_up(2))
    down3 = lax.ppermute(down2, "outer", steps_down(2))
    arrived = [
        hand_round(own, 0),
        hand_round(pick(layer, [down1, down1, up1, up1]), 1),
        hand_round(pick(layer, [down2, up1, down1, up2]), 2),
        hand_round(pick(layer, [down3, down2, up2, up3]), 3),
    ]

    rows_axes = ("outer", "inner")
    to_next_row = [(r, r + 1) for r in range(mesh_rows - 1)]
    to_prev_row = [(r + 1, r) for r in range(mesh_rows - 1)]
    to_next_col = [(c, c + 1) for c in range(cols - 1)]
    to_prev_col = [(c + 1, c) for c in range(cols - 1)]
    halo = jnp.concatenate(
        [
            lax.ppermute(feats[-1], rows_axes, to_next_row),
            lax.ppermute(feats[0], rows_axes, to_prev_row),
            lax.ppermute(feats[:, -1], "col", to_next_col),
            lax.ppermute(feats[:, 0], "col", to_prev_col),
        ],
        axis=0,
    ).reshape(-1, D)

    block = jnp.arange(nblocks, dtype=jnp.int32)
    bx = block // blocks_y
    by = block % blocks_y
    global_row = my_row * blocks_x + bx
    global_col = my_col * blocks_y + by
    links = link_mask.reshape(nblocks, 4) == 1
    north = jnp.where(bx > 0, block - blocks_y, by)
    south = jnp.where(bx < blocks_x - 1, block + blocks_y, blocks_y + by)
    west = jnp.where(by > 0, block - 1, 2 * blocks_y + bx)
    east = jnp.where(by < blocks_y - 1, block + 1, 2 * blocks_y + blocks_x + bx)
    dead = 2 + LAYERS
    near_slots = jnp.concatenate([block, north, south, west, east])
    near_phase = jnp.concatenate(
        [
            jnp.zeros((nblocks,), jnp.int32),
            jnp.where(links[:, 0] & (global_row > 0), jnp.where(bx > 0, 0, 1), dead),
            jnp.where(
                links[:, 1] & (global_row < grid_rows - 1),
                jnp.where(bx < blocks_x - 1, 0, 1),
                dead,
            ),
            jnp.where(links[:, 2] & (global_col > 0), jnp.where(by > 0, 0, 1), dead),
            jnp.where(
                links[:, 3] & (global_col < grid_cols - 1),
                jnp.where(by < blocks_y - 1, 0, 1),
                dead,
            ),
        ]
    )
    from_layer = dest // peers
    steps = [
        pick(from_layer, [jnp.int32(NEAREST[z].index(origin)) for origin in range(LAYERS)])
        for z in range(LAYERS)
    ]
    far_phase = 2 + pick(layer, steps)
    far_slots = dest % peers * capacity + rank_in
    entry_block = jnp.concatenate([jnp.tile(block, 5), own_slot])
    entry_slot = jnp.concatenate([near_slots, far_slots])
    entry_phase = jnp.concatenate([near_phase, far_phase])
    count = entry_block.shape[0]
    number = jnp.arange(count, dtype=jnp.int32)
    sort_key = entry_phase * count + number
    place = jnp.sum(sort_key[None, :] < sort_key[:, None], axis=1)
    at_place = place[None, :] == number[:, None]
    sorted_block = jnp.sum(jnp.where(at_place, entry_block[None, :], 0), axis=1).astype(jnp.int32)
    sorted_slot = jnp.sum(jnp.where(at_place, entry_slot[None, :], 0), axis=1).astype(jnp.int32)
    bounds = jnp.sum(
        entry_phase[None, :] < jnp.arange(dead + 1, dtype=jnp.int32)[:, None], axis=1
    ).astype(jnp.int32)
    entries = (bounds, sorted_block, sorted_slot)

    queries = project(flat, w_query)
    scaled = (queries * jnp.bfloat16(scale)).reshape(nblocks, BLK, D)
    keys = project(flat, w_key)
    values_t = project_transposed(flat, w_value)
    virtual_query = project(virt_emb, w_query)
    virtual_keys = project(virt_emb, w_key)
    virtual_values = project(virt_emb, w_value)

    slots_v = jnp.arange(NVIRT, dtype=jnp.int32)
    chosen = virt_ids.reshape(1, nblocks, BLK) == slots_v[:, None, None]
    virtual_score = lax.dot_general(
        per_head(virtual_keys),
        scaled.reshape(rows_total, D),
        (((1,), (1,)), ((), ())),
        preferred_element_type=jnp.float32,
    ).reshape(NVIRT, H, nblocks, BLK)
    m0 = jnp.transpose(jnp.sum(jnp.where(chosen[:, None], virtual_score, 0.0), axis=0), (1, 0, 2))
    acc0 = jnp.sum(
        jnp.where(
            chosen[:, :, None, :],
            virtual_values.astype(jnp.float32)[:, None, :, None],
            0.0,
        ),
        axis=0,
    )
    state = (m0, jnp.ones_like(m0), acc0)

    member = chosen.reshape(NVIRT, 1, rows_total)
    node_scores = lax.dot_general(
        per_head(virtual_query), keys, (((1,), (1,)), ((), ())), preferred_element_type=jnp.float32
    ).reshape(NVIRT, H, rows_total) * scale
    node_scores = jnp.where(member, node_scores, NEG_FILL)
    local_top = jnp.max(node_scores, axis=-1)
    shares = jnp.where(member, jnp.exp(node_scores - local_top[..., None]), 0.0)
    local_total = jnp.sum(shares, axis=-1)
    weighted = lax.dot_general(
        shares.reshape(NVIRT * H, rows_total),
        values_t.astype(jnp.float32),
        (((1,), (1,)), ((), ())),
        precision=lax.Precision.HIGHEST,
        preferred_element_type=jnp.float32,
    ).reshape(NVIRT, H, H, HD)
    same_head = jnp.arange(H)[:, None] == jnp.arange(H)[None, :]
    local_accum = jnp.sum(jnp.where(same_head[None, :, :, None], weighted, 0.0), axis=2)
    packed = jnp.concatenate(
        [
            local_accum.reshape(NVIRT * H, HD),
            jnp.broadcast_to(local_top.reshape(NVIRT * H, 1), (NVIRT * H, HD // 2)),
            jnp.broadcast_to(local_total.reshape(NVIRT * H, 1), (NVIRT * H, HD // 2)),
        ],
        axis=1,
    )
    parts = lax.all_gather(packed, AXES)

    state = attend(0, entries, 45, scaled, keys.reshape(nblocks, BLK, D), values_t, state)
    state = attend(
        1,
        entries,
        12,
        scaled,
        project(halo, w_key).reshape(-1, BLK, D),
        project_transposed(halo, w_value),
        state,
    )
    for step in range(LAYERS):
        remote_keys = project(arrived[step], w_key).reshape(-1, BLK, D)
        remote_values = project_transposed(arrived[step], w_value)
        if step < LAYERS - 1:
            state = attend(2 + step, entries, 16, scaled, remote_keys, remote_values, state)
        else:
            node_out = finish(
                2 + step, entries, 16, scaled, remote_keys, remote_values, state, own, w_out
            )

    own_score = (
        jnp.sum(
            (virtual_query.astype(jnp.float32) * virtual_keys.astype(jnp.float32)).reshape(
                NVIRT, H, HD
            ),
            axis=-1,
        )
        * scale
    ).reshape(NVIRT * H)
    part_top = parts[:, :, HD]
    part_total = parts[:, :, HD + HD // 2]
    final_top = jnp.maximum(jnp.max(part_top, axis=0), own_score)
    rescale = jnp.exp(part_top - final_top)
    own_share = jnp.exp(own_score - final_top)
    total = jnp.sum(part_total * rescale, axis=0) + own_share
    accum = jnp.sum(parts[:, :, :HD] * rescale[..., None], axis=0)
    accum = accum + own_share[:, None] * virtual_values.astype(jnp.float32).reshape(NVIRT * H, HD)
    virtual_context = (accum / total[:, None]).astype(jnp.bfloat16).reshape(NVIRT, D)
    virt_out = virt_emb.astype(jnp.float32) + jnp.dot(
        virtual_context, w_out, preferred_element_type=jnp.float32
    )
    return (node_out.reshape(feats.shape), virt_out)


def solution(mesh):
    inner = mesh.shape["row"] // LAYERS
    split = Mesh(mesh.devices.reshape(LAYERS, inner, mesh.shape["col"]), AXES)
    rows = ("outer", "inner")
    return jax.shard_map(
        shards,
        mesh=split,
        in_specs=(
            P(rows, "col", None, None),
            P(),
            P(),
            P(),
            P(),
            P(),
            P(rows, "col", None),
            P(rows, "col", None),
            P(rows, "col", None),
        ),
        out_specs=(P(rows, "col", None, None), P()),
        check_vma=False,
    )
```

```python
import math

import jax
import jax.numpy as jnp
from jax import lax
from jax.experimental import pallas as pl
from jax.experimental.pallas import tpu as pltpu
from jax.sharding import Mesh
from jax.sharding import PartitionSpec as P

D = 512
H = 8
HD = 64
BLK = 128
NEXP = 4
NVIRT = 4

NEG_FILL = -1e30
LAYERS = 4
NEAREST = ((0, 1, 2, 3), (1, 2, 0, 3), (2, 1, 3, 0), (3, 2, 1, 0))
VMEM_LIMIT = 56 * 1024 * 1024
AXES = ("outer", "inner", "col")
TABLE_ROWS = 16


def fold_entry(b, s, q_ref, k_ref, vt_ref, m_ref, l_ref, acc_ref):
    low = lax.broadcasted_iota(jnp.int32, (BLK, 2 * HD), 1) < HD
    zero = jnp.zeros((), jnp.bfloat16)
    columns = pl.ds(pl.multiple_of(s * BLK, BLK), BLK)
    scores = []
    tops = []
    for pair in range(H // 2):
        lanes = slice(pair * 2 * HD, (pair + 1) * 2 * HD)
        query = q_ref[b, :, lanes]
        both = jnp.concatenate([jnp.where(low, query, zero), jnp.where(low, zero, query)], axis=0)
        score = lax.dot_general(
            k_ref[s, :, lanes],
            both,
            (((1,), (1,)), ((), ())),
            preferred_element_type=jnp.float32,
        )
        scores.append(score)
        top = jnp.max(score, axis=0, keepdims=True)
        tops += [top[:, :BLK], top[:, BLK:]]
    m_old = m_ref[b]
    m_new = jnp.maximum(m_old, jnp.concatenate(tops, axis=0))
    alpha = jnp.exp(m_old - m_new)
    m_ref[b] = m_new
    sums = []
    for h in range(H):
        score = scores[h // 2][:, (h % 2) * BLK : (h % 2 + 1) * BLK]
        share = jnp.exp(score - m_new[h : h + 1])
        sums.append(jnp.sum(share, axis=0, keepdims=True))
        rows = slice(h * HD, (h + 1) * HD)
        part = jnp.dot(
            vt_ref[rows, columns], share.astype(jnp.bfloat16), preferred_element_type=jnp.float32
        )
        acc_ref[b, rows, :] = acc_ref[b, rows, :] * alpha[h : h + 1] + part
    l_ref[b] = l_ref[b] * alpha + jnp.concatenate(sums, axis=0)


def fold_range(low, high, blocks, slots, first, q_ref, k_ref, vt_ref, m_ref, l_ref, acc_ref):
    def fold(entry):
        slot = entry - first if slots is None else slots[entry]
        fold_entry(blocks[entry], slot, q_ref, k_ref, vt_ref, m_ref, l_ref, acc_ref)

    def two(step, carry):
        fold(low + 2 * step)
        fold(low + 2 * step + 1)
        return carry

    def one(entry, carry):
        fold(entry)
        return carry

    pairs = (high - low) // 2
    lax.fori_loop(0, pairs, two, 0)
    lax.fori_loop(low + 2 * pairs, high, one, 0)


def open_kernel(span, bounds, blocks, slots, q_ref, k_ref, vt_ref, ids_ref, vv_ref, m_in, *refs):
    m_ref, l_ref, acc_ref = refs[-3:]
    m_ref[...] = m_in[...]
    l_ref[...] = jnp.ones(l_ref.shape, jnp.float32)

    def open_block(b, carry):
        ids = ids_ref[pl.ds(b, 1), :]
        value = jnp.zeros((D, BLK), jnp.float32)
        for v in range(NVIRT):
            value = jnp.where(ids == v, vv_ref[:, v : v + 1], value)
        acc_ref[b] = value
        return carry

    lax.fori_loop(0, q_ref.shape[0], open_block, 0)
    low, high = span(bounds)
    fold_range(low, high, blocks, slots, 0, q_ref, k_ref, vt_ref, m_ref, l_ref, acc_ref)


def near_kernel(span, bounds, blocks, slots, q_ref, k_ref, vt_ref, m_in, l_in, acc_in, *refs):
    m_ref, l_ref, acc_ref = refs[-3:]
    pltpu.sync_copy(acc_in, acc_ref)
    m_ref[...] = m_in[...]
    l_ref[...] = l_in[...]
    low, high = span(bounds)
    fold_range(low, high, blocks, slots, 0, q_ref, k_ref, vt_ref, m_ref, l_ref, acc_ref)


GROUP = 4


def phase_kernel(phase, finish, ntokens, *refs):
    refs = list(refs)
    take = lambda count: [refs.pop(0) for _ in range(count)]
    bounds, blocks, slots = take(3)
    (source,) = take(1)
    wk_hbm, wv_hbm, q_hbm, m_hbm, l_hbm, acc_hbm = take(6)
    feats_hbm, wo_hbm = take(2) if finish else (None, None)
    take(ntokens)
    if finish:
        (out_hbm,) = take(1)
        m_ref, l_ref, acc_ref = take(3)
        feats_ref, wo_ref, out_ref, out_sems = take(4)
    else:
        m_ref, l_ref, acc_ref = take(3)
    raw_ref, wk_ref, wv_ref, q_ref, k_ref, vt_ref, sems = take(7)
    copies = []

    def fetch(source, target):
        copy = pltpu.make_async_copy(source, target, sems.at[len(copies)])
        copy.start()
        copies.append(copy)

    rows_in = raw_ref.shape[0] // source.shape[0]
    for peer in range(source.shape[0]):
        fetch(source.at[peer, pl.ds(0, rows_in)], raw_ref.at[pl.ds(peer * rows_in, rows_in)])
    fetch(wk_hbm, wk_ref)
    fetch(wv_hbm, wv_ref)
    needed = len(copies)
    fetch(q_hbm, q_ref)
    fetch(m_hbm, m_ref)
    fetch(l_hbm, l_ref)
    fetch(acc_hbm, acc_ref)
    if finish:
        fetch(feats_hbm, feats_ref)
        fetch(wo_hbm, wo_ref)
    for copy in copies[:needed]:
        copy.wait()
    low = bounds[phase]
    high = bounds[phase + 1]

    def project_group(group, carry):
        entries = [jnp.minimum(low + group * GROUP + u, high - 1) for u in range(GROUP)]
        rows = jnp.concatenate(
            [
                raw_ref[pl.ds(pl.multiple_of(slots[entry] * BLK, BLK), BLK), :]
                for entry in entries
            ],
            axis=0,
        )
        keys = jnp.dot(rows, wk_ref[...], preferred_element_type=jnp.float32)
        k_ref[pl.ds(group * GROUP, GROUP)] = keys.astype(jnp.bfloat16).reshape(GROUP, BLK, D)
        values = lax.dot_general(
            wv_ref[...], rows, (((1,), (1,)), ((), ())), preferred_element_type=jnp.float32
        )
        columns = pl.ds(pl.multiple_of(group * (GROUP * BLK), GROUP * BLK), GROUP * BLK)
        vt_ref[:, columns] = values.astype(jnp.bfloat16)
        return carry

    lax.fori_loop(0, (high - low + GROUP - 1) // GROUP, project_group, 0)
    for copy in copies[needed:]:
        copy.wait()
    fold_range(low, high, blocks, None, low, q_ref, k_ref, vt_ref, m_ref, l_ref, acc_ref)
    if not finish:
        return
    nblocks = q_ref.shape[0]

    def write(b):
        return pltpu.make_async_copy(out_ref.at[b], out_hbm.at[b], out_sems.at[b])

    def finish_block(b, carry):
        inverse = 1.0 / l_ref[b]
        context = jnp.concatenate(
            [acc_ref[b, h * HD : (h + 1) * HD, :] * inverse[h : h + 1] for h in range(H)], axis=0
        ).astype(jnp.bfloat16)
        mixed = lax.dot_general(
            context, wo_ref[...], (((0,), (0,)), ((), ())), preferred_element_type=jnp.float32
        )
        out_ref[b] = (feats_ref[b].astype(jnp.float32) + mixed).astype(jnp.bfloat16)
        write(b).start()
        return carry

    def settle(b, carry):
        write(b).wait()
        return carry

    lax.fori_loop(0, nblocks, finish_block, 0)
    lax.fori_loop(0, nblocks, settle, 0)


def pack_kernel(candidates, capacity, nsources, layer, wanted, *refs):
    sources = refs[:nsources]
    extra = refs[nsources]
    out_ref, sems = refs[-2:]
    peers = out_ref.shape[0]
    count = peers * capacity

    def block(source, slot):
        return source.at[pl.ds(pl.multiple_of(slot * BLK, BLK), BLK)]

    def place(index):
        return out_ref.at[index // capacity, pl.ds(index % capacity * BLK, BLK)]

    for which in sorted(set(candidates)):
        mine = [layer[0] == z for z in range(LAYERS) if candidates[z] == which]
        chosen = mine[0]
        for other in mine[1:]:
            chosen = jnp.logical_or(chosen, other)

        @pl.when(chosen)
        def start(source=sources[which]):
            for index in range(count):
                pltpu.make_async_copy(
                    block(source, wanted[index]), place(index), sems.at[index]
                ).start()

    rest = out_ref.shape[1] - capacity * BLK
    if rest:
        for peer in range(peers):
            out_ref[peer, capacity * BLK :, :] = extra[...]
    for index in range(count):
        pltpu.make_async_copy(block(sources[0], 0), place(index), sems.at[index]).wait()


VMEM = pl.BlockSpec(memory_space=pltpu.VMEM)
SMEM = pl.BlockSpec(memory_space=pltpu.SMEM)
HBM = pl.BlockSpec(memory_space=pl.ANY)


COST = pl.CostEstimate(flops=1, bytes_accessed=1, transcendentals=0)


def state_shapes(nblocks):
    return [
        jax.ShapeDtypeStruct((nblocks, H, BLK), jnp.float32),
        jax.ShapeDtypeStruct((nblocks, H, BLK), jnp.float32),
        jax.ShapeDtypeStruct((nblocks, D, BLK), jnp.float32),
    ]


def attend_near(name, span, entries, q, k, vt, state, opening, tokens):
    if state is None:
        body, rest, specs = open_kernel, opening, [VMEM] * len(opening)
    else:
        body, rest, specs = near_kernel, state, [VMEM, VMEM, HBM]

    def kernel(*refs):
        body(span, *refs)

    return pl.pallas_call(
        kernel,
        in_specs=[SMEM] * 3 + [VMEM] * 3 + specs + [HBM] * len(tokens),
        out_specs=[VMEM] * 3,
        out_shape=state_shapes(q.shape[0]),
        compiler_params=pltpu.CompilerParams(vmem_limit_bytes=VMEM_LIMIT),
        cost_estimate=COST,
        name=name,
    )(*entries, q, k, vt, *rest, *tokens)


def attend_phase(phase, entries, source, slots, w_key, w_value_t, q, state, tokens, last=None):
    room = -(-slots // GROUP) * GROUP
    finish = last is not None
    nblocks = q.shape[0]
    block = pltpu.VMEM((nblocks, BLK, D), jnp.bfloat16)
    square = pltpu.VMEM((D, D), jnp.bfloat16)
    shapes = state_shapes(nblocks)
    scratch = [
        pltpu.VMEM((slots * BLK, D), jnp.bfloat16),
        square,
        square,
        block,
        pltpu.VMEM((room, BLK, D), jnp.bfloat16),
        pltpu.VMEM((D, room * BLK), jnp.bfloat16),
        pltpu.SemaphoreType.DMA((source.shape[0] + 8,)),
    ]
    if finish:
        scratch = (
            [pltpu.VMEM(shape.shape, shape.dtype) for shape in shapes]
            + [block, square, block, pltpu.SemaphoreType.DMA((nblocks,))]
            + scratch
        )
    extra = list(last) if finish else []

    def kernel(*refs):
        phase_kernel(phase, finish, len(tokens), *refs)

    return pl.pallas_call(
        kernel,
        in_specs=[SMEM] * 3 + [HBM] * (7 + len(extra) + len(tokens)),
        out_specs=HBM if finish else [VMEM] * 3,
        out_shape=jax.ShapeDtypeStruct((nblocks, BLK, D), jnp.bfloat16) if finish else shapes,
        scratch_shapes=scratch,
        compiler_params=pltpu.CompilerParams(vmem_limit_bytes=VMEM_LIMIT),
        cost_estimate=COST,
        name=f"attend_{phase}",
    )(*entries, source, w_key, w_value_t, q, *state, *extra, *tokens)


def pack(candidates, capacity, layer, wanted, sources, extra, tokens):
    peers = wanted.shape[0] // capacity
    rows = capacity * BLK + (0 if extra is None else extra.shape[0])

    def kernel(*refs):
        pack_kernel(candidates, capacity, len(sources), *refs)

    return pl.pallas_call(
        kernel,
        in_specs=[SMEM] * 2 + [HBM] * len(sources) + [VMEM] * (extra is not None) + [HBM] * len(tokens),
        out_specs=VMEM,
        out_shape=jax.ShapeDtypeStruct((peers, rows, D), jnp.bfloat16),
        scratch_shapes=[pltpu.SemaphoreType.DMA((peers * capacity,))],
        compiler_params=pltpu.CompilerParams(vmem_limit_bytes=VMEM_LIMIT),
        cost_estimate=COST,
        name="pack",
    )(layer, wanted, *sources, *([] if extra is None else [extra]), *tokens)


def project(rows, weight):
    return jnp.dot(rows, weight, preferred_element_type=jnp.float32).astype(jnp.bfloat16)


def project_transposed(rows, weight):
    return lax.dot_general(
        weight, rows, (((0,), (1,)), ((), ())), preferred_element_type=jnp.float32
    ).astype(jnp.bfloat16)


def per_head(vectors):
    head = jnp.arange(D, dtype=jnp.int32)[None, None, :] // HD
    mine = head == jnp.arange(H, dtype=jnp.int32)[None, :, None]
    return jnp.where(mine, vectors[:, None, :], jnp.zeros((), vectors.dtype)).reshape(NVIRT * H, D)


def pick(index, choices):
    result = choices[-1]
    for place in range(len(choices) - 2, -1, -1):
        result = jnp.where(index == place, choices[place], result)
    return result


def sources_of(step):
    return ((0, 0, 0, 0), (0, 0, 1, 1), (0, 1, 2, 3), (0, 1, 2, 3))[step]


def steps_up(first):
    return [(z, z + 1) for z in range(first, LAYERS - 1)]


def steps_down(first):
    return [(LAYERS - 1 - z, LAYERS - 2 - z) for z in range(first, LAYERS - 1)]


def shards(feats, virt_emb, w_query, w_key, w_value, w_out, link_mask, partners, virt_ids):
    blocks_x, blocks_y = (feats.shape[0], feats.shape[1])
    nblocks = blocks_x * blocks_y
    rows_total = nblocks * BLK
    scale = 1.0 / math.sqrt(HD)
    inner = lax.axis_size("inner")
    cols = lax.axis_size("col")
    mesh_rows = LAYERS * inner
    peers = inner * cols
    devices = LAYERS * peers
    layer = lax.axis_index("outer")
    my_row = layer * inner + lax.axis_index("inner")
    my_col = lax.axis_index("col")
    flat = feats.reshape(rows_total, D)

    slot_count = nblocks * NEXP
    capacity = (slot_count + devices - 2) // (devices - 1)
    grid_cols = blocks_y * cols
    grid_rows = blocks_x * mesh_rows
    order = jnp.arange(slot_count, dtype=jnp.int32)
    own_slot = order % nblocks

    def locate(ids):
        ids = jnp.transpose(ids, (2, 0, 1)).reshape(slot_count)
        row = ids // grid_cols
        col = ids % grid_cols
        device = row // blocks_x * cols + col // blocks_y
        return device, row % blocks_x * blocks_y + col % blocks_y

    def ranks(device, sequence):
        same = device[:, None] == device[None, :]
        return jnp.sum(same & (sequence[None, :] < sequence[:, None]), axis=1)

    dest, partner_slot = locate(partners)
    rank_in = ranks(dest, order // nblocks * nblocks + partner_slot)
    target = dest * capacity + ranks(dest, order)
    hits = target[None, :] == jnp.arange(devices * capacity, dtype=jnp.int32)[:, None]
    wanted = jnp.sum(jnp.where(hits, own_slot[None, :], 0), axis=1).astype(jnp.int32)
    wanted = wanted.reshape(LAYERS, peers * capacity)

    rows = jnp.pad(
        wanted.astype(jnp.bfloat16),
        ((0, TABLE_ROWS - LAYERS), (0, D - peers * capacity)),
    )
    own = jnp.concatenate([flat, rows], axis=0)

    def table(step, sources):
        line = pick(
            layer, [sources[which][rows_total + z] for z, which in enumerate(sources_of(step))]
        )
        return line[: peers * capacity].astype(jnp.int32)

    layer_table = jnp.broadcast_to(layer, (1,)).astype(jnp.int32)

    def hand_round(step, sources, tokens, extra=None):
        slots = pick(layer, list(wanted)) if step == 0 else table(step, sources)
        sent = pack(
            sources_of(step), capacity, layer_table, slots, sources, extra, tokens
        )
        return sent, lax.all_to_all(sent, ("inner", "col"), 0, 0, tiled=True)

    up1 = lax.ppermute(own, "outer", steps_up(0))
    down1 = lax.ppermute(own, "outer", steps_down(0))
    up2 = lax.ppermute(up1, "outer", steps_up(1))
    down2 = lax.ppermute(down1, "outer", steps_down(1))
    up3 = lax.ppermute(up2, "outer", steps_up(2))
    down3 = lax.ppermute(down2, "outer", steps_down(2))

    rows_axes = ("outer", "inner")
    to_next_row = [(r, r + 1) for r in range(mesh_rows - 1)]
    to_prev_row = [(r + 1, r) for r in range(mesh_rows - 1)]
    to_next_col = [(c, c + 1) for c in range(cols - 1)]
    to_prev_col = [(c + 1, c) for c in range(cols - 1)]
    halo_rows = [
        lax.ppermute(feats[-1], rows_axes, to_next_row),
        lax.ppermute(feats[0], rows_axes, to_prev_row),
    ]
    halo_cols = [
        lax.ppermute(feats[:, -1], "col", to_next_col),
        lax.ppermute(feats[:, 0], "col", to_prev_col),
    ]

    block = jnp.arange(nblocks, dtype=jnp.int32)
    bx = block // blocks_y
    by = block % blocks_y
    global_row = my_row * blocks_x + bx
    global_col = my_col * blocks_y + by
    links = link_mask.reshape(nblocks, 4) == 1
    north = jnp.where(bx > 0, block - blocks_y, by)
    south = jnp.where(bx < blocks_x - 1, block + blocks_y, blocks_y + by)
    west = jnp.where(by > 0, block - 1, 2 * blocks_y + bx)
    east = jnp.where(by < blocks_y - 1, block + 1, 2 * blocks_y + blocks_x + bx)
    dead = 2 + LAYERS
    near_slots = jnp.concatenate([block, north, south, west, east])
    near_phase = jnp.concatenate(
        [
            jnp.zeros((nblocks,), jnp.int32),
            jnp.where(links[:, 0] & (global_row > 0), jnp.where(bx > 0, 0, 1), dead),
            jnp.where(
                links[:, 1] & (global_row < grid_rows - 1),
                jnp.where(bx < blocks_x - 1, 0, 1),
                dead,
            ),
            jnp.where(links[:, 2] & (global_col > 0), jnp.where(by > 0, 0, 1), dead),
            jnp.where(
                links[:, 3] & (global_col < grid_cols - 1),
                jnp.where(by < blocks_y - 1, 0, 1),
                dead,
            ),
        ]
    )
    from_layer = dest // peers
    steps = [
        pick(from_layer, [jnp.int32(NEAREST[z].index(origin)) for origin in range(LAYERS)])
        for z in range(LAYERS)
    ]
    far_phase = 2 + pick(layer, steps)
    far_slots = dest % peers * capacity + rank_in
    entry_block = jnp.concatenate([jnp.tile(block, 5), own_slot])
    entry_slot = jnp.concatenate([near_slots, far_slots])
    entry_phase = jnp.concatenate([near_phase, far_phase])
    count = entry_block.shape[0]
    number = jnp.arange(count, dtype=jnp.int32)
    sort_key = entry_phase * count + number
    place = jnp.sum(sort_key[None, :] < sort_key[:, None], axis=1)
    at_place = place[None, :] == number[:, None]
    sorted_block = jnp.sum(jnp.where(at_place, entry_block[None, :], 0), axis=1).astype(jnp.int32)
    sorted_slot = jnp.sum(jnp.where(at_place, entry_slot[None, :], 0), axis=1).astype(jnp.int32)
    bounds = jnp.sum(
        entry_phase[None, :] < jnp.arange(dead + 1, dtype=jnp.int32)[:, None], axis=1
    ).astype(jnp.int32)
    entries = (bounds, sorted_block, sorted_slot)

    sent, first = hand_round(0, [own], [])
    flat, _ = lax.optimization_barrier((flat, sent))

    queries = project(flat, w_query)
    scaled = (queries * jnp.bfloat16(scale)).reshape(nblocks, BLK, D)
    keys = project(flat, w_key)
    values_t = project_transposed(flat, w_value)
    virtual_query = project(virt_emb, w_query)
    virtual_keys = project(virt_emb, w_key)
    virtual_values = project(virt_emb, w_value)

    slots_v = jnp.arange(NVIRT, dtype=jnp.int32)
    chosen = virt_ids.reshape(1, nblocks, BLK) == slots_v[:, None, None]
    virtual_score = lax.dot_general(
        per_head(virtual_keys),
        scaled.reshape(rows_total, D),
        (((1,), (1,)), ((), ())),
        preferred_element_type=jnp.float32,
    ).reshape(NVIRT, H, nblocks, BLK)
    m0 = jnp.transpose(jnp.sum(jnp.where(chosen[:, None], virtual_score, 0.0), axis=0), (1, 0, 2))
    values_wide = jnp.zeros((D, BLK), jnp.float32)
    values_wide = values_wide.at[:, :NVIRT].set(virtual_values.astype(jnp.float32).T)

    member = chosen.reshape(NVIRT, 1, rows_total)
    node_scores = lax.dot_general(
        per_head(virtual_query), keys, (((1,), (1,)), ((), ())), preferred_element_type=jnp.float32
    ).reshape(NVIRT, H, rows_total) * scale
    node_scores = jnp.where(member, node_scores, NEG_FILL)
    local_top = jnp.max(node_scores, axis=-1)
    shares = jnp.where(member, jnp.exp(node_scores - local_top[..., None]), 0.0)
    local_total = jnp.sum(shares, axis=-1)
    weighted = lax.dot_general(
        shares.reshape(NVIRT * H, rows_total),
        values_t.astype(jnp.float32),
        (((1,), (1,)), ((), ())),
        precision=lax.Precision.HIGHEST,
        preferred_element_type=jnp.float32,
    ).reshape(NVIRT, H, H, HD)
    same_head = jnp.arange(H)[:, None] == jnp.arange(H)[None, :]
    local_accum = jnp.sum(jnp.where(same_head[None, :, :, None], weighted, 0.0), axis=2)
    packed = jnp.concatenate(
        [
            local_accum.reshape(NVIRT * H, HD),
            jnp.broadcast_to(local_top.reshape(NVIRT * H, 1), (NVIRT * H, HD // 2)),
            jnp.broadcast_to(local_total.reshape(NVIRT * H, 1), (NVIRT * H, HD // 2)),
        ],
        axis=1,
    )
    planes = []
    left = packed
    for _ in range(3):
        plane = lax.reduce_precision(left, 8, 7)
        planes.append(plane.astype(jnp.bfloat16))
        left = left - plane
    planes = jnp.concatenate(planes + [jnp.zeros_like(planes[0])], axis=1)

    def merge(parts):
        tops = parts[:, :, HD : HD + 1]
        top = jnp.max(tops, axis=0)
        rescale = jnp.exp(tops - top)
        accum = jnp.sum(parts[:, :, :HD] * rescale, axis=0)
        total = jnp.sum(parts[:, :, HD + HD // 2 :] * rescale, axis=0)
        return jnp.concatenate([accum, jnp.broadcast_to(top, (NVIRT * H, HD // 2)), total], axis=1)

    w_value_t = w_value.T
    keys = keys.reshape(nblocks, BLK, D)
    opening = (virt_ids.reshape(nblocks, BLK), values_wide, m0)
    state = attend_near(
        "attend_own_a",
        lambda bounds: (bounds[0], bounds[1] // 3),
        entries,
        scaled,
        keys,
        values_t,
        None,
        opening,
        [sent],
    )

    def phase(step, source, state, tokens, last=None):
        return attend_phase(
            2 + step,
            entries,
            source,
            peers * capacity,
            w_key,
            w_value_t,
            scaled,
            state,
            tokens,
            last,
        )

    sent, second = hand_round(1, [down1, up1], [state[1], *halo_rows], planes)
    state = attend_near(
        "attend_own_b",
        lambda bounds: (bounds[1] // 3, bounds[1]),
        entries,
        scaled,
        keys,
        values_t,
        state,
        None,
        [sent],
    )
    state = phase(0, first, state, [])
    sent, third = hand_round(2, [down2, up1, down1, up2], [state[1], *halo_cols])
    layer_parts = second[:, capacity * BLK :, :].astype(jnp.float32)
    layer_parts = layer_parts.reshape(peers, NVIRT * H, 4, 2 * HD)
    layer_part = merge(layer_parts[:, :, 0] + layer_parts[:, :, 1] + layer_parts[:, :, 2])
    state = phase(1, second, state, [sent])
    around_parts = [layer_part] + [
        lax.ppermute(layer_part, "outer", [((z + turn) % LAYERS, z) for z in range(LAYERS)])
        for turn in range(1, LAYERS)
    ]
    halo = jnp.concatenate(halo_rows + halo_cols, axis=0).reshape(-1, D)
    halo, _ = lax.optimization_barrier((halo, sent))
    state = attend_near(
        "attend_halo",
        lambda bounds: (bounds[1], bounds[2]),
        entries,
        scaled,
        project(halo, w_key).reshape(-1, BLK, D),
        project_transposed(halo, w_value),
        state,
        None,
        [],
    )
    sent, fourth = hand_round(
        3, [down3, down2, up2, up3], [state[1], *around_parts[1:]]
    )
    state = phase(2, third, state, [sent])
    node_out = phase(3, fourth, state, [], (feats.reshape(nblocks, BLK, D), w_out))
    parts = jnp.stack(
        [
            pick(layer, [around_parts[(origin - z) % LAYERS] for z in range(LAYERS)])
            for origin in range(LAYERS)
        ]
    )

    own_score = (
        jnp.sum(
            (virtual_query.astype(jnp.float32) * virtual_keys.astype(jnp.float32)).reshape(
                NVIRT, H, HD
            ),
            axis=-1,
        )
        * scale
    ).reshape(NVIRT * H)
    part_top = parts[:, :, HD]
    part_total = parts[:, :, HD + HD // 2]
    final_top = jnp.maximum(jnp.max(part_top, axis=0), own_score)
    rescale = jnp.exp(part_top - final_top)
    own_share = jnp.exp(own_score - final_top)
    total = jnp.sum(part_total * rescale, axis=0) + own_share
    accum = jnp.sum(parts[:, :, :HD] * rescale[..., None], axis=0)
    accum = accum + own_share[:, None] * virtual_values.astype(jnp.float32).reshape(NVIRT * H, HD)
    virtual_context = (accum / total[:, None]).astype(jnp.bfloat16).reshape(NVIRT, D)
    virt_out = virt_emb.astype(jnp.float32) + jnp.dot(
        virtual_context, w_out, preferred_element_type=jnp.float32
    )
    return (node_out.reshape(feats.shape), virt_out)


def solution(mesh):
    inner = mesh.shape["row"] // LAYERS
    split = Mesh(mesh.devices.reshape(LAYERS, inner, mesh.shape["col"]), AXES)
    rows = ("outer", "inner")
    return jax.shard_map(
        shards,
        mesh=split,
        in_specs=(
            P(rows, "col", None, None),
            P(),
            P(),
            P(),
            P(),
            P(),
            P(rows, "col", None),
            P(rows, "col", None),
            P(rows, "col", None),
        ),
        out_specs=(P(rows, "col", None, None), P()),
        check_vma=False,
    )
```

```python
import math

import jax
import jax.numpy as jnp
from jax import lax
from jax.experimental import pallas as pl
from jax.experimental.pallas import tpu as pltpu
from jax.sharding import Mesh
from jax.sharding import PartitionSpec as P

D = 512
H = 8
HD = 64
BLK = 128
NEXP = 4
NVIRT = 4

NEG_FILL = -1e30
LAYERS = 4
NEAREST = ((0, 1, 2, 3), (1, 2, 0, 3), (2, 1, 3, 0), (3, 2, 1, 0))
VMEM_LIMIT = 56 * 1024 * 1024
AXES = ("outer", "inner", "col")
TABLE_ROWS = 16


def fold_entry(b, s, q_ref, k_ref, vt_ref, m_ref, l_ref, acc_ref):
    low = lax.broadcasted_iota(jnp.int32, (BLK, 2 * HD), 1) < HD
    zero = jnp.zeros((), jnp.bfloat16)
    columns = pl.ds(pl.multiple_of(s * BLK, BLK), BLK)
    scores = []
    tops = []
    for pair in range(H // 2):
        lanes = slice(pair * 2 * HD, (pair + 1) * 2 * HD)
        query = q_ref[b, :, lanes]
        both = jnp.concatenate([jnp.where(low, query, zero), jnp.where(low, zero, query)], axis=0)
        score = lax.dot_general(
            k_ref[s, :, lanes],
            both,
            (((1,), (1,)), ((), ())),
            preferred_element_type=jnp.float32,
        )
        scores.append(score)
        top = jnp.max(score, axis=0, keepdims=True)
        tops += [top[:, :BLK], top[:, BLK:]]
    m_old = m_ref[b]
    m_new = jnp.maximum(m_old, jnp.concatenate(tops, axis=0))
    alpha = jnp.exp(m_old - m_new)
    m_ref[b] = m_new
    sums = []
    for h in range(H):
        score = scores[h // 2][:, (h % 2) * BLK : (h % 2 + 1) * BLK]
        share = jnp.exp(score - m_new[h : h + 1])
        sums.append(jnp.sum(share, axis=0, keepdims=True))
        rows = slice(h * HD, (h + 1) * HD)
        part = jnp.dot(
            vt_ref[rows, columns], share.astype(jnp.bfloat16), preferred_element_type=jnp.float32
        )
        acc_ref[b, rows, :] = acc_ref[b, rows, :] * alpha[h : h + 1] + part
    l_ref[b] = l_ref[b] * alpha + jnp.concatenate(sums, axis=0)


def fold_range(low, high, blocks, slots, first, q_ref, k_ref, vt_ref, m_ref, l_ref, acc_ref):
    def fold(entry):
        slot = entry - first if slots is None else slots[entry]
        fold_entry(blocks[entry], slot, q_ref, k_ref, vt_ref, m_ref, l_ref, acc_ref)

    def two(step, carry):
        fold(low + 2 * step)
        fold(low + 2 * step + 1)
        return carry

    def one(entry, carry):
        fold(entry)
        return carry

    pairs = (high - low) // 2
    lax.fori_loop(0, pairs, two, 0)
    lax.fori_loop(low + 2 * pairs, high, one, 0)


def open_kernel(span, bounds, blocks, slots, q_ref, k_ref, vt_ref, ids_ref, vv_ref, m_in, *refs):
    m_ref, l_ref, acc_ref = refs[-3:]
    m_ref[...] = m_in[...]
    l_ref[...] = jnp.ones(l_ref.shape, jnp.float32)

    def open_block(b, carry):
        ids = ids_ref[pl.ds(b, 1), :]
        value = jnp.zeros((D, BLK), jnp.float32)
        for v in range(NVIRT):
            value = jnp.where(ids == v, vv_ref[:, v : v + 1], value)
        acc_ref[b] = value
        return carry

    lax.fori_loop(0, q_ref.shape[0], open_block, 0)
    low, high = span(bounds)
    fold_range(low, high, blocks, slots, 0, q_ref, k_ref, vt_ref, m_ref, l_ref, acc_ref)


def near_kernel(span, bounds, blocks, slots, q_ref, k_ref, vt_ref, m_in, l_in, acc_in, *refs):
    m_ref, l_ref, acc_ref = refs[-3:]
    pltpu.sync_copy(acc_in, acc_ref)
    m_ref[...] = m_in[...]
    l_ref[...] = l_in[...]
    low, high = span(bounds)
    fold_range(low, high, blocks, slots, 0, q_ref, k_ref, vt_ref, m_ref, l_ref, acc_ref)


GROUP = 4


def phase_kernel(phase, nsources, finish, ntokens, *refs):
    refs = list(refs)
    take = lambda count: [refs.pop(0) for _ in range(count)]
    bounds, blocks, slots = take(3)
    sources = take(nsources)
    wk_hbm, wv_hbm, q_hbm, m_hbm, l_hbm, acc_hbm = take(6)
    feats_hbm, wo_hbm = take(2) if finish else (None, None)
    take(ntokens)
    if finish:
        (out_hbm,) = take(1)
        m_ref, l_ref, acc_ref = take(3)
        feats_ref, wo_ref, out_ref, out_sems = take(4)
    else:
        m_ref, l_ref, acc_ref = take(3)
    raw_ref, wk_ref, wv_ref, q_ref, k_ref, vt_ref, sems = take(7)
    copies = []

    def fetch(source, target):
        copy = pltpu.make_async_copy(source, target, sems.at[len(copies)])
        copy.start()
        copies.append(copy)

    senders = sum(source.shape[0] for source in sources)
    rows_in = raw_ref.shape[0] // senders
    at = 0
    for source in sources:
        for sender in range(source.shape[0]):
            fetch(source.at[sender, pl.ds(0, rows_in)], raw_ref.at[pl.ds(at, rows_in)])
            at += rows_in
    fetch(wk_hbm, wk_ref)
    fetch(wv_hbm, wv_ref)
    needed = len(copies)
    fetch(q_hbm, q_ref)
    fetch(m_hbm, m_ref)
    fetch(l_hbm, l_ref)
    fetch(acc_hbm, acc_ref)
    if finish:
        fetch(feats_hbm, feats_ref)
        fetch(wo_hbm, wo_ref)
    for copy in copies[:needed]:
        copy.wait()
    low = bounds[phase]
    high = bounds[phase + 1]

    def project_group(group, carry):
        entries = [jnp.minimum(low + group * GROUP + u, high - 1) for u in range(GROUP)]
        rows = jnp.concatenate(
            [
                raw_ref[pl.ds(pl.multiple_of(slots[entry] * BLK, BLK), BLK), :]
                for entry in entries
            ],
            axis=0,
        )
        keys = jnp.dot(rows, wk_ref[...], preferred_element_type=jnp.float32)
        k_ref[pl.ds(group * GROUP, GROUP)] = keys.astype(jnp.bfloat16).reshape(GROUP, BLK, D)
        values = lax.dot_general(
            wv_ref[...], rows, (((1,), (1,)), ((), ())), preferred_element_type=jnp.float32
        )
        columns = pl.ds(pl.multiple_of(group * (GROUP * BLK), GROUP * BLK), GROUP * BLK)
        vt_ref[:, columns] = values.astype(jnp.bfloat16)
        return carry

    lax.fori_loop(0, (high - low + GROUP - 1) // GROUP, project_group, 0)
    for copy in copies[needed:]:
        copy.wait()
    fold_range(low, high, blocks, None, low, q_ref, k_ref, vt_ref, m_ref, l_ref, acc_ref)
    if not finish:
        return
    nblocks = q_ref.shape[0]

    def write(b):
        return pltpu.make_async_copy(out_ref.at[b], out_hbm.at[b], out_sems.at[b])

    def finish_block(b, carry):
        inverse = 1.0 / l_ref[b]
        context = jnp.concatenate(
            [acc_ref[b, h * HD : (h + 1) * HD, :] * inverse[h : h + 1] for h in range(H)], axis=0
        ).astype(jnp.bfloat16)
        mixed = lax.dot_general(
            context, wo_ref[...], (((0,), (0,)), ((), ())), preferred_element_type=jnp.float32
        )
        out_ref[b] = (feats_ref[b].astype(jnp.float32) + mixed).astype(jnp.bfloat16)
        write(b).start()
        return carry

    def settle(b, carry):
        write(b).wait()
        return carry

    lax.fori_loop(0, nblocks, finish_block, 0)
    lax.fori_loop(0, nblocks, settle, 0)


def pack_kernel(candidates, capacity, nsources, layer, wanted, *refs):
    sources = refs[:nsources]
    extra = refs[nsources]
    out_ref, sems = refs[-2:]
    peers = out_ref.shape[0]
    count = peers * capacity

    def block(source, slot):
        return source.at[pl.ds(pl.multiple_of(slot * BLK, BLK), BLK)]

    def place(index):
        return out_ref.at[index // capacity, pl.ds(index % capacity * BLK, BLK)]

    for which in sorted(set(candidates)):
        mine = [layer[0] == z for z in range(LAYERS) if candidates[z] == which]
        chosen = mine[0]
        for other in mine[1:]:
            chosen = jnp.logical_or(chosen, other)

        @pl.when(chosen)
        def start(source=sources[which]):
            for index in range(count):
                pltpu.make_async_copy(
                    block(source, wanted[index]), place(index), sems.at[index]
                ).start()

    rest = out_ref.shape[1] - capacity * BLK
    if rest:
        for peer in range(peers):
            out_ref[peer, capacity * BLK :, :] = extra[...]
    for index in range(count):
        pltpu.make_async_copy(block(sources[0], 0), place(index), sems.at[index]).wait()


VMEM = pl.BlockSpec(memory_space=pltpu.VMEM)
SMEM = pl.BlockSpec(memory_space=pltpu.SMEM)
HBM = pl.BlockSpec(memory_space=pl.ANY)


def cost(big):
    return pl.CostEstimate(
        flops=30_000_000_000 if big else 1, bytes_accessed=1, transcendentals=0
    )


def state_shapes(nblocks):
    return [
        jax.ShapeDtypeStruct((nblocks, H, BLK), jnp.float32),
        jax.ShapeDtypeStruct((nblocks, H, BLK), jnp.float32),
        jax.ShapeDtypeStruct((nblocks, D, BLK), jnp.float32),
    ]


def attend_near(name, span, entries, q, k, vt, state, opening, tokens, big=False):
    if state is None:
        body, rest, specs = open_kernel, opening, [VMEM] * len(opening)
    else:
        body, rest, specs = near_kernel, state, [VMEM, VMEM, HBM]

    def kernel(*refs):
        body(span, *refs)

    return pl.pallas_call(
        kernel,
        in_specs=[SMEM] * 3 + [VMEM] * 3 + specs + [HBM] * len(tokens),
        out_specs=[VMEM] * 3,
        out_shape=state_shapes(q.shape[0]),
        compiler_params=pltpu.CompilerParams(vmem_limit_bytes=VMEM_LIMIT),
        cost_estimate=cost(big),
        name=name,
    )(*entries, q, k, vt, *rest, *tokens)


def attend_phase(phase, entries, sources, slots, w_key, w_value_t, q, state, tokens, last=None, big=False):
    room = -(-slots // GROUP) * GROUP
    finish = last is not None
    nblocks = q.shape[0]
    block = pltpu.VMEM((nblocks, BLK, D), jnp.bfloat16)
    square = pltpu.VMEM((D, D), jnp.bfloat16)
    shapes = state_shapes(nblocks)
    scratch = [
        pltpu.VMEM((slots * BLK, D), jnp.bfloat16),
        square,
        square,
        block,
        pltpu.VMEM((room, BLK, D), jnp.bfloat16),
        pltpu.VMEM((D, room * BLK), jnp.bfloat16),
        pltpu.SemaphoreType.DMA((sum(source.shape[0] for source in sources) + 8,)),
    ]
    if finish:
        scratch = (
            [pltpu.VMEM(shape.shape, shape.dtype) for shape in shapes]
            + [block, square, block, pltpu.SemaphoreType.DMA((nblocks,))]
            + scratch
        )
    extra = list(last) if finish else []

    def kernel(*refs):
        phase_kernel(phase, len(sources), finish, len(tokens), *refs)

    return pl.pallas_call(
        kernel,
        in_specs=[SMEM] * 3 + [HBM] * (6 + len(sources) + len(extra) + len(tokens)),
        out_specs=HBM if finish else [VMEM] * 3,
        out_shape=jax.ShapeDtypeStruct((nblocks, BLK, D), jnp.bfloat16) if finish else shapes,
        scratch_shapes=scratch,
        compiler_params=pltpu.CompilerParams(vmem_limit_bytes=VMEM_LIMIT),
        cost_estimate=cost(big),
        name=f"attend_{phase}",
    )(*entries, *sources, w_key, w_value_t, q, *state, *extra, *tokens)


def pack(candidates, capacity, layer, wanted, sources, extra, tokens):
    peers = wanted.shape[0] // capacity
    rows = capacity * BLK + (0 if extra is None else extra.shape[0])

    def kernel(*refs):
        pack_kernel(candidates, capacity, len(sources), *refs)

    return pl.pallas_call(
        kernel,
        in_specs=[SMEM] * 2 + [HBM] * len(sources) + [VMEM] * (extra is not None) + [HBM] * len(tokens),
        out_specs=VMEM,
        out_shape=jax.ShapeDtypeStruct((peers, rows, D), jnp.bfloat16),
        scratch_shapes=[pltpu.SemaphoreType.DMA((peers * capacity,))],
        compiler_params=pltpu.CompilerParams(vmem_limit_bytes=VMEM_LIMIT),
        cost_estimate=cost(False),
        name="pack",
    )(layer, wanted, *sources, *([] if extra is None else [extra]), *tokens)


def project(rows, weight):
    return jnp.dot(rows, weight, preferred_element_type=jnp.float32).astype(jnp.bfloat16)


def project_transposed(rows, weight):
    return lax.dot_general(
        weight, rows, (((0,), (1,)), ((), ())), preferred_element_type=jnp.float32
    ).astype(jnp.bfloat16)


def per_head(vectors):
    head = jnp.arange(D, dtype=jnp.int32)[None, None, :] // HD
    mine = head == jnp.arange(H, dtype=jnp.int32)[None, :, None]
    return jnp.where(mine, vectors[:, None, :], jnp.zeros((), vectors.dtype)).reshape(NVIRT * H, D)


def pick(index, choices):
    result = choices[-1]
    for place in range(len(choices) - 2, -1, -1):
        result = jnp.where(index == place, choices[place], result)
    return result


def sources_of(step):
    return ((0, 0, 0, 0), (0, 0, 1, 1), (0, 1, 2, 3), (0, 1, 2, 3))[step]


def steps_up(first):
    return [(z, z + 1) for z in range(first, LAYERS - 1)]


def steps_down(first):
    return [(LAYERS - 1 - z, LAYERS - 2 - z) for z in range(first, LAYERS - 1)]


def shards(feats, virt_emb, w_query, w_key, w_value, w_out, link_mask, partners, virt_ids):
    blocks_x, blocks_y = (feats.shape[0], feats.shape[1])
    nblocks = blocks_x * blocks_y
    rows_total = nblocks * BLK
    scale = 1.0 / math.sqrt(HD)
    inner = lax.axis_size("inner")
    cols = lax.axis_size("col")
    mesh_rows = LAYERS * inner
    peers = inner * cols
    devices = LAYERS * peers
    layer = lax.axis_index("outer")
    my_row = layer * inner + lax.axis_index("inner")
    my_col = lax.axis_index("col")
    flat = feats.reshape(rows_total, D)

    slot_count = nblocks * NEXP
    capacity = (slot_count + devices - 2) // (devices - 1)
    grid_cols = blocks_y * cols
    grid_rows = blocks_x * mesh_rows
    order = jnp.arange(slot_count, dtype=jnp.int32)
    own_slot = order % nblocks

    def locate(ids):
        ids = jnp.transpose(ids, (2, 0, 1)).reshape(slot_count)
        row = ids // grid_cols
        col = ids % grid_cols
        device = row // blocks_x * cols + col // blocks_y
        return device, row % blocks_x * blocks_y + col % blocks_y

    def ranks(device, sequence):
        same = device[:, None] == device[None, :]
        return jnp.sum(same & (sequence[None, :] < sequence[:, None]), axis=1)

    dest, partner_slot = locate(partners)
    rank_in = ranks(dest, order // nblocks * nblocks + partner_slot)
    target = dest * capacity + ranks(dest, order)
    hits = target[None, :] == jnp.arange(devices * capacity, dtype=jnp.int32)[:, None]
    wanted = jnp.sum(jnp.where(hits, own_slot[None, :], 0), axis=1).astype(jnp.int32)
    wanted = wanted.reshape(LAYERS, peers * capacity)

    rows = jnp.pad(
        wanted.astype(jnp.bfloat16),
        ((0, TABLE_ROWS - LAYERS), (0, D - peers * capacity)),
    )
    own = jnp.concatenate([flat, rows], axis=0)

    def table(step, sources):
        line = pick(
            layer, [sources[which][rows_total + z] for z, which in enumerate(sources_of(step))]
        )
        return line[: peers * capacity].astype(jnp.int32)

    layer_table = jnp.broadcast_to(layer, (1,)).astype(jnp.int32)

    def hand_round(step, sources, tokens, extra=None):
        slots = pick(layer, list(wanted)) if step == 0 else table(step, sources)
        sent = pack(
            sources_of(step), capacity, layer_table, slots, sources, extra, tokens
        )
        return sent, lax.all_to_all(sent, ("inner", "col"), 0, 0, tiled=True)

    up1 = lax.ppermute(own, "outer", steps_up(0))
    down1 = lax.ppermute(own, "outer", steps_down(0))
    up2 = lax.ppermute(up1, "outer", steps_up(1))
    down2 = lax.ppermute(down1, "outer", steps_down(1))
    up3 = lax.ppermute(up2, "outer", steps_up(2))
    down3 = lax.ppermute(down2, "outer", steps_down(2))

    rows_axes = ("outer", "inner")
    to_next_row = [(r, r + 1) for r in range(mesh_rows - 1)]
    to_prev_row = [(r + 1, r) for r in range(mesh_rows - 1)]
    to_next_col = [(c, c + 1) for c in range(cols - 1)]
    to_prev_col = [(c + 1, c) for c in range(cols - 1)]
    block = jnp.arange(nblocks, dtype=jnp.int32)
    bx = block // blocks_y
    by = block % blocks_y
    global_row = my_row * blocks_x + bx
    global_col = my_col * blocks_y + by
    links = link_mask.reshape(nblocks, 4) == 1
    north = jnp.where(bx > 0, block - blocks_y, by)
    south = jnp.where(bx < blocks_x - 1, block + blocks_y, blocks_y + by)
    west = jnp.where(by > 0, block - 1, 2 * blocks_y + bx)
    east = jnp.where(by < blocks_y - 1, block + 1, 2 * blocks_y + blocks_x + bx)
    dead = 2 + LAYERS
    near_slots = jnp.concatenate([block, north, south, west, east])
    near_phase = jnp.concatenate(
        [
            jnp.zeros((nblocks,), jnp.int32),
            jnp.where(links[:, 0] & (global_row > 0), jnp.where(bx > 0, 0, 1), dead),
            jnp.where(
                links[:, 1] & (global_row < grid_rows - 1),
                jnp.where(bx < blocks_x - 1, 0, 1),
                dead,
            ),
            jnp.where(links[:, 2] & (global_col > 0), jnp.where(by > 0, 0, 1), dead),
            jnp.where(
                links[:, 3] & (global_col < grid_cols - 1),
                jnp.where(by < blocks_y - 1, 0, 1),
                dead,
            ),
        ]
    )
    from_layer = dest // peers
    steps = [
        pick(from_layer, [jnp.int32(NEAREST[z].index(origin)) for origin in range(LAYERS)])
        for z in range(LAYERS)
    ]
    far_phase = 2 + pick(layer, steps)
    far_slots = dest % peers * capacity + rank_in
    entry_block = jnp.concatenate([jnp.tile(block, 5), own_slot])
    entry_slot = jnp.concatenate([near_slots, far_slots])
    entry_phase = jnp.concatenate([near_phase, far_phase])
    count = entry_block.shape[0]
    number = jnp.arange(count, dtype=jnp.int32)
    sort_key = entry_phase * count + number
    place = jnp.sum(sort_key[None, :] < sort_key[:, None], axis=1)
    at_place = place[None, :] == number[:, None]
    sorted_block = jnp.sum(jnp.where(at_place, entry_block[None, :], 0), axis=1).astype(jnp.int32)
    sorted_slot = jnp.sum(jnp.where(at_place, entry_slot[None, :], 0), axis=1).astype(jnp.int32)
    bounds = jnp.sum(
        entry_phase[None, :] < jnp.arange(dead + 1, dtype=jnp.int32)[:, None], axis=1
    ).astype(jnp.int32)
    entries = (bounds, sorted_block, sorted_slot)

    sent, first = hand_round(0, [own], [])
    halo_rows = [
        lax.ppermute(part, rows_axes, steps)
        for part, steps in zip(
            lax.optimization_barrier((feats[-1], feats[0], sent))[:2], (to_next_row, to_prev_row)
        )
    ]
    flat, _ = lax.optimization_barrier((flat, sent))

    queries = project(flat, w_query)
    scaled = (queries * jnp.bfloat16(scale)).reshape(nblocks, BLK, D)
    keys = project(flat, w_key)
    values_t = project_transposed(flat, w_value)
    virtual_query = project(virt_emb, w_query)
    virtual_keys = project(virt_emb, w_key)
    virtual_values = project(virt_emb, w_value)

    slots_v = jnp.arange(NVIRT, dtype=jnp.int32)
    chosen = virt_ids.reshape(1, nblocks, BLK) == slots_v[:, None, None]
    virtual_score = lax.dot_general(
        per_head(virtual_keys),
        scaled.reshape(rows_total, D),
        (((1,), (1,)), ((), ())),
        preferred_element_type=jnp.float32,
    ).reshape(NVIRT, H, nblocks, BLK)
    m0 = jnp.transpose(jnp.sum(jnp.where(chosen[:, None], virtual_score, 0.0), axis=0), (1, 0, 2))
    values_wide = jnp.zeros((D, BLK), jnp.float32)
    values_wide = values_wide.at[:, :NVIRT].set(virtual_values.astype(jnp.float32).T)

    member = chosen.reshape(NVIRT, 1, rows_total)
    node_scores = lax.dot_general(
        per_head(virtual_query), keys, (((1,), (1,)), ((), ())), preferred_element_type=jnp.float32
    ).reshape(NVIRT, H, rows_total) * scale
    node_scores = jnp.where(member, node_scores, NEG_FILL)
    local_top = jnp.max(node_scores, axis=-1)
    shares = jnp.where(member, jnp.exp(node_scores - local_top[..., None]), 0.0)
    local_total = jnp.sum(shares, axis=-1)
    weighted = lax.dot_general(
        shares.reshape(NVIRT * H, rows_total),
        values_t.astype(jnp.float32),
        (((1,), (1,)), ((), ())),
        precision=lax.Precision.HIGHEST,
        preferred_element_type=jnp.float32,
    ).reshape(NVIRT, H, H, HD)
    same_head = jnp.arange(H)[:, None] == jnp.arange(H)[None, :]
    local_accum = jnp.sum(jnp.where(same_head[None, :, :, None], weighted, 0.0), axis=2)
    packed = jnp.concatenate(
        [
            local_accum.reshape(NVIRT * H, HD),
            jnp.broadcast_to(local_top.reshape(NVIRT * H, 1), (NVIRT * H, HD // 2)),
            jnp.broadcast_to(local_total.reshape(NVIRT * H, 1), (NVIRT * H, HD // 2)),
        ],
        axis=1,
    )
    planes = []
    left = packed
    for _ in range(3):
        plane = lax.reduce_precision(left, 8, 7)
        planes.append(plane.astype(jnp.bfloat16))
        left = left - plane
    planes = jnp.concatenate(planes + [jnp.zeros_like(planes[0])], axis=1)

    def merge(parts):
        tops = parts[:, :, HD : HD + 1]
        top = jnp.max(tops, axis=0)
        rescale = jnp.exp(tops - top)
        accum = jnp.sum(parts[:, :, :HD] * rescale, axis=0)
        total = jnp.sum(parts[:, :, HD + HD // 2 :] * rescale, axis=0)
        return jnp.concatenate([accum, jnp.broadcast_to(top, (NVIRT * H, HD // 2)), total], axis=1)

    w_value_t = w_value.T
    keys = keys.reshape(nblocks, BLK, D)

    def phase(number, sources, slots, state, tokens, last=None, big=False):
        return attend_phase(
            number, entries, sources, slots, w_key, w_value_t, scaled, state, tokens, last, big
        )

    slots = peers * capacity
    packed, m0, keys, values_t, scaled = lax.optimization_barrier(
        (packed, m0, keys, values_t, scaled)
    )
    sent, second = hand_round(1, [down1, up1], [m0, packed])
    opening = (virt_ids.reshape(nblocks, BLK), values_wide, m0)
    state = attend_near(
        "attend_own",
        lambda bounds: (bounds[0], bounds[1]),
        entries,
        scaled,
        keys,
        values_t,
        None,
        opening,
        [sent],
        True,
    )
    sent, third = hand_round(2, [down2, up1, down1, up2], [state[1]], planes)
    state = phase(2, [first], slots, state, [sent, second, *halo_rows], big=True)
    halo_cols = [
        lax.ppermute(part, "col", steps)
        for part, steps in zip(
            lax.optimization_barrier((feats[:, -1], feats[:, 0], state[1]))[:2],
            (to_next_col, to_prev_col),
        )
    ]
    state = phase(3, [second], slots, state, [])
    sent, fourth = hand_round(3, [down3, down2, up2, up3], [state[1]])
    layer_parts = third[:, capacity * BLK :, :].astype(jnp.float32)
    layer_parts = layer_parts.reshape(peers, NVIRT * H, 4, 2 * HD)
    layer_part = merge(layer_parts[:, :, 0] + layer_parts[:, :, 1] + layer_parts[:, :, 2])
    around_parts = [layer_part] + [
        lax.ppermute(layer_part, "outer", [((z + turn) % LAYERS, z) for z in range(LAYERS)])
        for turn in range(1, LAYERS)
    ]
    halo = halo_rows + halo_cols
    halo_slots = 2 * (blocks_x + blocks_y)
    state = phase(1, halo, halo_slots, state, [sent, third], big=True)
    state = phase(4, [third], slots, state, [*around_parts[1:]])
    node_out = phase(5, [fourth], slots, state, [], (feats.reshape(nblocks, BLK, D), w_out))
    parts = jnp.stack(
        [
            pick(layer, [around_parts[(origin - z) % LAYERS] for z in range(LAYERS)])
            for origin in range(LAYERS)
        ]
    )

    own_score = (
        jnp.sum(
            (virtual_query.astype(jnp.float32) * virtual_keys.astype(jnp.float32)).reshape(
                NVIRT, H, HD
            ),
            axis=-1,
        )
        * scale
    ).reshape(NVIRT * H)
    part_top = parts[:, :, HD]
    part_total = parts[:, :, HD + HD // 2]
    final_top = jnp.maximum(jnp.max(part_top, axis=0), own_score)
    rescale = jnp.exp(part_top - final_top)
    own_share = jnp.exp(own_score - final_top)
    total = jnp.sum(part_total * rescale, axis=0) + own_share
    accum = jnp.sum(parts[:, :, :HD] * rescale[..., None], axis=0)
    accum = accum + own_share[:, None] * virtual_values.astype(jnp.float32).reshape(NVIRT * H, HD)
    virtual_context = (accum / total[:, None]).astype(jnp.bfloat16).reshape(NVIRT, D)
    virt_out = virt_emb.astype(jnp.float32) + jnp.dot(
        virtual_context, w_out, preferred_element_type=jnp.float32
    )
    return (node_out.reshape(feats.shape), virt_out)


def solution(mesh):
    inner = mesh.shape["row"] // LAYERS
    split = Mesh(mesh.devices.reshape(LAYERS, inner, mesh.shape["col"]), AXES)
    rows = ("outer", "inner")
    return jax.shard_map(
        shards,
        mesh=split,
        in_specs=(
            P(rows, "col", None, None),
            P(),
            P(),
            P(),
            P(),
            P(),
            P(rows, "col", None),
            P(rows, "col", None),
            P(rows, "col", None),
        ),
        out_specs=(P(rows, "col", None, None), P()),
        check_vma=False,
    )
```

```python
import math

import jax
import jax.numpy as jnp
from jax import lax
from jax.experimental import pallas as pl
from jax.experimental.pallas import tpu as pltpu
from jax.sharding import Mesh
from jax.sharding import PartitionSpec as P

D = 512
H = 8
HD = 64
BLK = 128
NEXP = 4
NVIRT = 4

NEG_FILL = -1e30
LAYERS = 4
NEAREST = ((0, 1, 2, 3), (1, 0, 2, 3), (2, 3, 1, 0), (3, 2, 1, 0))
VMEM_LIMIT = 56 * 1024 * 1024
AXES = ("outer", "inner", "col")
TABLE_ROWS = 16


def fold_entry(b, s, q_ref, k_ref, vt_ref, m_ref, l_ref, acc_ref):
    low = lax.broadcasted_iota(jnp.int32, (BLK, 2 * HD), 1) < HD
    zero = jnp.zeros((), jnp.bfloat16)
    columns = pl.ds(pl.multiple_of(s * BLK, BLK), BLK)
    scores = []
    tops = []
    for pair in range(H // 2):
        lanes = slice(pair * 2 * HD, (pair + 1) * 2 * HD)
        query = q_ref[b, :, lanes]
        both = jnp.concatenate([jnp.where(low, query, zero), jnp.where(low, zero, query)], axis=0)
        score = lax.dot_general(
            k_ref[s, :, lanes],
            both,
            (((1,), (1,)), ((), ())),
            preferred_element_type=jnp.float32,
        )
        scores.append(score)
        top = jnp.max(score, axis=0, keepdims=True)
        tops += [top[:, :BLK], top[:, BLK:]]
    m_old = m_ref[b]
    m_new = jnp.maximum(m_old, jnp.concatenate(tops, axis=0))
    alpha = jnp.exp(m_old - m_new)
    m_ref[b] = m_new
    sums = []
    for h in range(H):
        score = scores[h // 2][:, (h % 2) * BLK : (h % 2 + 1) * BLK]
        share = jnp.exp(score - m_new[h : h + 1])
        sums.append(jnp.sum(share, axis=0, keepdims=True))
        rows = slice(h * HD, (h + 1) * HD)
        part = jnp.dot(
            vt_ref[rows, columns], share.astype(jnp.bfloat16), preferred_element_type=jnp.float32
        )
        acc_ref[b, rows, :] = acc_ref[b, rows, :] * alpha[h : h + 1] + part
    l_ref[b] = l_ref[b] * alpha + jnp.concatenate(sums, axis=0)


def fold_range(low, high, blocks, slots, first, q_ref, k_ref, vt_ref, m_ref, l_ref, acc_ref):
    def fold(entry):
        slot = entry - first if slots is None else slots[entry]
        fold_entry(blocks[entry], slot, q_ref, k_ref, vt_ref, m_ref, l_ref, acc_ref)

    def two(step, carry):
        fold(low + 2 * step)
        fold(low + 2 * step + 1)
        return carry

    def one(entry, carry):
        fold(entry)
        return carry

    pairs = (high - low) // 2
    lax.fori_loop(0, pairs, two, 0)
    lax.fori_loop(low + 2 * pairs, high, one, 0)


def open_kernel(bounds, blocks, slots, q_ref, k_ref, vt_ref, ids_ref, vv_ref, m_in, *refs):
    m_ref, l_ref, acc_ref = refs[-3:]
    m_ref[...] = m_in[...]
    l_ref[...] = jnp.ones(l_ref.shape, jnp.float32)

    def open_block(b, carry):
        ids = ids_ref[pl.ds(b, 1), :]
        value = jnp.zeros((D, BLK), jnp.float32)
        for v in range(NVIRT):
            value = jnp.where(ids == v, vv_ref[:, v : v + 1], value)
        acc_ref[b] = value
        return carry

    lax.fori_loop(0, q_ref.shape[0], open_block, 0)
    fold_range(bounds[0], bounds[1], blocks, slots, 0, q_ref, k_ref, vt_ref, m_ref, l_ref, acc_ref)


GROUP = 4


def phase_kernel(phase, nsources, finish, ntokens, *refs):
    refs = list(refs)
    take = lambda count: [refs.pop(0) for _ in range(count)]
    bounds, blocks, slots = take(3)
    sources = take(nsources)
    wk_hbm, wv_hbm, q_hbm, m_hbm, l_hbm, acc_hbm = take(6)
    feats_hbm, wo_hbm = take(2) if finish else (None, None)
    take(ntokens)
    if finish:
        (out_hbm,) = take(1)
        m_ref, l_ref, acc_ref = take(3)
        feats_ref, wo_ref, out_ref, out_sems = take(4)
    else:
        m_ref, l_ref, acc_ref = take(3)
    raw_ref, wk_ref, wv_ref, q_ref, k_ref, vt_ref, sems = take(7)
    copies = []

    def fetch(source, target):
        copy = pltpu.make_async_copy(source, target, sems.at[len(copies)])
        copy.start()
        copies.append(copy)

    senders = sum(source.shape[0] for source in sources)
    rows_in = raw_ref.shape[0] // senders
    at = 0
    for source in sources:
        for sender in range(source.shape[0]):
            fetch(source.at[sender, pl.ds(0, rows_in)], raw_ref.at[pl.ds(at, rows_in)])
            at += rows_in
    fetch(wk_hbm, wk_ref)
    fetch(wv_hbm, wv_ref)
    needed = len(copies)
    fetch(q_hbm, q_ref)
    fetch(m_hbm, m_ref)
    fetch(l_hbm, l_ref)
    fetch(acc_hbm, acc_ref)
    if finish:
        fetch(feats_hbm, feats_ref)
        fetch(wo_hbm, wo_ref)
    for copy in copies[:needed]:
        copy.wait()
    low = bounds[phase]
    high = bounds[phase + 1]

    def project_group(group, carry):
        entries = [jnp.minimum(low + group * GROUP + u, high - 1) for u in range(GROUP)]
        rows = jnp.concatenate(
            [
                raw_ref[pl.ds(pl.multiple_of(slots[entry] * BLK, BLK), BLK), :]
                for entry in entries
            ],
            axis=0,
        )
        keys = jnp.dot(rows, wk_ref[...], preferred_element_type=jnp.float32)
        k_ref[pl.ds(group * GROUP, GROUP)] = keys.astype(jnp.bfloat16).reshape(GROUP, BLK, D)
        values = lax.dot_general(
            wv_ref[...], rows, (((1,), (1,)), ((), ())), preferred_element_type=jnp.float32
        )
        columns = pl.ds(pl.multiple_of(group * (GROUP * BLK), GROUP * BLK), GROUP * BLK)
        vt_ref[:, columns] = values.astype(jnp.bfloat16)
        return carry

    lax.fori_loop(0, (high - low + GROUP - 1) // GROUP, project_group, 0)
    for copy in copies[needed:]:
        copy.wait()
    fold_range(low, high, blocks, None, low, q_ref, k_ref, vt_ref, m_ref, l_ref, acc_ref)
    if not finish:
        return
    nblocks = q_ref.shape[0]

    def write(b):
        return pltpu.make_async_copy(out_ref.at[b], out_hbm.at[b], out_sems.at[b])

    def finish_block(b, carry):
        inverse = 1.0 / l_ref[b]
        context = jnp.concatenate(
            [acc_ref[b, h * HD : (h + 1) * HD, :] * inverse[h : h + 1] for h in range(H)], axis=0
        ).astype(jnp.bfloat16)
        mixed = lax.dot_general(
            context, wo_ref[...], (((0,), (0,)), ((), ())), preferred_element_type=jnp.float32
        )
        out_ref[b] = (feats_ref[b].astype(jnp.float32) + mixed).astype(jnp.bfloat16)
        write(b).start()
        return carry

    def settle(b, carry):
        write(b).wait()
        return carry

    lax.fori_loop(0, nblocks, finish_block, 0, unroll=2)
    lax.fori_loop(0, nblocks, settle, 0)


def pack_kernel(candidates, capacity, nsources, layer, wanted, *refs):
    sources = refs[:nsources]
    extra = refs[nsources]
    out_hbm, out_ref, sems, out_sems = refs[-4:]
    peers = out_ref.shape[0]
    count = peers * capacity

    def block(source, slot):
        return source.at[pl.ds(pl.multiple_of(slot * BLK, BLK), BLK)]

    def place(index):
        return out_ref.at[index // capacity, pl.ds(index % capacity * BLK, BLK)]

    for which in sorted(set(candidates)):
        mine = [layer[0] == z for z in range(LAYERS) if candidates[z] == which]
        chosen = mine[0]
        for other in mine[1:]:
            chosen = jnp.logical_or(chosen, other)

        @pl.when(chosen)
        def start(source=sources[which]):
            for index in range(count):
                pltpu.make_async_copy(
                    block(source, wanted[index]), place(index), sems.at[index]
                ).start()

    rest = out_ref.shape[1] - capacity * BLK
    if rest:
        for peer in range(peers):
            out_ref[peer, capacity * BLK :, :] = extra[...]
    leaving = [
        pltpu.make_async_copy(out_ref.at[peer], out_hbm.at[peer], out_sems.at[peer])
        for peer in range(peers)
    ]
    for index in range(count):
        pltpu.make_async_copy(block(sources[0], 0), place(index), sems.at[index]).wait()
        if index % capacity == capacity - 1:
            leaving[index // capacity].start()
    for copy in leaving:
        copy.wait()


VMEM = pl.BlockSpec(memory_space=pltpu.VMEM)
SMEM = pl.BlockSpec(memory_space=pltpu.SMEM)
HBM = pl.BlockSpec(memory_space=pl.ANY)


def cost(big):
    return pl.CostEstimate(
        flops=30_000_000_000 if big else 1, bytes_accessed=1, transcendentals=0
    )


def state_shapes(nblocks):
    return [
        jax.ShapeDtypeStruct((nblocks, H, BLK), jnp.float32),
        jax.ShapeDtypeStruct((nblocks, H, BLK), jnp.float32),
        jax.ShapeDtypeStruct((nblocks, D, BLK), jnp.float32),
    ]


def attend_own(entries, q, k, vt, ids, virtual_values, m0, token):
    return pl.pallas_call(
        open_kernel,
        in_specs=[SMEM] * 3 + [VMEM] * 6 + [HBM],
        out_specs=[VMEM] * 3,
        out_shape=state_shapes(q.shape[0]),
        compiler_params=pltpu.CompilerParams(vmem_limit_bytes=VMEM_LIMIT),
        cost_estimate=cost(True),
        name="attend_own",
    )(*entries, q, k, vt, ids, virtual_values, m0, token)


def attend_phase(phase, entries, sources, slots, w_key, w_value_t, q, state, tokens, last=None, big=False):
    room = -(-slots // GROUP) * GROUP
    finish = last is not None
    nblocks = q.shape[0]
    block = pltpu.VMEM((nblocks, BLK, D), jnp.bfloat16)
    square = pltpu.VMEM((D, D), jnp.bfloat16)
    shapes = state_shapes(nblocks)
    scratch = [
        pltpu.VMEM((slots * BLK, D), jnp.bfloat16),
        square,
        square,
        block,
        pltpu.VMEM((room, BLK, D), jnp.bfloat16),
        pltpu.VMEM((D, room * BLK), jnp.bfloat16),
        pltpu.SemaphoreType.DMA((sum(source.shape[0] for source in sources) + 8,)),
    ]
    if finish:
        scratch = (
            [pltpu.VMEM(shape.shape, shape.dtype) for shape in shapes]
            + [block, square, block, pltpu.SemaphoreType.DMA((nblocks,))]
            + scratch
        )
    extra = list(last) if finish else []

    def kernel(*refs):
        phase_kernel(phase, len(sources), finish, len(tokens), *refs)

    return pl.pallas_call(
        kernel,
        in_specs=[SMEM] * 3 + [HBM] * (6 + len(sources) + len(extra) + len(tokens)),
        out_specs=HBM if finish else [VMEM] * 3,
        out_shape=jax.ShapeDtypeStruct((nblocks, BLK, D), jnp.bfloat16) if finish else shapes,
        scratch_shapes=scratch,
        compiler_params=pltpu.CompilerParams(vmem_limit_bytes=VMEM_LIMIT),
        cost_estimate=cost(big),
        name=f"attend_{phase}",
    )(*entries, *sources, w_key, w_value_t, q, *state, *extra, *tokens)


def pack(candidates, capacity, layer, wanted, sources, extra, tokens):
    peers = wanted.shape[0] // capacity
    rows = capacity * BLK + (0 if extra is None else extra.shape[0])

    def kernel(*refs):
        pack_kernel(candidates, capacity, len(sources), *refs)

    return pl.pallas_call(
        kernel,
        in_specs=[SMEM] * 2 + [HBM] * len(sources) + [VMEM] * (extra is not None) + [HBM] * len(tokens),
        out_specs=HBM,
        out_shape=jax.ShapeDtypeStruct((peers, rows, D), jnp.bfloat16),
        scratch_shapes=[
            pltpu.VMEM((peers, rows, D), jnp.bfloat16),
            pltpu.SemaphoreType.DMA((peers * capacity,)),
            pltpu.SemaphoreType.DMA((peers,)),
        ],
        compiler_params=pltpu.CompilerParams(vmem_limit_bytes=VMEM_LIMIT),
        cost_estimate=cost(False),
        name="pack",
    )(layer, wanted, *sources, *([] if extra is None else [extra]), *tokens)


def project(rows, weight):
    return jnp.dot(rows, weight, preferred_element_type=jnp.float32).astype(jnp.bfloat16)


def project_transposed(rows, weight):
    return lax.dot_general(
        weight, rows, (((0,), (1,)), ((), ())), preferred_element_type=jnp.float32
    ).astype(jnp.bfloat16)


def per_head(vectors):
    head = jnp.arange(D, dtype=jnp.int32)[None, None, :] // HD
    mine = head == jnp.arange(H, dtype=jnp.int32)[None, :, None]
    return jnp.where(mine, vectors[:, None, :], jnp.zeros((), vectors.dtype)).reshape(NVIRT * H, D)


def pick(index, choices):
    result = choices[-1]
    for place in range(len(choices) - 2, -1, -1):
        result = jnp.where(index == place, choices[place], result)
    return result


def sources_of(step):
    return ((0, 0, 0, 0), (0, 0, 0, 0), (0, 1, 1, 0), (0, 1, 1, 0))[step]


ENDS = [(0, 1), (1, 0), (2, 3), (3, 2)]
MIDDLE = [(1, 2), (2, 1)]
OUTWARDS = [(1, 0), (2, 3)]


def shards(feats, virt_emb, w_query, w_key, w_value, w_out, link_mask, partners, virt_ids):
    blocks_x, blocks_y = (feats.shape[0], feats.shape[1])
    nblocks = blocks_x * blocks_y
    rows_total = nblocks * BLK
    scale = 1.0 / math.sqrt(HD)
    inner = lax.axis_size("inner")
    cols = lax.axis_size("col")
    mesh_rows = LAYERS * inner
    peers = inner * cols
    devices = LAYERS * peers
    layer = lax.axis_index("outer")
    my_row = layer * inner + lax.axis_index("inner")
    my_col = lax.axis_index("col")
    flat = feats.reshape(rows_total, D)

    slot_count = nblocks * NEXP
    capacity = (slot_count + devices - 2) // (devices - 1)
    grid_cols = blocks_y * cols
    grid_rows = blocks_x * mesh_rows
    order = jnp.arange(slot_count, dtype=jnp.int32)
    own_slot = order % nblocks

    def locate(ids):
        ids = jnp.transpose(ids, (2, 0, 1)).reshape(slot_count)
        row = ids // grid_cols
        col = ids % grid_cols
        device = row // blocks_x * cols + col // blocks_y
        return device, row % blocks_x * blocks_y + col % blocks_y

    def ranks(device, sequence):
        same = device[:, None] == device[None, :]
        return jnp.sum(same & (sequence[None, :] < sequence[:, None]), axis=1)

    dest, partner_slot = locate(partners)
    rank_in = ranks(dest, order // nblocks * nblocks + partner_slot)
    target = dest * capacity + ranks(dest, order)
    hits = target[None, :] == jnp.arange(devices * capacity, dtype=jnp.int32)[:, None]
    wanted = jnp.sum(jnp.where(hits, own_slot[None, :], 0), axis=1).astype(jnp.int32)
    wanted = wanted.reshape(LAYERS, peers * capacity)

    rows = jnp.pad(
        wanted.astype(jnp.bfloat16),
        ((0, TABLE_ROWS - LAYERS), (0, D - peers * capacity)),
    )
    own = jnp.concatenate([flat, rows], axis=0)

    def table(step, sources):
        line = pick(
            layer, [sources[which][rows_total + z] for z, which in enumerate(sources_of(step))]
        )
        return line[: peers * capacity].astype(jnp.int32)

    layer_table = jnp.broadcast_to(layer, (1,)).astype(jnp.int32)

    def hand_round(step, sources, tokens, extra=None):
        slots = pick(layer, list(wanted)) if step == 0 else table(step, sources)
        sent = pack(
            sources_of(step), capacity, layer_table, slots, sources, extra, tokens
        )
        return sent, lax.all_to_all(sent, ("inner", "col"), 0, 0, tiled=True)

    end1 = lax.ppermute(own, "outer", ENDS)
    middle1 = lax.ppermute(own, "outer", MIDDLE)
    end2 = lax.ppermute(middle1, "outer", OUTWARDS)
    middle2 = lax.ppermute(end1, "outer", MIDDLE)
    end3 = lax.ppermute(middle2, "outer", OUTWARDS)

    rows_axes = ("outer", "inner")
    to_next_row = [(r, r + 1) for r in range(mesh_rows - 1)]
    to_prev_row = [(r + 1, r) for r in range(mesh_rows - 1)]
    to_next_col = [(c, c + 1) for c in range(cols - 1)]
    to_prev_col = [(c + 1, c) for c in range(cols - 1)]
    block = jnp.arange(nblocks, dtype=jnp.int32)
    bx = block // blocks_y
    by = block % blocks_y
    global_row = my_row * blocks_x + bx
    global_col = my_col * blocks_y + by
    links = link_mask.reshape(nblocks, 4) == 1
    north = jnp.where(bx > 0, block - blocks_y, by)
    south = jnp.where(bx < blocks_x - 1, block + blocks_y, blocks_y + by)
    west = jnp.where(by > 0, block - 1, 2 * blocks_y + bx)
    east = jnp.where(by < blocks_y - 1, block + 1, 2 * blocks_y + blocks_x + bx)
    dead = 2 + LAYERS
    near_slots = jnp.concatenate([block, north, south, west, east])
    near_phase = jnp.concatenate(
        [
            jnp.zeros((nblocks,), jnp.int32),
            jnp.where(links[:, 0] & (global_row > 0), jnp.where(bx > 0, 0, 1), dead),
            jnp.where(
                links[:, 1] & (global_row < grid_rows - 1),
                jnp.where(bx < blocks_x - 1, 0, 1),
                dead,
            ),
            jnp.where(links[:, 2] & (global_col > 0), jnp.where(by > 0, 0, 1), dead),
            jnp.where(
                links[:, 3] & (global_col < grid_cols - 1),
                jnp.where(by < blocks_y - 1, 0, 1),
                dead,
            ),
        ]
    )
    from_layer = dest // peers
    steps = [
        pick(from_layer, [jnp.int32(NEAREST[z].index(origin)) for origin in range(LAYERS)])
        for z in range(LAYERS)
    ]
    far_phase = 2 + pick(layer, steps)
    far_slots = dest % peers * capacity + rank_in
    entry_block = jnp.concatenate([jnp.tile(block, 5), own_slot])
    entry_slot = jnp.concatenate([near_slots, far_slots])
    entry_phase = jnp.concatenate([near_phase, far_phase])
    count = entry_block.shape[0]
    number = jnp.arange(count, dtype=jnp.int32)
    sort_key = entry_phase * count + number
    place = jnp.sum(sort_key[None, :] < sort_key[:, None], axis=1)
    at_place = place[None, :] == number[:, None]
    sorted_block = jnp.sum(jnp.where(at_place, entry_block[None, :], 0), axis=1).astype(jnp.int32)
    sorted_slot = jnp.sum(jnp.where(at_place, entry_slot[None, :], 0), axis=1).astype(jnp.int32)
    bounds = jnp.sum(
        entry_phase[None, :] < jnp.arange(dead + 1, dtype=jnp.int32)[:, None], axis=1
    ).astype(jnp.int32)
    entries = (bounds, sorted_block, sorted_slot)

    sent, first = hand_round(0, [own], [])
    halo_rows = [
        lax.ppermute(part, rows_axes, steps)
        for part, steps in zip(
            lax.optimization_barrier((feats[-1], feats[0], sent))[:2], (to_next_row, to_prev_row)
        )
    ]
    flat, _ = lax.optimization_barrier((flat, sent))

    queries = project(flat, w_query)
    scaled = (queries * jnp.bfloat16(scale)).reshape(nblocks, BLK, D)
    keys = project(flat, w_key)
    values_t = project_transposed(flat, w_value)
    virtual_query = project(virt_emb, w_query)
    virtual_keys = project(virt_emb, w_key)
    virtual_values = project(virt_emb, w_value)

    slots_v = jnp.arange(NVIRT, dtype=jnp.int32)
    chosen = virt_ids.reshape(1, nblocks, BLK) == slots_v[:, None, None]
    virtual_score = lax.dot_general(
        per_head(virtual_keys),
        scaled.reshape(rows_total, D),
        (((1,), (1,)), ((), ())),
        preferred_element_type=jnp.float32,
    ).reshape(NVIRT, H, nblocks, BLK)
    m0 = jnp.transpose(jnp.sum(jnp.where(chosen[:, None], virtual_score, 0.0), axis=0), (1, 0, 2))
    values_wide = jnp.zeros((D, BLK), jnp.float32)
    values_wide = values_wide.at[:, :NVIRT].set(virtual_values.astype(jnp.float32).T)

    member = chosen.reshape(NVIRT, 1, rows_total)
    node_scores = lax.dot_general(
        per_head(virtual_query), keys, (((1,), (1,)), ((), ())), preferred_element_type=jnp.float32
    ).reshape(NVIRT, H, rows_total) * scale
    node_scores = jnp.where(member, node_scores, NEG_FILL)
    local_top = jnp.max(node_scores, axis=-1)
    shares = jnp.where(member, jnp.exp(node_scores - local_top[..., None]), 0.0)
    local_total = jnp.sum(shares, axis=-1)
    weighted = lax.dot_general(
        shares.reshape(NVIRT * H, rows_total),
        values_t.astype(jnp.float32),
        (((1,), (1,)), ((), ())),
        precision=lax.Precision.HIGHEST,
        preferred_element_type=jnp.float32,
    ).reshape(NVIRT, H, H, HD)
    same_head = jnp.arange(H)[:, None] == jnp.arange(H)[None, :]
    local_accum = jnp.sum(jnp.where(same_head[None, :, :, None], weighted, 0.0), axis=2)
    packed = jnp.concatenate(
        [
            local_accum.reshape(NVIRT * H, HD),
            jnp.broadcast_to(local_top.reshape(NVIRT * H, 1), (NVIRT * H, HD // 2)),
            jnp.broadcast_to(local_total.reshape(NVIRT * H, 1), (NVIRT * H, HD // 2)),
        ],
        axis=1,
    )
    planes = []
    left = packed
    for _ in range(3):
        plane = lax.reduce_precision(left, 8, 7)
        planes.append(plane.astype(jnp.bfloat16))
        left = left - plane
    planes = jnp.concatenate(planes + [jnp.zeros_like(planes[0])], axis=1)

    def merge(parts):
        tops = parts[:, :, HD : HD + 1]
        top = jnp.max(tops, axis=0)
        rescale = jnp.exp(tops - top)
        accum = jnp.sum(parts[:, :, :HD] * rescale, axis=0)
        total = jnp.sum(parts[:, :, HD + HD // 2 :] * rescale, axis=0)
        return jnp.concatenate([accum, jnp.broadcast_to(top, (NVIRT * H, HD // 2)), total], axis=1)

    w_value_t = w_value.T
    keys = keys.reshape(nblocks, BLK, D)

    def phase(number, sources, slots, state, tokens, last=None, big=False):
        return attend_phase(
            number, entries, sources, slots, w_key, w_value_t, scaled, state, tokens, last, big
        )

    slots = peers * capacity
    packed, m0, keys, values_t, scaled = lax.optimization_barrier(
        (packed, m0, keys, values_t, scaled)
    )
    sent, second = hand_round(1, [end1], [m0, packed])
    state = attend_own(
        entries, scaled, keys, values_t, virt_ids.reshape(nblocks, BLK), values_wide, m0, sent
    )
    sent, third = hand_round(2, [end2, middle1], [state[1]], planes)
    state = phase(2, [first], slots, state, [sent, second, *halo_rows], big=True)
    halo_cols = [
        lax.ppermute(part, "col", steps)
        for part, steps in zip(
            lax.optimization_barrier((feats[:, -1], feats[:, 0], state[1]))[:2],
            (to_next_col, to_prev_col),
        )
    ]
    state = phase(3, [second], slots, state, [])
    sent, fourth = hand_round(3, [end3, middle2], [state[1]])
    layer_parts = third[:, capacity * BLK :, :].astype(jnp.float32)
    layer_parts = layer_parts.reshape(peers, NVIRT * H, 4, 2 * HD)
    layer_part = merge(layer_parts[:, :, 0] + layer_parts[:, :, 1] + layer_parts[:, :, 2])
    around_parts = [layer_part] + [
        lax.ppermute(layer_part, "outer", [((z + turn) % LAYERS, z) for z in range(LAYERS)])
        for turn in range(1, LAYERS)
    ]
    halo = halo_rows + halo_cols
    halo_slots = 2 * (blocks_x + blocks_y)
    state = phase(1, halo, halo_slots, state, [sent, third], big=True)
    state = phase(4, [third], slots, state, [*around_parts[1:]])
    node_out = phase(5, [fourth], slots, state, [], (feats.reshape(nblocks, BLK, D), w_out))
    parts = jnp.stack(
        [
            pick(layer, [around_parts[(origin - z) % LAYERS] for z in range(LAYERS)])
            for origin in range(LAYERS)
        ]
    )

    own_score = (
        jnp.sum(
            (virtual_query.astype(jnp.float32) * virtual_keys.astype(jnp.float32)).reshape(
                NVIRT, H, HD
            ),
            axis=-1,
        )
        * scale
    ).reshape(NVIRT * H)
    part_top = parts[:, :, HD]
    part_total = parts[:, :, HD + HD // 2]
    final_top = jnp.maximum(jnp.max(part_top, axis=0), own_score)
    rescale = jnp.exp(part_top - final_top)
    own_share = jnp.exp(own_score - final_top)
    total = jnp.sum(part_total * rescale, axis=0) + own_share
    accum = jnp.sum(parts[:, :, :HD] * rescale[..., None], axis=0)
    accum = accum + own_share[:, None] * virtual_values.astype(jnp.float32).reshape(NVIRT * H, HD)
    virtual_context = (accum / total[:, None]).astype(jnp.bfloat16).reshape(NVIRT, D)
    virt_out = virt_emb.astype(jnp.float32) + jnp.dot(
        virtual_context, w_out, preferred_element_type=jnp.float32
    )
    return (node_out.reshape(feats.shape), virt_out)


def solution(mesh):
    inner = mesh.shape["row"] // LAYERS
    split = Mesh(mesh.devices.reshape(LAYERS, inner, mesh.shape["col"]), AXES)
    rows = ("outer", "inner")
    return jax.shard_map(
        shards,
        mesh=split,
        in_specs=(
            P(rows, "col", None, None),
            P(),
            P(),
            P(),
            P(),
            P(),
            P(rows, "col", None),
            P(rows, "col", None),
            P(rows, "col", None),
        ),
        out_specs=(P(rows, "col", None, None), P()),
        check_vma=False,
    )
```

```python
import math

import jax
import jax.numpy as jnp
from jax import lax
from jax.experimental import pallas as pl
from jax.experimental.pallas import tpu as pltpu
from jax.sharding import Mesh
from jax.sharding import PartitionSpec as P

D = 512
H = 8
HD = 64
BLK = 128
NEXP = 4
NVIRT = 4

NEG_FILL = -1e30
LAYERS = 4
PHASES = 2 + LAYERS
UNROLL = 4
NEAREST = ((0, 1, 2, 3), (1, 0, 2, 3), (2, 3, 1, 0), (3, 2, 1, 0))
VMEM_LIMIT = 56 * 1024 * 1024
AXES = ("outer", "inner", "col")
TABLE_ROWS = 16


def fold_entry(b, s, q_ref, k_ref, vt_ref, m_ref, l_ref, acc_ref):
    low = lax.broadcasted_iota(jnp.int32, (BLK, 2 * HD), 1) < HD
    zero = jnp.zeros((), jnp.bfloat16)
    columns = pl.ds(pl.multiple_of(s * BLK, BLK), BLK)
    scores = []
    tops = []
    for pair in range(H // 2):
        lanes = slice(pair * 2 * HD, (pair + 1) * 2 * HD)
        query = q_ref[b, :, lanes]
        both = jnp.concatenate([jnp.where(low, query, zero), jnp.where(low, zero, query)], axis=0)
        score = lax.dot_general(
            k_ref[s, :, lanes],
            both,
            (((1,), (1,)), ((), ())),
            preferred_element_type=jnp.float32,
        )
        scores.append(score)
        top = jnp.max(score, axis=0, keepdims=True)
        tops += [top[:, :BLK], top[:, BLK:]]
    m_old = m_ref[b]
    m_new = jnp.maximum(m_old, jnp.concatenate(tops, axis=0))
    alpha = jnp.exp(m_old - m_new)
    m_ref[b] = m_new
    sums = []
    for h in range(H):
        score = scores[h // 2][:, (h % 2) * BLK : (h % 2 + 1) * BLK]
        share = jnp.exp(score - m_new[h : h + 1])
        sums.append(jnp.sum(share, axis=0, keepdims=True))
        rows = slice(h * HD, (h + 1) * HD)
        part = jnp.dot(
            vt_ref[rows, columns], share.astype(jnp.bfloat16), preferred_element_type=jnp.float32
        )
        acc_ref[b, rows, :] = acc_ref[b, rows, :] * alpha[h : h + 1] + part
    l_ref[b] = l_ref[b] * alpha + jnp.concatenate(sums, axis=0)


class Entries:
    def __init__(self, ref):
        self.ref = ref
        self.count = (ref.shape[0] - PHASES - 1) // 2

    def bound(self, phase):
        return self.ref[phase]

    def block(self, entry):
        return self.ref[entry + (PHASES + 1)]

    def slot(self, entry):
        return self.ref[entry + (PHASES + 1 + self.count)]


def fold_range(low, high, entries, own_slots, q_ref, k_ref, vt_ref, m_ref, l_ref, acc_ref):
    def fold(entry):
        slot = entry - low if own_slots else entries.slot(entry)
        fold_entry(entries.block(entry), slot, q_ref, k_ref, vt_ref, m_ref, l_ref, acc_ref)

    def several(step, carry):
        for u in range(UNROLL):
            fold(low + UNROLL * step + u)
        return carry

    def one(entry, carry):
        fold(entry)
        return carry

    full = (high - low) // UNROLL
    lax.fori_loop(0, full, several, 0)
    lax.fori_loop(low + UNROLL * full, high, one, 0)


def open_kernel(table, q_ref, k_ref, vt_ref, ids_ref, vv_ref, m_in, *refs):
    m_ref, l_ref, acc_ref = refs[-3:]
    m_ref[...] = m_in[...]
    l_ref[...] = jnp.ones(l_ref.shape, jnp.float32)

    def open_block(b, carry):
        ids = ids_ref[pl.ds(b, 1), :]
        value = jnp.zeros((D, BLK), jnp.float32)
        for v in range(NVIRT):
            value = jnp.where(ids == v, vv_ref[:, v : v + 1], value)
        acc_ref[b] = value
        return carry

    lax.fori_loop(0, q_ref.shape[0], open_block, 0)
    entries = Entries(table)
    fold_range(
        entries.bound(0), entries.bound(1), entries, False, q_ref, k_ref, vt_ref, m_ref, l_ref, acc_ref
    )


GROUP = 4


def phase_kernel(phase, capacity, nsources, finish, ntokens, *refs):
    refs = list(refs)
    take = lambda count: [refs.pop(0) for _ in range(count)]
    entries = Entries(take(1)[0])
    sources = take(nsources)
    wk_hbm, wv_hbm, q_hbm, m_hbm, l_hbm, acc_hbm = take(6)
    feats_hbm, wo_hbm = take(2) if finish else (None, None)
    take(ntokens)
    if finish:
        (out_hbm,) = take(1)
        m_ref, l_ref, acc_ref = take(3)
        feats_ref, wo_ref, out_ref, out_sems = take(4)
    else:
        m_ref, l_ref, acc_ref = take(3)
    raw_ref, wk_ref, wv_ref, q_ref, k_ref, vt_ref, sems, raw_sems = take(8)
    copies = []

    def fetch(source, target):
        copy = pltpu.make_async_copy(source, target, sems.at[len(copies)])
        copy.start()
        copies.append(copy)

    fetch(wk_hbm, wk_ref)
    fetch(wv_hbm, wv_ref)
    needed = len(copies)
    low = entries.bound(phase)
    high = entries.bound(phase + 1)

    def wanted_block(number):
        return raw_ref.at[pl.ds(pl.multiple_of(number * BLK, BLK), BLK)]

    def start_block(number, carry):
        slot = entries.slot(low + number)
        at = 0
        for source in sources:
            each = capacity if len(sources) == 1 else 1
            count = source.shape[0] * each

            @pl.when((slot >= at) & (slot < at + count))
            def start(source=source, place=slot - at):
                sender = lax.div(place, each)
                rows = pl.ds(pl.multiple_of((place - sender * each) * BLK, BLK), BLK)
                pltpu.make_async_copy(
                    source.at[sender, rows], wanted_block(number), raw_sems.at[number]
                ).start()

            at += count
        return carry

    lax.fori_loop(0, high - low, start_block, 0)
    fetch(q_hbm, q_ref)
    fetch(m_hbm, m_ref)
    fetch(l_hbm, l_ref)
    fetch(acc_hbm, acc_ref)
    if finish:
        fetch(feats_hbm, feats_ref)
        fetch(wo_hbm, wo_ref)
    for copy in copies[:needed]:
        copy.wait()

    def project_group(group, carry):
        for u in range(GROUP):
            number = group * GROUP + u

            @pl.when(number < high - low)
            def arrive(number=number):
                pltpu.make_async_copy(
                    sources[0].at[0, pl.ds(0, BLK)], wanted_block(number), raw_sems.at[number]
                ).wait()

        rows = raw_ref[pl.ds(pl.multiple_of(group * (GROUP * BLK), GROUP * BLK), GROUP * BLK), :]
        keys = jnp.dot(rows, wk_ref[...], preferred_element_type=jnp.float32)
        k_ref[pl.ds(group * GROUP, GROUP)] = keys.astype(jnp.bfloat16).reshape(GROUP, BLK, D)
        values = lax.dot_general(
            wv_ref[...], rows, (((1,), (1,)), ((), ())), preferred_element_type=jnp.float32
        )
        columns = pl.ds(pl.multiple_of(group * (GROUP * BLK), GROUP * BLK), GROUP * BLK)
        vt_ref[:, columns] = values.astype(jnp.bfloat16)
        return carry

    lax.fori_loop(0, (high - low + GROUP - 1) // GROUP, project_group, 0)
    for copy in copies[needed:]:
        copy.wait()
    fold_range(low, high, entries, True, q_ref, k_ref, vt_ref, m_ref, l_ref, acc_ref)
    if not finish:
        return
    nblocks = q_ref.shape[0]

    def write(b):
        return pltpu.make_async_copy(out_ref.at[b], out_hbm.at[b], out_sems.at[b])

    def finish_block(b, carry):
        inverse = 1.0 / l_ref[b]
        context = jnp.concatenate(
            [acc_ref[b, h * HD : (h + 1) * HD, :] * inverse[h : h + 1] for h in range(H)], axis=0
        ).astype(jnp.bfloat16)
        mixed = lax.dot_general(
            context, wo_ref[...], (((0,), (0,)), ((), ())), preferred_element_type=jnp.float32
        )
        out_ref[b] = (feats_ref[b].astype(jnp.float32) + mixed).astype(jnp.bfloat16)
        write(b).start()
        return carry

    def settle(b, carry):
        write(b).wait()
        return carry

    lax.fori_loop(0, nblocks, finish_block, 0, unroll=4)
    lax.fori_loop(0, nblocks, settle, 0)


def pack_kernel(candidates, capacity, nsources, wanted, *refs):
    sources = refs[:nsources]
    extra = refs[nsources]
    out_hbm, out_ref, sems, out_sems = refs[-4:]
    peers = out_ref.shape[0]
    count = peers * capacity

    def block(source, slot):
        return source.at[pl.ds(pl.multiple_of(slot * BLK, BLK), BLK)]

    def place(index):
        return out_ref.at[index // capacity, pl.ds(index % capacity * BLK, BLK)]

    for which in sorted(set(candidates)):
        mine = [wanted[count] == z for z in range(LAYERS) if candidates[z] == which]
        chosen = mine[0]
        for other in mine[1:]:
            chosen = jnp.logical_or(chosen, other)

        @pl.when(chosen)
        def start(source=sources[which]):
            for index in range(count):
                pltpu.make_async_copy(
                    block(source, wanted[index]), place(index), sems.at[index]
                ).start()

    rest = out_ref.shape[1] - capacity * BLK
    if rest:
        for peer in range(peers):
            out_ref[peer, capacity * BLK :, :] = extra[...]
    leaving = [
        pltpu.make_async_copy(out_ref.at[peer], out_hbm.at[peer], out_sems.at[peer])
        for peer in range(peers)
    ]
    for index in range(count):
        pltpu.make_async_copy(block(sources[0], 0), place(index), sems.at[index]).wait()
        if index % capacity == capacity - 1:
            leaving[index // capacity].start()
    for copy in leaving:
        copy.wait()


VMEM = pl.BlockSpec(memory_space=pltpu.VMEM)
SMEM = pl.BlockSpec(memory_space=pltpu.SMEM)
HBM = pl.BlockSpec(memory_space=pl.ANY)


def cost(big):
    return pl.CostEstimate(
        flops=30_000_000_000 if big else 1, bytes_accessed=1, transcendentals=0
    )


def state_shapes(nblocks):
    return [
        jax.ShapeDtypeStruct((nblocks, H, BLK), jnp.float32),
        jax.ShapeDtypeStruct((nblocks, H, BLK), jnp.float32),
        jax.ShapeDtypeStruct((nblocks, D, BLK), jnp.float32),
    ]


def attend_own(entries, q, k, vt, ids, virtual_values, m0, token):
    return pl.pallas_call(
        open_kernel,
        in_specs=[SMEM] + [VMEM] * 6 + [HBM],
        out_specs=[VMEM] * 3,
        out_shape=state_shapes(q.shape[0]),
        compiler_params=pltpu.CompilerParams(vmem_limit_bytes=VMEM_LIMIT),
        cost_estimate=cost(True),
        name="attend_own",
    )(entries, q, k, vt, ids, virtual_values, m0, token)


def attend_phase(phase, entries, sources, slots, w_key, w_value_t, q, state, tokens, last=None, big=False):
    room = -(-slots // GROUP) * GROUP
    capacity = slots // sources[0].shape[0]
    finish = last is not None
    nblocks = q.shape[0]
    block = pltpu.VMEM((nblocks, BLK, D), jnp.bfloat16)
    square = pltpu.VMEM((D, D), jnp.bfloat16)
    shapes = state_shapes(nblocks)
    scratch = [
        pltpu.VMEM((room * BLK, D), jnp.bfloat16),
        square,
        square,
        block,
        pltpu.VMEM((room, BLK, D), jnp.bfloat16),
        pltpu.VMEM((D, room * BLK), jnp.bfloat16),
        pltpu.SemaphoreType.DMA((8,)),
        pltpu.SemaphoreType.DMA((room,)),
    ]
    if finish:
        scratch = (
            [pltpu.VMEM(shape.shape, shape.dtype) for shape in shapes]
            + [block, square, block, pltpu.SemaphoreType.DMA((nblocks,))]
            + scratch
        )
    extra = list(last) if finish else []

    def kernel(*refs):
        phase_kernel(phase, capacity, len(sources), finish, len(tokens), *refs)

    return pl.pallas_call(
        kernel,
        in_specs=[SMEM] + [HBM] * (6 + len(sources) + len(extra) + len(tokens)),
        out_specs=HBM if finish else [VMEM] * 3,
        out_shape=jax.ShapeDtypeStruct((nblocks, BLK, D), jnp.bfloat16) if finish else shapes,
        scratch_shapes=scratch,
        compiler_params=pltpu.CompilerParams(vmem_limit_bytes=VMEM_LIMIT),
        cost_estimate=cost(big),
        name=f"attend_{phase}",
    )(entries, *sources, w_key, w_value_t, q, *state, *extra, *tokens)


def pack(candidates, capacity, wanted, sources, extra, tokens):
    peers = (wanted.shape[0] - 1) // capacity
    rows = capacity * BLK + (0 if extra is None else extra.shape[0])

    def kernel(*refs):
        pack_kernel(candidates, capacity, len(sources), *refs)

    return pl.pallas_call(
        kernel,
        in_specs=[SMEM] + [HBM] * len(sources) + [VMEM] * (extra is not None) + [HBM] * len(tokens),
        out_specs=HBM,
        out_shape=jax.ShapeDtypeStruct((peers, rows, D), jnp.bfloat16),
        scratch_shapes=[
            pltpu.VMEM((peers, rows, D), jnp.bfloat16),
            pltpu.SemaphoreType.DMA((peers * capacity,)),
            pltpu.SemaphoreType.DMA((peers,)),
        ],
        compiler_params=pltpu.CompilerParams(vmem_limit_bytes=VMEM_LIMIT),
        cost_estimate=cost(False),
        name="pack",
    )(wanted, *sources, *([] if extra is None else [extra]), *tokens)


def project(rows, weight):
    return jnp.dot(rows, weight, preferred_element_type=jnp.float32).astype(jnp.bfloat16)


def project_transposed(rows, weight):
    return lax.dot_general(
        weight, rows, (((0,), (1,)), ((), ())), preferred_element_type=jnp.float32
    ).astype(jnp.bfloat16)


def per_head(vectors):
    head = jnp.arange(D, dtype=jnp.int32)[None, None, :] // HD
    mine = head == jnp.arange(H, dtype=jnp.int32)[None, :, None]
    return jnp.where(mine, vectors[:, None, :], jnp.zeros((), vectors.dtype)).reshape(NVIRT * H, D)


def pick(index, choices):
    result = choices[-1]
    for place in range(len(choices) - 2, -1, -1):
        result = jnp.where(index == place, choices[place], result)
    return result


def sources_of(step):
    return ((0, 0, 0, 0), (0, 0, 0, 0), (0, 1, 1, 0), (0, 1, 1, 0))[step]


ENDS = [(0, 1), (1, 0), (2, 3), (3, 2)]
MIDDLE = [(1, 2), (2, 1)]
OUTWARDS = [(1, 0), (2, 3)]


def shards(feats, virt_emb, w_query, w_key, w_value, w_out, link_mask, partners, virt_ids):
    blocks_x, blocks_y = (feats.shape[0], feats.shape[1])
    nblocks = blocks_x * blocks_y
    rows_total = nblocks * BLK
    scale = 1.0 / math.sqrt(HD)
    inner = lax.axis_size("inner")
    cols = lax.axis_size("col")
    mesh_rows = LAYERS * inner
    peers = inner * cols
    devices = LAYERS * peers
    layer = lax.axis_index("outer")
    my_row = layer * inner + lax.axis_index("inner")
    my_col = lax.axis_index("col")
    flat = feats.reshape(rows_total, D)

    slot_count = nblocks * NEXP
    capacity = (slot_count + devices - 2) // (devices - 1)
    grid_cols = blocks_y * cols
    grid_rows = blocks_x * mesh_rows
    order = jnp.arange(slot_count, dtype=jnp.int32)
    own_slot = order % nblocks

    def locate(ids):
        ids = jnp.transpose(ids, (2, 0, 1)).reshape(slot_count)
        row = ids // grid_cols
        col = ids % grid_cols
        device = row // blocks_x * cols + col // blocks_y
        return device, row % blocks_x * blocks_y + col % blocks_y

    def ranks(device, sequence):
        same = device[:, None] == device[None, :]
        return jnp.sum(same & (sequence[None, :] < sequence[:, None]), axis=1)

    dest, partner_slot = locate(partners)
    rank_in = ranks(dest, order // nblocks * nblocks + partner_slot)
    target = dest * capacity + ranks(dest, order)
    hits = target[None, :] == jnp.arange(devices * capacity, dtype=jnp.int32)[:, None]
    wanted = jnp.sum(jnp.where(hits, own_slot[None, :], 0), axis=1).astype(jnp.int32)
    wanted = wanted.reshape(LAYERS, peers * capacity)

    rows = jnp.pad(
        wanted.astype(jnp.bfloat16),
        ((0, TABLE_ROWS - LAYERS), (0, D - peers * capacity)),
    )
    own = jnp.concatenate([flat, rows], axis=0)

    def table(step, sources):
        line = pick(
            layer, [sources[which][rows_total + z] for z, which in enumerate(sources_of(step))]
        )
        return line[: peers * capacity].astype(jnp.int32)

    this_layer = jnp.broadcast_to(layer, (1,)).astype(jnp.int32)

    def hand_round(step, sources, tokens, extra=None):
        slots = pick(layer, list(wanted)) if step == 0 else table(step, sources)
        slots = jnp.concatenate([slots, this_layer])
        sent = pack(
            sources_of(step), capacity, slots, sources, extra, tokens
        )
        return sent, lax.all_to_all(sent, ("inner", "col"), 0, 0, tiled=True)

    end1 = lax.ppermute(own, "outer", ENDS)
    middle1 = lax.ppermute(own, "outer", MIDDLE)
    end2 = lax.ppermute(middle1, "outer", OUTWARDS)
    middle2 = lax.ppermute(end1, "outer", MIDDLE)
    end3 = lax.ppermute(middle2, "outer", OUTWARDS)

    rows_axes = ("outer", "inner")
    to_next_row = [(r, r + 1) for r in range(mesh_rows - 1)]
    to_prev_row = [(r + 1, r) for r in range(mesh_rows - 1)]
    to_next_col = [(c, c + 1) for c in range(cols - 1)]
    to_prev_col = [(c + 1, c) for c in range(cols - 1)]
    block = jnp.arange(nblocks, dtype=jnp.int32)
    bx = block // blocks_y
    by = block % blocks_y
    global_row = my_row * blocks_x + bx
    global_col = my_col * blocks_y + by
    links = link_mask.reshape(nblocks, 4) == 1
    north = jnp.where(bx > 0, block - blocks_y, by)
    south = jnp.where(bx < blocks_x - 1, block + blocks_y, blocks_y + by)
    west = jnp.where(by > 0, block - 1, 2 * blocks_y + bx)
    east = jnp.where(by < blocks_y - 1, block + 1, 2 * blocks_y + blocks_x + bx)
    dead = PHASES
    near_slots = jnp.concatenate([block, north, south, west, east])
    near_phase = jnp.concatenate(
        [
            jnp.zeros((nblocks,), jnp.int32),
            jnp.where(links[:, 0] & (global_row > 0), jnp.where(bx > 0, 0, 1), dead),
            jnp.where(
                links[:, 1] & (global_row < grid_rows - 1),
                jnp.where(bx < blocks_x - 1, 0, 1),
                dead,
            ),
            jnp.where(links[:, 2] & (global_col > 0), jnp.where(by > 0, 0, 1), dead),
            jnp.where(
                links[:, 3] & (global_col < grid_cols - 1),
                jnp.where(by < blocks_y - 1, 0, 1),
                dead,
            ),
        ]
    )
    from_layer = dest // peers
    steps = [
        pick(from_layer, [jnp.int32(NEAREST[z].index(origin)) for origin in range(LAYERS)])
        for z in range(LAYERS)
    ]
    far_phase = 2 + pick(layer, steps)
    far_slots = dest % peers * capacity + rank_in
    entry_block = jnp.concatenate([jnp.tile(block, 5), own_slot])
    entry_slot = jnp.concatenate([near_slots, far_slots])
    entry_phase = jnp.concatenate([near_phase, far_phase])
    count = entry_block.shape[0]
    number = jnp.arange(count, dtype=jnp.int32)
    sort_key = entry_phase * count + number
    place = jnp.sum(sort_key[None, :] < sort_key[:, None], axis=1)
    at_place = place[None, :] == number[:, None]
    sorted_block = jnp.sum(jnp.where(at_place, entry_block[None, :], 0), axis=1).astype(jnp.int32)
    sorted_slot = jnp.sum(jnp.where(at_place, entry_slot[None, :], 0), axis=1).astype(jnp.int32)
    bounds = jnp.sum(
        entry_phase[None, :] < jnp.arange(dead + 1, dtype=jnp.int32)[:, None], axis=1
    ).astype(jnp.int32)
    entries = jnp.concatenate([bounds, sorted_block, sorted_slot])

    sent, first = hand_round(0, [own], [])
    halo_rows = [
        lax.ppermute(part, rows_axes, steps)
        for part, steps in zip(
            lax.optimization_barrier((feats[-1], feats[0], sent))[:2], (to_next_row, to_prev_row)
        )
    ]
    flat, _ = lax.optimization_barrier((flat, sent))

    queries = project(flat, w_query)
    scaled = (queries * jnp.bfloat16(scale)).reshape(nblocks, BLK, D)
    keys = project(flat, w_key)
    values_t = project_transposed(flat, w_value)
    virtual_query = project(virt_emb, w_query)
    virtual_keys = project(virt_emb, w_key)
    virtual_values = project(virt_emb, w_value)

    slots_v = jnp.arange(NVIRT, dtype=jnp.int32)
    chosen = virt_ids.reshape(1, nblocks, BLK) == slots_v[:, None, None]
    virtual_score = lax.dot_general(
        per_head(virtual_keys),
        scaled.reshape(rows_total, D),
        (((1,), (1,)), ((), ())),
        preferred_element_type=jnp.float32,
    ).reshape(NVIRT, H, nblocks, BLK)
    m0 = jnp.transpose(jnp.sum(jnp.where(chosen[:, None], virtual_score, 0.0), axis=0), (1, 0, 2))
    values_wide = jnp.zeros((D, BLK), jnp.float32)
    values_wide = values_wide.at[:, :NVIRT].set(virtual_values.astype(jnp.float32).T)

    member = chosen.reshape(NVIRT, 1, rows_total)
    node_scores = lax.dot_general(
        per_head(virtual_query), keys, (((1,), (1,)), ((), ())), preferred_element_type=jnp.float32
    ).reshape(NVIRT, H, rows_total) * scale
    node_scores = jnp.where(member, node_scores, NEG_FILL)
    local_top = jnp.max(node_scores, axis=-1)
    shares = jnp.where(member, jnp.exp(node_scores - local_top[..., None]), 0.0)
    local_total = jnp.sum(shares, axis=-1)
    weighted = lax.dot_general(
        shares.reshape(NVIRT * H, rows_total),
        values_t.astype(jnp.float32),
        (((1,), (1,)), ((), ())),
        precision=lax.Precision.HIGHEST,
        preferred_element_type=jnp.float32,
    ).reshape(NVIRT, H, H, HD)
    same_head = jnp.arange(H)[:, None] == jnp.arange(H)[None, :]
    local_accum = jnp.sum(jnp.where(same_head[None, :, :, None], weighted, 0.0), axis=2)
    packed = jnp.concatenate(
        [
            local_accum.reshape(NVIRT * H, HD),
            jnp.broadcast_to(local_top.reshape(NVIRT * H, 1), (NVIRT * H, HD // 2)),
            jnp.broadcast_to(local_total.reshape(NVIRT * H, 1), (NVIRT * H, HD // 2)),
        ],
        axis=1,
    )
    planes = []
    left = packed
    for _ in range(3):
        plane = lax.reduce_precision(left, 8, 7)
        planes.append(plane.astype(jnp.bfloat16))
        left = left - plane
    planes = jnp.concatenate(planes + [jnp.zeros_like(planes[0])], axis=1)

    def merge(parts):
        tops = parts[:, :, HD : HD + 1]
        top = jnp.max(tops, axis=0)
        rescale = jnp.exp(tops - top)
        accum = jnp.sum(parts[:, :, :HD] * rescale, axis=0)
        total = jnp.sum(parts[:, :, HD + HD // 2 :] * rescale, axis=0)
        return jnp.concatenate([accum, jnp.broadcast_to(top, (NVIRT * H, HD // 2)), total], axis=1)

    w_value_t = w_value.T
    keys = keys.reshape(nblocks, BLK, D)

    def phase(number, sources, slots, state, tokens, last=None, big=False):
        return attend_phase(
            number, entries, sources, slots, w_key, w_value_t, scaled, state, tokens, last, big
        )

    slots = peers * capacity
    packed, m0, keys, values_t, scaled = lax.optimization_barrier(
        (packed, m0, keys, values_t, scaled)
    )
    sent, second = hand_round(1, [end1], [m0, packed])
    state = attend_own(
        entries, scaled, keys, values_t, virt_ids.reshape(nblocks, BLK), values_wide, m0, sent
    )
    sent, third = hand_round(2, [end2, middle1], [state[1]], planes)
    state = phase(2, [first], slots, state, [sent, second, *halo_rows], big=True)
    halo_cols = [
        lax.ppermute(part, "col", steps)
        for part, steps in zip(
            lax.optimization_barrier((feats[:, -1], feats[:, 0], state[1]))[:2],
            (to_next_col, to_prev_col),
        )
    ]
    state = phase(3, [second], slots, state, [])
    sent, fourth = hand_round(3, [end3, middle2], [state[1]])
    layer_parts = third[:, capacity * BLK :, :].astype(jnp.float32)
    layer_parts = layer_parts.reshape(peers, NVIRT * H, 4, 2 * HD)
    layer_part = merge(layer_parts[:, :, 0] + layer_parts[:, :, 1] + layer_parts[:, :, 2])
    around_parts = [layer_part] + [
        lax.ppermute(layer_part, "outer", [((z + turn) % LAYERS, z) for z in range(LAYERS)])
        for turn in range(1, LAYERS)
    ]
    halo = halo_rows + halo_cols
    halo_slots = 2 * (blocks_x + blocks_y)
    state = phase(1, halo, halo_slots, state, [sent, third], big=True)
    state = phase(4, [third], slots, state, [*around_parts[1:]])
    node_out = phase(5, [fourth], slots, state, [], (feats.reshape(nblocks, BLK, D), w_out))
    parts = jnp.stack(
        [
            pick(layer, [around_parts[(origin - z) % LAYERS] for z in range(LAYERS)])
            for origin in range(LAYERS)
        ]
    )

    own_score = (
        jnp.sum(
            (virtual_query.astype(jnp.float32) * virtual_keys.astype(jnp.float32)).reshape(
                NVIRT, H, HD
            ),
            axis=-1,
        )
        * scale
    ).reshape(NVIRT * H)
    part_top = parts[:, :, HD]
    part_total = parts[:, :, HD + HD // 2]
    final_top = jnp.maximum(jnp.max(part_top, axis=0), own_score)
    rescale = jnp.exp(part_top - final_top)
    own_share = jnp.exp(own_score - final_top)
    total = jnp.sum(part_total * rescale, axis=0) + own_share
    accum = jnp.sum(parts[:, :, :HD] * rescale[..., None], axis=0)
    accum = accum + own_share[:, None] * virtual_values.astype(jnp.float32).reshape(NVIRT * H, HD)
    virtual_context = (accum / total[:, None]).astype(jnp.bfloat16).reshape(NVIRT, D)
    virt_out = virt_emb.astype(jnp.float32) + jnp.dot(
        virtual_context, w_out, preferred_element_type=jnp.float32
    )
    return (node_out.reshape(feats.shape), virt_out)


def solution(mesh):
    inner = mesh.shape["row"] // LAYERS
    split = Mesh(mesh.devices.reshape(LAYERS, inner, mesh.shape["col"]), AXES)
    rows = ("outer", "inner")
    return jax.shard_map(
        shards,
        mesh=split,
        in_specs=(
            P(rows, "col", None, None),
            P(),
            P(),
            P(),
            P(),
            P(),
            P(rows, "col", None),
            P(rows, "col", None),
            P(rows, "col", None),
        ),
        out_specs=(P(rows, "col", None, None), P()),
        check_vma=False,
    )
```

```python
import math

import jax
import jax.numpy as jnp
from jax import lax
from jax.experimental import pallas as pl
from jax.experimental.pallas import tpu as pltpu
from jax.sharding import Mesh
from jax.sharding import PartitionSpec as P

D = 512
H = 8
HD = 64
BLK = 128
NEXP = 4
NVIRT = 4

NEG_FILL = -1e30
LAYERS = 4
PHASES = 2 + LAYERS
UNROLL = 4
NEAREST = ((0, 1, 2, 3), (1, 0, 2, 3), (2, 3, 1, 0), (3, 2, 1, 0))
VMEM_LIMIT = 56 * 1024 * 1024
AXES = ("outer", "inner", "col")
TABLE_ROWS = 16


def fold_entry(b, s, q_ref, k_ref, vt_ref, m_ref, l_ref, acc_ref):
    low = lax.broadcasted_iota(jnp.int32, (BLK, 2 * HD), 1) < HD
    zero = jnp.zeros((), jnp.bfloat16)
    columns = pl.ds(pl.multiple_of(s * BLK, BLK), BLK)
    scores = []
    tops = []
    for pair in range(H // 2):
        lanes = slice(pair * 2 * HD, (pair + 1) * 2 * HD)
        query = q_ref[b, :, lanes]
        both = jnp.concatenate([jnp.where(low, query, zero), jnp.where(low, zero, query)], axis=0)
        score = lax.dot_general(
            k_ref[s, :, lanes],
            both,
            (((1,), (1,)), ((), ())),
            preferred_element_type=jnp.float32,
        )
        scores.append(score)
        top = jnp.max(score, axis=0, keepdims=True)
        tops += [top[:, :BLK], top[:, BLK:]]
    m_old = m_ref[b]
    m_new = jnp.maximum(m_old, jnp.concatenate(tops, axis=0))
    alpha = jnp.exp(m_old - m_new)
    m_ref[b] = m_new
    sums = []
    for h in range(H):
        score = scores[h // 2][:, (h % 2) * BLK : (h % 2 + 1) * BLK]
        share = jnp.exp(score - m_new[h : h + 1])
        sums.append(jnp.sum(share, axis=0, keepdims=True))
        rows = slice(h * HD, (h + 1) * HD)
        part = jnp.dot(
            vt_ref[rows, columns], share.astype(jnp.bfloat16), preferred_element_type=jnp.float32
        )
        acc_ref[b, rows, :] = acc_ref[b, rows, :] * alpha[h : h + 1] + part
    l_ref[b] = l_ref[b] * alpha + jnp.concatenate(sums, axis=0)


class Entries:
    def __init__(self, ref):
        self.ref = ref
        self.count = (ref.shape[0] - PHASES - 1) // 2

    def bound(self, phase):
        return self.ref[phase]

    def block(self, entry):
        return self.ref[entry + (PHASES + 1)]

    def slot(self, entry):
        return self.ref[entry + (PHASES + 1 + self.count)]


def fold_range(low, high, entries, own_slots, q_ref, k_ref, vt_ref, m_ref, l_ref, acc_ref):
    def fold(entry):
        slot = entry - low if own_slots else entries.slot(entry)
        fold_entry(entries.block(entry), slot, q_ref, k_ref, vt_ref, m_ref, l_ref, acc_ref)

    def several(step, carry):
        for u in range(UNROLL):
            fold(low + UNROLL * step + u)
        return carry

    def one(entry, carry):
        fold(entry)
        return carry

    full = (high - low) // UNROLL
    lax.fori_loop(0, full, several, 0)
    lax.fori_loop(low + UNROLL * full, high, one, 0)


def open_kernel(table, q_ref, k_ref, vt_ref, ids_ref, vv_ref, m_in, *refs):
    m_ref, l_ref, acc_ref = refs[-3:]
    m_ref[...] = m_in[...]
    l_ref[...] = jnp.ones(l_ref.shape, jnp.float32)

    def open_block(b, carry):
        ids = ids_ref[pl.ds(b, 1), :]
        value = jnp.zeros((D, BLK), jnp.float32)
        for v in range(NVIRT):
            value = jnp.where(ids == v, vv_ref[:, v : v + 1], value)
        acc_ref[b] = value
        return carry

    lax.fori_loop(0, q_ref.shape[0], open_block, 0)
    entries = Entries(table)
    fold_range(
        entries.bound(0), entries.bound(1), entries, False, q_ref, k_ref, vt_ref, m_ref, l_ref, acc_ref
    )


GROUP = 4


def phase_kernel(phase, capacity, nsources, finish, ntokens, *refs):
    refs = list(refs)
    take = lambda count: [refs.pop(0) for _ in range(count)]
    entries = Entries(take(1)[0])
    sources = take(nsources)
    wk_hbm, wv_hbm, q_hbm, m_hbm, l_hbm, acc_hbm = take(6)
    feats_hbm, wo_hbm = take(2) if finish else (None, None)
    take(ntokens)
    if finish:
        (out_hbm,) = take(1)
        m_ref, l_ref, acc_ref = take(3)
        feats_ref, wo_ref, out_ref, out_sems = take(4)
    else:
        m_ref, l_ref, acc_ref = take(3)
    raw_ref, wk_ref, wv_ref, q_ref, k_ref, vt_ref, sems, raw_sems = take(8)
    copies = []

    def fetch(source, target):
        copy = pltpu.make_async_copy(source, target, sems.at[len(copies)])
        copy.start()
        copies.append(copy)

    fetch(wk_hbm, wk_ref)
    fetch(wv_hbm, wv_ref)
    needed = len(copies)
    low = entries.bound(phase)
    high = entries.bound(phase + 1)

    def wanted_block(number):
        return raw_ref.at[pl.ds(pl.multiple_of(number * BLK, BLK), BLK)]

    def start_block(number, carry):
        slot = entries.slot(low + number)
        at = 0
        for source in sources:
            each = capacity if len(sources) == 1 else 1
            count = source.shape[0] * each

            @pl.when((slot >= at) & (slot < at + count))
            def start(source=source, place=slot - at):
                sender = lax.div(place, each)
                rows = pl.ds(pl.multiple_of((place - sender * each) * BLK, BLK), BLK)
                pltpu.make_async_copy(
                    source.at[sender, rows], wanted_block(number), raw_sems.at[number]
                ).start()

            at += count
        return carry

    lax.fori_loop(0, high - low, start_block, 0)
    fetch(q_hbm, q_ref)
    fetch(m_hbm, m_ref)
    fetch(l_hbm, l_ref)
    fetch(acc_hbm, acc_ref)
    if finish:
        fetch(feats_hbm, feats_ref)
        fetch(wo_hbm, wo_ref)
    for copy in copies[:needed]:
        copy.wait()

    def project_group(group, carry):
        for u in range(GROUP):
            number = group * GROUP + u

            @pl.when(number < high - low)
            def arrive(number=number):
                pltpu.make_async_copy(
                    sources[0].at[0, pl.ds(0, BLK)], wanted_block(number), raw_sems.at[number]
                ).wait()

        rows = raw_ref[pl.ds(pl.multiple_of(group * (GROUP * BLK), GROUP * BLK), GROUP * BLK), :]
        keys = jnp.dot(rows, wk_ref[...], preferred_element_type=jnp.float32)
        k_ref[pl.ds(group * GROUP, GROUP)] = keys.astype(jnp.bfloat16).reshape(GROUP, BLK, D)
        values = lax.dot_general(
            wv_ref[...], rows, (((1,), (1,)), ((), ())), preferred_element_type=jnp.float32
        )
        columns = pl.ds(pl.multiple_of(group * (GROUP * BLK), GROUP * BLK), GROUP * BLK)
        vt_ref[:, columns] = values.astype(jnp.bfloat16)
        return carry

    lax.fori_loop(0, (high - low + GROUP - 1) // GROUP, project_group, 0)
    for copy in copies[needed:]:
        copy.wait()
    fold_range(low, high, entries, True, q_ref, k_ref, vt_ref, m_ref, l_ref, acc_ref)
    if not finish:
        return
    nblocks = q_ref.shape[0]

    def write(b):
        return pltpu.make_async_copy(out_ref.at[b], out_hbm.at[b], out_sems.at[b])

    def finish_block(b, carry):
        inverse = 1.0 / l_ref[b]
        context = jnp.concatenate(
            [acc_ref[b, h * HD : (h + 1) * HD, :] * inverse[h : h + 1] for h in range(H)], axis=0
        ).astype(jnp.bfloat16)
        mixed = lax.dot_general(
            context, wo_ref[...], (((0,), (0,)), ((), ())), preferred_element_type=jnp.float32
        )
        out_ref[b] = (feats_ref[b].astype(jnp.float32) + mixed).astype(jnp.bfloat16)
        write(b).start()
        return carry

    def settle(b, carry):
        write(b).wait()
        return carry

    lax.fori_loop(0, nblocks, finish_block, 0, unroll=4)
    lax.fori_loop(0, nblocks, settle, 0)


def pack_kernel(candidates, capacity, nsources, wanted, *refs):
    sources = refs[:nsources]
    extra = refs[nsources]
    out_hbm, out_ref, sems, out_sems = refs[-4:]
    peers = out_ref.shape[0]
    count = peers * capacity

    def block(source, slot):
        return source.at[pl.ds(pl.multiple_of(slot * BLK, BLK), BLK)]

    def place(index):
        return out_ref.at[index // capacity, pl.ds(index % capacity * BLK, BLK)]

    for which in sorted(set(candidates)):
        mine = [wanted[count] == z for z in range(LAYERS) if candidates[z] == which]
        chosen = mine[0]
        for other in mine[1:]:
            chosen = jnp.logical_or(chosen, other)

        @pl.when(chosen)
        def start(source=sources[which]):
            for index in range(count):
                pltpu.make_async_copy(
                    block(source, wanted[index]), place(index), sems.at[index]
                ).start()

    rest = out_ref.shape[1] - capacity * BLK
    if rest:
        for peer in range(peers):
            out_ref[peer, capacity * BLK :, :] = extra[...]
    leaving = [
        pltpu.make_async_copy(out_ref.at[peer], out_hbm.at[peer], out_sems.at[peer])
        for peer in range(peers)
    ]
    for index in range(count):
        pltpu.make_async_copy(block(sources[0], 0), place(index), sems.at[index]).wait()
        if index % capacity == capacity - 1:
            leaving[index // capacity].start()
    for copy in leaving:
        copy.wait()


VMEM = pl.BlockSpec(memory_space=pltpu.VMEM)
SMEM = pl.BlockSpec(memory_space=pltpu.SMEM)
HBM = pl.BlockSpec(memory_space=pl.ANY)


def cost(big):
    return pl.CostEstimate(
        flops=30_000_000_000 if big else 1, bytes_accessed=1, transcendentals=0
    )


def state_shapes(nblocks):
    return [
        jax.ShapeDtypeStruct((nblocks, H, BLK), jnp.float32),
        jax.ShapeDtypeStruct((nblocks, H, BLK), jnp.float32),
        jax.ShapeDtypeStruct((nblocks, D, BLK), jnp.float32),
    ]


def attend_own(entries, q, k, vt, ids, virtual_values, m0, token):
    return pl.pallas_call(
        open_kernel,
        in_specs=[SMEM] + [VMEM] * 6 + [HBM],
        out_specs=[VMEM] * 3,
        out_shape=state_shapes(q.shape[0]),
        compiler_params=pltpu.CompilerParams(vmem_limit_bytes=VMEM_LIMIT),
        cost_estimate=cost(True),
        name="attend_own",
    )(entries, q, k, vt, ids, virtual_values, m0, token)


def attend_phase(phase, entries, sources, slots, w_key, w_value_t, q, state, tokens, last=None, big=False):
    room = -(-slots // GROUP) * GROUP
    capacity = slots // sources[0].shape[0]
    finish = last is not None
    nblocks = q.shape[0]
    block = pltpu.VMEM((nblocks, BLK, D), jnp.bfloat16)
    square = pltpu.VMEM((D, D), jnp.bfloat16)
    shapes = state_shapes(nblocks)
    scratch = [
        pltpu.VMEM((room * BLK, D), jnp.bfloat16),
        square,
        square,
        block,
        pltpu.VMEM((room, BLK, D), jnp.bfloat16),
        pltpu.VMEM((D, room * BLK), jnp.bfloat16),
        pltpu.SemaphoreType.DMA((8,)),
        pltpu.SemaphoreType.DMA((room,)),
    ]
    if finish:
        scratch = (
            [pltpu.VMEM(shape.shape, shape.dtype) for shape in shapes]
            + [block, square, block, pltpu.SemaphoreType.DMA((nblocks,))]
            + scratch
        )
    extra = list(last) if finish else []

    def kernel(*refs):
        phase_kernel(phase, capacity, len(sources), finish, len(tokens), *refs)

    return pl.pallas_call(
        kernel,
        in_specs=[SMEM] + [HBM] * (6 + len(sources) + len(extra) + len(tokens)),
        out_specs=HBM if finish else [VMEM] * 3,
        out_shape=jax.ShapeDtypeStruct((nblocks, BLK, D), jnp.bfloat16) if finish else shapes,
        scratch_shapes=scratch,
        compiler_params=pltpu.CompilerParams(vmem_limit_bytes=VMEM_LIMIT),
        cost_estimate=cost(big),
        name=f"attend_{phase}",
    )(entries, *sources, w_key, w_value_t, q, *state, *extra, *tokens)


def pack(candidates, capacity, wanted, sources, extra, tokens):
    peers = (wanted.shape[0] - 1) // capacity
    rows = capacity * BLK + (0 if extra is None else extra.shape[0])

    def kernel(*refs):
        pack_kernel(candidates, capacity, len(sources), *refs)

    return pl.pallas_call(
        kernel,
        in_specs=[SMEM] + [HBM] * len(sources) + [VMEM] * (extra is not None) + [HBM] * len(tokens),
        out_specs=HBM,
        out_shape=jax.ShapeDtypeStruct((peers, rows, D), jnp.bfloat16),
        scratch_shapes=[
            pltpu.VMEM((peers, rows, D), jnp.bfloat16),
            pltpu.SemaphoreType.DMA((peers * capacity,)),
            pltpu.SemaphoreType.DMA((peers,)),
        ],
        compiler_params=pltpu.CompilerParams(vmem_limit_bytes=VMEM_LIMIT),
        cost_estimate=cost(False),
        name="pack",
    )(wanted, *sources, *([] if extra is None else [extra]), *tokens)


def project(rows, weight):
    return jnp.dot(rows, weight, preferred_element_type=jnp.float32).astype(jnp.bfloat16)


def project_transposed(rows, weight):
    return lax.dot_general(
        weight, rows, (((0,), (1,)), ((), ())), preferred_element_type=jnp.float32
    ).astype(jnp.bfloat16)


def per_head(vectors):
    head = jnp.arange(D, dtype=jnp.int32)[None, None, :] // HD
    mine = head == jnp.arange(H, dtype=jnp.int32)[None, :, None]
    return jnp.where(mine, vectors[:, None, :], jnp.zeros((), vectors.dtype)).reshape(NVIRT * H, D)


def pick(index, choices):
    result = choices[-1]
    for place in range(len(choices) - 2, -1, -1):
        result = jnp.where(index == place, choices[place], result)
    return result


def sources_of(step):
    return ((0, 0, 0, 0), (0, 0, 0, 0), (0, 1, 1, 0), (0, 1, 1, 0))[step]


ENDS = [(0, 1), (1, 0), (2, 3), (3, 2)]
MIDDLE = [(1, 2), (2, 1)]
OUTWARDS = [(1, 0), (2, 3)]


def shards(feats, virt_emb, w_query, w_key, w_value, w_out, link_mask, partners, virt_ids):
    blocks_x, blocks_y = (feats.shape[0], feats.shape[1])
    nblocks = blocks_x * blocks_y
    rows_total = nblocks * BLK
    scale = 1.0 / math.sqrt(HD)
    inner = lax.axis_size("inner")
    cols = lax.axis_size("col")
    mesh_rows = LAYERS * inner
    peers = inner * cols
    devices = LAYERS * peers
    layer = lax.axis_index("outer")
    my_row = layer * inner + lax.axis_index("inner")
    my_col = lax.axis_index("col")
    flat = feats.reshape(rows_total, D)

    slot_count = nblocks * NEXP
    capacity = (slot_count + devices - 2) // (devices - 1)
    grid_cols = blocks_y * cols
    grid_rows = blocks_x * mesh_rows
    order = jnp.arange(slot_count, dtype=jnp.int32)
    own_slot = order % nblocks

    def locate(ids):
        ids = jnp.transpose(ids, (2, 0, 1)).reshape(slot_count)
        row = ids // grid_cols
        col = ids % grid_cols
        device = row // blocks_x * cols + col // blocks_y
        return device, row % blocks_x * blocks_y + col % blocks_y

    def ranks(device, sequence):
        same = device[:, None] == device[None, :]
        return jnp.sum(same & (sequence[None, :] < sequence[:, None]), axis=1)

    dest, partner_slot = locate(partners)
    rank_in = ranks(dest, order // nblocks * nblocks + partner_slot)
    target = dest * capacity + ranks(dest, order)
    hits = target[None, :] == jnp.arange(devices * capacity, dtype=jnp.int32)[:, None]
    wanted = jnp.sum(jnp.where(hits, own_slot[None, :], 0), axis=1).astype(jnp.int32)
    wanted = wanted.reshape(LAYERS, peers * capacity)

    rows = jnp.pad(
        wanted.astype(jnp.bfloat16),
        ((0, TABLE_ROWS - LAYERS), (0, D - peers * capacity)),
    )
    own = jnp.concatenate([flat, rows], axis=0)

    def table(step, sources):
        line = pick(
            layer, [sources[which][rows_total + z] for z, which in enumerate(sources_of(step))]
        )
        return line[: peers * capacity].astype(jnp.int32)

    this_layer = jnp.broadcast_to(layer, (1,)).astype(jnp.int32)

    def hand_round(step, sources, tokens, extra=None):
        slots = pick(layer, list(wanted)) if step == 0 else table(step, sources)
        slots = jnp.concatenate([slots, this_layer])
        sent = pack(
            sources_of(step), capacity, slots, sources, extra, tokens
        )
        return sent, lax.all_to_all(sent, ("inner", "col"), 0, 0, tiled=True)

    end1 = lax.ppermute(own, "outer", ENDS)
    middle1 = lax.ppermute(own, "outer", MIDDLE)
    end2 = lax.ppermute(middle1, "outer", OUTWARDS)
    middle2 = lax.ppermute(end1, "outer", MIDDLE)
    end3 = lax.ppermute(middle2, "outer", OUTWARDS)

    to_next_row = [(r, r + 1) for r in range(inner - 1)]
    to_prev_row = [(r + 1, r) for r in range(inner - 1)]
    to_next_col = [(c, c + 1) for c in range(cols - 1)]
    to_prev_col = [(c + 1, c) for c in range(cols - 1)]
    block = jnp.arange(nblocks, dtype=jnp.int32)
    bx = block // blocks_y
    by = block % blocks_y
    global_row = my_row * blocks_x + bx
    global_col = my_col * blocks_y + by
    links = link_mask.reshape(nblocks, 4) == 1
    in_layer = lax.axis_index("inner")
    from_north = jnp.where(in_layer == 0, 2 * blocks_y, 0)
    from_south = jnp.where(in_layer == inner - 1, 2 * blocks_y, blocks_y)
    north = jnp.where(bx > 0, block - blocks_y, from_north + by)
    south = jnp.where(bx < blocks_x - 1, block + blocks_y, from_south + by)
    west = jnp.where(by > 0, block - 1, 3 * blocks_y + bx)
    east = jnp.where(by < blocks_y - 1, block + 1, 3 * blocks_y + blocks_x + bx)
    dead = PHASES
    near_slots = jnp.concatenate([block, north, south, west, east])
    near_phase = jnp.concatenate(
        [
            jnp.zeros((nblocks,), jnp.int32),
            jnp.where(links[:, 0] & (global_row > 0), jnp.where(bx > 0, 0, 1), dead),
            jnp.where(
                links[:, 1] & (global_row < grid_rows - 1),
                jnp.where(bx < blocks_x - 1, 0, 1),
                dead,
            ),
            jnp.where(links[:, 2] & (global_col > 0), jnp.where(by > 0, 0, 1), dead),
            jnp.where(
                links[:, 3] & (global_col < grid_cols - 1),
                jnp.where(by < blocks_y - 1, 0, 1),
                dead,
            ),
        ]
    )
    from_layer = dest // peers
    steps = [
        pick(from_layer, [jnp.int32(NEAREST[z].index(origin)) for origin in range(LAYERS)])
        for z in range(LAYERS)
    ]
    far_phase = 2 + pick(layer, steps)
    far_slots = dest % peers * capacity + rank_in
    entry_block = jnp.concatenate([jnp.tile(block, 5), own_slot])
    entry_slot = jnp.concatenate([near_slots, far_slots])
    entry_phase = jnp.concatenate([near_phase, far_phase])
    count = entry_block.shape[0]
    number = jnp.arange(count, dtype=jnp.int32)
    sort_key = entry_phase * count + number
    place = jnp.sum(sort_key[None, :] < sort_key[:, None], axis=1)
    at_place = place[None, :] == number[:, None]
    sorted_block = jnp.sum(jnp.where(at_place, entry_block[None, :], 0), axis=1).astype(jnp.int32)
    sorted_slot = jnp.sum(jnp.where(at_place, entry_slot[None, :], 0), axis=1).astype(jnp.int32)
    bounds = jnp.sum(
        entry_phase[None, :] < jnp.arange(dead + 1, dtype=jnp.int32)[:, None], axis=1
    ).astype(jnp.int32)
    entries = jnp.concatenate([bounds, sorted_block, sorted_slot])

    sent, first = hand_round(0, [own], [])
    halo_rows = [
        lax.ppermute(part, "inner", steps)
        for part, steps in zip(
            lax.optimization_barrier((feats[-1], feats[0], sent))[:2], (to_next_row, to_prev_row)
        )
    ]
    place = lax.axis_index("inner")
    edge = blocks_y * BLK
    before = jnp.where(layer == 2, middle1[rows_total - edge : rows_total], end1[rows_total - edge : rows_total])
    after = jnp.where(layer == 1, middle1[:edge], end1[:edge])
    crossing = jnp.where(place == 0, after, before).reshape(blocks_y, BLK, D)
    halo_rows.append(lax.ppermute(crossing, "inner", [(0, inner - 1), (inner - 1, 0)]))
    flat, _ = lax.optimization_barrier((flat, sent))

    queries = project(flat, w_query)
    scaled = (queries * jnp.bfloat16(scale)).reshape(nblocks, BLK, D)
    keys = project(flat, w_key)
    values_t = project_transposed(flat, w_value)
    virtual_query = project(virt_emb, w_query)
    virtual_keys = project(virt_emb, w_key)
    virtual_values = project(virt_emb, w_value)

    slots_v = jnp.arange(NVIRT, dtype=jnp.int32)
    chosen = virt_ids.reshape(1, nblocks, BLK) == slots_v[:, None, None]
    virtual_score = lax.dot_general(
        per_head(virtual_keys),
        scaled.reshape(rows_total, D),
        (((1,), (1,)), ((), ())),
        preferred_element_type=jnp.float32,
    ).reshape(NVIRT, H, nblocks, BLK)
    m0 = jnp.transpose(jnp.sum(jnp.where(chosen[:, None], virtual_score, 0.0), axis=0), (1, 0, 2))
    values_wide = jnp.zeros((D, BLK), jnp.float32)
    values_wide = values_wide.at[:, :NVIRT].set(virtual_values.astype(jnp.float32).T)

    member = chosen.reshape(NVIRT, 1, rows_total)
    node_scores = lax.dot_general(
        per_head(virtual_query), keys, (((1,), (1,)), ((), ())), preferred_element_type=jnp.float32
    ).reshape(NVIRT, H, rows_total) * scale
    node_scores = jnp.where(member, node_scores, NEG_FILL)
    local_top = jnp.max(node_scores, axis=-1)
    shares = jnp.where(member, jnp.exp(node_scores - local_top[..., None]), 0.0)
    local_total = jnp.sum(shares, axis=-1)
    weighted = lax.dot_general(
        shares.reshape(NVIRT * H, rows_total),
        values_t.astype(jnp.float32),
        (((1,), (1,)), ((), ())),
        precision=lax.Precision.HIGHEST,
        preferred_element_type=jnp.float32,
    ).reshape(NVIRT, H, H, HD)
    same_head = jnp.arange(H)[:, None] == jnp.arange(H)[None, :]
    local_accum = jnp.sum(jnp.where(same_head[None, :, :, None], weighted, 0.0), axis=2)
    packed = jnp.concatenate(
        [
            local_accum.reshape(NVIRT * H, HD),
            jnp.broadcast_to(local_top.reshape(NVIRT * H, 1), (NVIRT * H, HD // 2)),
            jnp.broadcast_to(local_total.reshape(NVIRT * H, 1), (NVIRT * H, HD // 2)),
        ],
        axis=1,
    )
    planes = []
    left = packed
    for _ in range(3):
        plane = lax.reduce_precision(left, 8, 7)
        planes.append(plane.astype(jnp.bfloat16))
        left = left - plane
    planes = jnp.concatenate(planes + [jnp.zeros_like(planes[0])], axis=1)

    def merge(parts):
        tops = parts[:, :, HD : HD + 1]
        top = jnp.max(tops, axis=0)
        rescale = jnp.exp(tops - top)
        accum = jnp.sum(parts[:, :, :HD] * rescale, axis=0)
        total = jnp.sum(parts[:, :, HD + HD // 2 :] * rescale, axis=0)
        return jnp.concatenate([accum, jnp.broadcast_to(top, (NVIRT * H, HD // 2)), total], axis=1)

    w_value_t = w_value.T
    keys = keys.reshape(nblocks, BLK, D)

    def phase(number, sources, slots, state, tokens, last=None, big=False):
        return attend_phase(
            number, entries, sources, slots, w_key, w_value_t, scaled, state, tokens, last, big
        )

    slots = peers * capacity
    packed, m0, keys, values_t, scaled = lax.optimization_barrier(
        (packed, m0, keys, values_t, scaled)
    )
    sent, second = hand_round(1, [end1], [m0, packed])
    state = attend_own(
        entries, scaled, keys, values_t, virt_ids.reshape(nblocks, BLK), values_wide, m0, sent
    )
    sent, third = hand_round(2, [end2, middle1], [state[1]], planes)
    state = phase(2, [first], slots, state, [sent, second, *halo_rows], big=True)
    halo_cols = [
        lax.ppermute(part, "col", steps)
        for part, steps in zip(
            lax.optimization_barrier((feats[:, -1], feats[:, 0], state[1]))[:2],
            (to_next_col, to_prev_col),
        )
    ]
    state = phase(3, [second], slots, state, [])
    sent, fourth = hand_round(3, [end3, middle2], [state[1]])
    layer_parts = third[:, capacity * BLK :, :].astype(jnp.float32)
    layer_parts = layer_parts.reshape(peers, NVIRT * H, 4, 2 * HD)
    layer_part = merge(layer_parts[:, :, 0] + layer_parts[:, :, 1] + layer_parts[:, :, 2])
    around_parts = [layer_part] + [
        lax.ppermute(layer_part, "outer", [((z + turn) % LAYERS, z) for z in range(LAYERS)])
        for turn in range(1, LAYERS)
    ]
    halo = halo_rows + halo_cols
    halo_slots = 3 * blocks_y + 2 * blocks_x
    state = phase(1, halo, halo_slots, state, [sent, third], big=True)
    state = phase(4, [third], slots, state, [*around_parts[1:]])
    node_out = phase(5, [fourth], slots, state, [], (feats.reshape(nblocks, BLK, D), w_out))
    parts = jnp.stack(
        [
            pick(layer, [around_parts[(origin - z) % LAYERS] for z in range(LAYERS)])
            for origin in range(LAYERS)
        ]
    )

    own_score = (
        jnp.sum(
            (virtual_query.astype(jnp.float32) * virtual_keys.astype(jnp.float32)).reshape(
                NVIRT, H, HD
            ),
            axis=-1,
        )
        * scale
    ).reshape(NVIRT * H)
    part_top = parts[:, :, HD]
    part_total = parts[:, :, HD + HD // 2]
    final_top = jnp.maximum(jnp.max(part_top, axis=0), own_score)
    rescale = jnp.exp(part_top - final_top)
    own_share = jnp.exp(own_score - final_top)
    total = jnp.sum(part_total * rescale, axis=0) + own_share
    accum = jnp.sum(parts[:, :, :HD] * rescale[..., None], axis=0)
    accum = accum + own_share[:, None] * virtual_values.astype(jnp.float32).reshape(NVIRT * H, HD)
    virtual_context = (accum / total[:, None]).astype(jnp.bfloat16).reshape(NVIRT, D)
    virt_out = virt_emb.astype(jnp.float32) + jnp.dot(
        virtual_context, w_out, preferred_element_type=jnp.float32
    )
    return (node_out.reshape(feats.shape), virt_out)


def solution(mesh):
    inner = mesh.shape["row"] // LAYERS
    split = Mesh(mesh.devices.reshape(LAYERS, inner, mesh.shape["col"]), AXES)
    rows = ("outer", "inner")
    return jax.shard_map(
        shards,
        mesh=split,
        in_specs=(
            P(rows, "col", None, None),
            P(),
            P(),
            P(),
            P(),
            P(),
            P(rows, "col", None),
            P(rows, "col", None),
            P(rows, "col", None),
        ),
        out_specs=(P(rows, "col", None, None), P()),
        check_vma=False,
    )
```

```python
import math

import jax
import jax.numpy as jnp
from jax import lax
from jax.experimental import pallas as pl
from jax.experimental.pallas import tpu as pltpu
from jax.sharding import Mesh
from jax.sharding import PartitionSpec as P

D = 512
H = 8
HD = 64
BLK = 128
NEXP = 4
NVIRT = 4

NEG_FILL = -1e30
LAYERS = 4
PHASES = 2 + LAYERS
UNROLL = 4
NEAREST = ((0, 1, 2, 3), (1, 0, 2, 3), (2, 3, 1, 0), (3, 2, 1, 0))
VMEM_LIMIT = 56 * 1024 * 1024
AXES = ("outer", "inner", "col")
TABLE_ROWS = 16


def fold_entry(b, s, q_ref, k_ref, vt_ref, m_ref, l_ref, acc_ref):
    low = lax.broadcasted_iota(jnp.int32, (BLK, 2 * HD), 1) < HD
    zero = jnp.zeros((), jnp.bfloat16)
    columns = pl.ds(pl.multiple_of(s * BLK, BLK), BLK)
    scores = []
    tops = []
    for pair in range(H // 2):
        lanes = slice(pair * 2 * HD, (pair + 1) * 2 * HD)
        query = q_ref[b, :, lanes]
        both = jnp.concatenate([jnp.where(low, query, zero), jnp.where(low, zero, query)], axis=0)
        score = lax.dot_general(
            k_ref[s, :, lanes],
            both,
            (((1,), (1,)), ((), ())),
            preferred_element_type=jnp.float32,
        )
        scores.append(score)
        top = jnp.max(score, axis=0, keepdims=True)
        tops += [top[:, :BLK], top[:, BLK:]]
    m_old = m_ref[b]
    m_new = jnp.maximum(m_old, jnp.concatenate(tops, axis=0))
    alpha = jnp.exp(m_old - m_new)
    m_ref[b] = m_new
    sums = []
    for h in range(H):
        score = scores[h // 2][:, (h % 2) * BLK : (h % 2 + 1) * BLK]
        share = jnp.exp(score - m_new[h : h + 1])
        sums.append(jnp.sum(share, axis=0, keepdims=True))
        rows = slice(h * HD, (h + 1) * HD)
        part = jnp.dot(
            vt_ref[rows, columns], share.astype(jnp.bfloat16), preferred_element_type=jnp.float32
        )
        acc_ref[b, rows, :] = acc_ref[b, rows, :] * alpha[h : h + 1] + part
    l_ref[b] = l_ref[b] * alpha + jnp.concatenate(sums, axis=0)


class Entries:
    def __init__(self, ref):
        self.ref = ref
        self.count = (ref.shape[0] - PHASES - 1) // 2

    def bound(self, phase):
        return self.ref[phase]

    def block(self, entry):
        return self.ref[entry + (PHASES + 1)]

    def slot(self, entry):
        return self.ref[entry + (PHASES + 1 + self.count)]


def fold_range(low, high, entries, own_slots, q_ref, k_ref, vt_ref, m_ref, l_ref, acc_ref):
    def fold(entry):
        slot = entry - low if own_slots else entries.slot(entry)
        fold_entry(entries.block(entry), slot, q_ref, k_ref, vt_ref, m_ref, l_ref, acc_ref)

    def several(step, carry):
        for u in range(UNROLL):
            fold(low + UNROLL * step + u)
        return carry

    def one(entry, carry):
        fold(entry)
        return carry

    full = (high - low) // UNROLL
    lax.fori_loop(0, full, several, 0)
    lax.fori_loop(low + UNROLL * full, high, one, 0)


def open_kernel(table, q_ref, k_ref, vt_ref, ids_ref, vv_ref, m_in, *refs):
    m_ref, l_ref, acc_ref = refs[-3:]
    m_ref[...] = m_in[...]
    l_ref[...] = jnp.ones(l_ref.shape, jnp.float32)

    def open_block(b, carry):
        ids = ids_ref[pl.ds(b, 1), :]
        value = jnp.zeros((D, BLK), jnp.float32)
        for v in range(NVIRT):
            value = jnp.where(ids == v, vv_ref[:, v : v + 1], value)
        acc_ref[b] = value
        return carry

    lax.fori_loop(0, q_ref.shape[0], open_block, 0)
    entries = Entries(table)
    fold_range(
        entries.bound(0), entries.bound(1), entries, False, q_ref, k_ref, vt_ref, m_ref, l_ref, acc_ref
    )


GROUP = 4


def phase_kernel(phase, capacity, nsources, finish, ntokens, *refs):
    refs = list(refs)
    take = lambda count: [refs.pop(0) for _ in range(count)]
    entries = Entries(take(1)[0])
    sources = take(nsources)
    wk_hbm, wv_hbm, q_hbm, m_hbm, l_hbm, acc_hbm = take(6)
    feats_hbm, wo_hbm = take(2) if finish else (None, None)
    take(ntokens)
    if finish:
        (out_hbm,) = take(1)
        m_ref, l_ref, acc_ref = take(3)
        feats_ref, wo_ref, out_ref, out_sems = take(4)
    else:
        m_ref, l_ref, acc_ref = take(3)
    raw_ref, wk_ref, wv_ref, q_ref, k_ref, vt_ref, sems, raw_sems = take(8)
    copies = []

    def fetch(source, target):
        copy = pltpu.make_async_copy(source, target, sems.at[len(copies)])
        copy.start()
        copies.append(copy)

    fetch(wk_hbm, wk_ref)
    fetch(wv_hbm, wv_ref)
    needed = len(copies)
    low = entries.bound(phase)
    high = entries.bound(phase + 1)

    def wanted_block(number):
        return raw_ref.at[pl.ds(pl.multiple_of(number * BLK, BLK), BLK)]

    def start_block(number, carry):
        slot = entries.slot(low + number)
        at = 0
        for source in sources:
            each = capacity if len(sources) == 1 else 1
            count = source.shape[0] * each

            @pl.when((slot >= at) & (slot < at + count))
            def start(source=source, place=slot - at):
                sender = lax.div(place, each)
                rows = pl.ds(pl.multiple_of((place - sender * each) * BLK, BLK), BLK)
                pltpu.make_async_copy(
                    source.at[sender, rows], wanted_block(number), raw_sems.at[number]
                ).start()

            at += count
        return carry

    lax.fori_loop(0, high - low, start_block, 0)
    fetch(q_hbm, q_ref)
    fetch(m_hbm, m_ref)
    fetch(l_hbm, l_ref)
    fetch(acc_hbm, acc_ref)
    if finish:
        fetch(feats_hbm, feats_ref)
        fetch(wo_hbm, wo_ref)
    for copy in copies[:needed]:
        copy.wait()

    def project_group(group, carry):
        for u in range(GROUP):
            number = group * GROUP + u

            @pl.when(number < high - low)
            def arrive(number=number):
                pltpu.make_async_copy(
                    sources[0].at[0, pl.ds(0, BLK)], wanted_block(number), raw_sems.at[number]
                ).wait()

        rows = raw_ref[pl.ds(pl.multiple_of(group * (GROUP * BLK), GROUP * BLK), GROUP * BLK), :]
        keys = jnp.dot(rows, wk_ref[...], preferred_element_type=jnp.float32)
        k_ref[pl.ds(group * GROUP, GROUP)] = keys.astype(jnp.bfloat16).reshape(GROUP, BLK, D)
        values = lax.dot_general(
            wv_ref[...], rows, (((1,), (1,)), ((), ())), preferred_element_type=jnp.float32
        )
        columns = pl.ds(pl.multiple_of(group * (GROUP * BLK), GROUP * BLK), GROUP * BLK)
        vt_ref[:, columns] = values.astype(jnp.bfloat16)
        return carry

    lax.fori_loop(0, (high - low + GROUP - 1) // GROUP, project_group, 0)
    for copy in copies[needed:]:
        copy.wait()
    fold_range(low, high, entries, True, q_ref, k_ref, vt_ref, m_ref, l_ref, acc_ref)
    if not finish:
        return
    nblocks = q_ref.shape[0]

    def write(b):
        return pltpu.make_async_copy(out_ref.at[b], out_hbm.at[b], out_sems.at[b])

    def finish_block(b, carry):
        inverse = 1.0 / l_ref[b]
        context = jnp.concatenate(
            [acc_ref[b, h * HD : (h + 1) * HD, :] * inverse[h : h + 1] for h in range(H)], axis=0
        ).astype(jnp.bfloat16)
        mixed = lax.dot_general(
            context, wo_ref[...], (((0,), (0,)), ((), ())), preferred_element_type=jnp.float32
        )
        out_ref[b] = (feats_ref[b].astype(jnp.float32) + mixed).astype(jnp.bfloat16)
        write(b).start()
        return carry

    def settle(b, carry):
        write(b).wait()
        return carry

    lax.fori_loop(0, nblocks, finish_block, 0, unroll=4)
    lax.fori_loop(0, nblocks, settle, 0)


def pack_kernel(candidates, capacity, nsources, wanted, *refs):
    sources = refs[:nsources]
    extra = refs[nsources]
    out_hbm, out_ref, sems, out_sems = refs[-4:]
    peers = out_ref.shape[0]
    count = peers * capacity

    def block(source, slot):
        return source.at[pl.ds(pl.multiple_of(slot * BLK, BLK), BLK)]

    def place(index):
        return out_ref.at[index // capacity, pl.ds(index % capacity * BLK, BLK)]

    for which in sorted(set(candidates)):
        mine = [wanted[count] == z for z in range(LAYERS) if candidates[z] == which]
        chosen = mine[0]
        for other in mine[1:]:
            chosen = jnp.logical_or(chosen, other)

        @pl.when(chosen)
        def start(source=sources[which]):
            for index in range(count):
                pltpu.make_async_copy(
                    block(source, wanted[index]), place(index), sems.at[index]
                ).start()

    rest = out_ref.shape[1] - capacity * BLK
    if rest:
        for peer in range(peers):
            out_ref[peer, capacity * BLK :, :] = extra[...]
    leaving = [
        pltpu.make_async_copy(out_ref.at[peer], out_hbm.at[peer], out_sems.at[peer])
        for peer in range(peers)
    ]
    for index in range(count):
        pltpu.make_async_copy(block(sources[0], 0), place(index), sems.at[index]).wait()
        if index % capacity == capacity - 1:
            leaving[index // capacity].start()
    for copy in leaving:
        copy.wait()


VMEM = pl.BlockSpec(memory_space=pltpu.VMEM)
SMEM = pl.BlockSpec(memory_space=pltpu.SMEM)
HBM = pl.BlockSpec(memory_space=pl.ANY)


def cost(big):
    return pl.CostEstimate(
        flops=30_000_000_000 if big else 1, bytes_accessed=1, transcendentals=0
    )


def state_shapes(nblocks):
    return [
        jax.ShapeDtypeStruct((nblocks, H, BLK), jnp.float32),
        jax.ShapeDtypeStruct((nblocks, H, BLK), jnp.float32),
        jax.ShapeDtypeStruct((nblocks, D, BLK), jnp.float32),
    ]


def attend_own(entries, q, k, vt, ids, virtual_values, m0, token):
    return pl.pallas_call(
        open_kernel,
        in_specs=[SMEM] + [VMEM] * 6 + [HBM],
        out_specs=[VMEM] * 3,
        out_shape=state_shapes(q.shape[0]),
        compiler_params=pltpu.CompilerParams(vmem_limit_bytes=VMEM_LIMIT),
        cost_estimate=cost(True),
        name="attend_own",
    )(entries, q, k, vt, ids, virtual_values, m0, token)


def attend_phase(phase, entries, sources, slots, w_key, w_value_t, q, state, tokens, last=None, big=False):
    room = -(-slots // GROUP) * GROUP
    capacity = slots // sources[0].shape[0]
    finish = last is not None
    nblocks = q.shape[0]
    block = pltpu.VMEM((nblocks, BLK, D), jnp.bfloat16)
    square = pltpu.VMEM((D, D), jnp.bfloat16)
    shapes = state_shapes(nblocks)
    scratch = [
        pltpu.VMEM((room * BLK, D), jnp.bfloat16),
        square,
        square,
        block,
        pltpu.VMEM((room, BLK, D), jnp.bfloat16),
        pltpu.VMEM((D, room * BLK), jnp.bfloat16),
        pltpu.SemaphoreType.DMA((8,)),
        pltpu.SemaphoreType.DMA((room,)),
    ]
    if finish:
        scratch = (
            [pltpu.VMEM(shape.shape, shape.dtype) for shape in shapes]
            + [block, square, block, pltpu.SemaphoreType.DMA((nblocks,))]
            + scratch
        )
    extra = list(last) if finish else []

    def kernel(*refs):
        phase_kernel(phase, capacity, len(sources), finish, len(tokens), *refs)

    return pl.pallas_call(
        kernel,
        in_specs=[SMEM] + [HBM] * (6 + len(sources) + len(extra) + len(tokens)),
        out_specs=HBM if finish else [VMEM] * 3,
        out_shape=jax.ShapeDtypeStruct((nblocks, BLK, D), jnp.bfloat16) if finish else shapes,
        scratch_shapes=scratch,
        compiler_params=pltpu.CompilerParams(vmem_limit_bytes=VMEM_LIMIT),
        cost_estimate=cost(big),
        name=f"attend_{phase}",
    )(entries, *sources, w_key, w_value_t, q, *state, *extra, *tokens)


def pack(candidates, capacity, wanted, sources, extra, tokens):
    peers = (wanted.shape[0] - 1) // capacity
    rows = capacity * BLK + (0 if extra is None else extra.shape[0])

    def kernel(*refs):
        pack_kernel(candidates, capacity, len(sources), *refs)

    return pl.pallas_call(
        kernel,
        in_specs=[SMEM] + [HBM] * len(sources) + [VMEM] * (extra is not None) + [HBM] * len(tokens),
        out_specs=HBM,
        out_shape=jax.ShapeDtypeStruct((peers, rows, D), jnp.bfloat16),
        scratch_shapes=[
            pltpu.VMEM((peers, rows, D), jnp.bfloat16),
            pltpu.SemaphoreType.DMA((peers * capacity,)),
            pltpu.SemaphoreType.DMA((peers,)),
        ],
        compiler_params=pltpu.CompilerParams(vmem_limit_bytes=VMEM_LIMIT),
        cost_estimate=cost(False),
        name="pack",
    )(wanted, *sources, *([] if extra is None else [extra]), *tokens)


def project(rows, weight):
    return jnp.dot(rows, weight, preferred_element_type=jnp.float32).astype(jnp.bfloat16)


def project_transposed(rows, weight):
    return lax.dot_general(
        weight, rows, (((0,), (1,)), ((), ())), preferred_element_type=jnp.float32
    ).astype(jnp.bfloat16)


def per_head(vectors):
    head = jnp.arange(D, dtype=jnp.int32)[None, None, :] // HD
    mine = head == jnp.arange(H, dtype=jnp.int32)[None, :, None]
    return jnp.where(mine, vectors[:, None, :], jnp.zeros((), vectors.dtype)).reshape(NVIRT * H, D)


def pick(index, choices):
    result = choices[-1]
    for place in range(len(choices) - 2, -1, -1):
        result = jnp.where(index == place, choices[place], result)
    return result


def sources_of(step):
    return ((0, 0, 0, 0), (0, 0, 0, 0), (0, 1, 1, 0), (0, 1, 1, 0))[step]


ENDS = [(0, 1), (1, 0), (2, 3), (3, 2)]
MIDDLE = [(1, 2), (2, 1)]
OUTWARDS = [(1, 0), (2, 3)]


def shards(feats, virt_emb, w_query, w_key, w_value, w_out, link_mask, partners, virt_ids):
    blocks_x, blocks_y = (feats.shape[0], feats.shape[1])
    nblocks = blocks_x * blocks_y
    rows_total = nblocks * BLK
    scale = 1.0 / math.sqrt(HD)
    inner = lax.axis_size("inner")
    cols = lax.axis_size("col")
    mesh_rows = LAYERS * inner
    peers = inner * cols
    devices = LAYERS * peers
    layer = lax.axis_index("outer")
    my_row = layer * inner + lax.axis_index("inner")
    my_col = lax.axis_index("col")
    flat = feats.reshape(rows_total, D)

    slot_count = nblocks * NEXP
    capacity = (slot_count + devices - 2) // (devices - 1)
    grid_cols = blocks_y * cols
    grid_rows = blocks_x * mesh_rows
    order = jnp.arange(slot_count, dtype=jnp.int32)
    own_slot = order % nblocks

    def locate(ids):
        ids = jnp.transpose(ids, (2, 0, 1)).reshape(slot_count)
        row = ids // grid_cols
        col = ids % grid_cols
        device = row // blocks_x * cols + col // blocks_y
        return device, row % blocks_x * blocks_y + col % blocks_y

    def ranks(device, sequence):
        same = device[:, None] == device[None, :]
        return jnp.sum(same & (sequence[None, :] < sequence[:, None]), axis=1)

    dest, partner_slot = locate(partners)
    rank_in = ranks(dest, order // nblocks * nblocks + partner_slot)
    target = dest * capacity + ranks(dest, order)
    hits = target[None, :] == jnp.arange(devices * capacity, dtype=jnp.int32)[:, None]
    wanted = jnp.sum(jnp.where(hits, own_slot[None, :], 0), axis=1).astype(jnp.int32)
    wanted = wanted.reshape(LAYERS, peers * capacity)

    rows = jnp.pad(
        wanted.astype(jnp.bfloat16),
        ((0, TABLE_ROWS - LAYERS), (0, D - peers * capacity)),
    )
    own = jnp.concatenate([flat, rows], axis=0)

    def table(step, sources):
        line = pick(
            layer, [sources[which][rows_total + z] for z, which in enumerate(sources_of(step))]
        )
        return line[: peers * capacity].astype(jnp.int32)

    this_layer = jnp.broadcast_to(layer, (1,)).astype(jnp.int32)

    def hand_round(step, sources, tokens, extra=None):
        slots = pick(layer, list(wanted)) if step == 0 else table(step, sources)
        slots = jnp.concatenate([slots, this_layer])
        sent = pack(
            sources_of(step), capacity, slots, sources, extra, tokens
        )
        return sent, lax.all_to_all(sent, ("inner", "col"), 0, 0, tiled=True)

    end1 = lax.ppermute(own, "outer", ENDS)
    middle1 = lax.ppermute(own, "outer", MIDDLE)
    end2 = lax.ppermute(middle1, "outer", OUTWARDS)
    middle2 = lax.ppermute(end1, "outer", MIDDLE)
    end3 = lax.ppermute(middle2, "outer", OUTWARDS)

    to_next_row = [(r, r + 1) for r in range(inner - 1)]
    to_prev_row = [(r + 1, r) for r in range(inner - 1)]
    to_next_col = [(c, c + 1) for c in range(cols - 1)]
    to_prev_col = [(c + 1, c) for c in range(cols - 1)]
    block = jnp.arange(nblocks, dtype=jnp.int32)
    bx = block // blocks_y
    by = block % blocks_y
    global_row = my_row * blocks_x + bx
    global_col = my_col * blocks_y + by
    links = link_mask.reshape(nblocks, 4) == 1
    in_layer = lax.axis_index("inner")
    from_north = jnp.where(in_layer == 0, 2 * blocks_y, 0)
    from_south = jnp.where(in_layer == inner - 1, 2 * blocks_y, blocks_y)
    north = jnp.where(bx > 0, block - blocks_y, from_north + by)
    south = jnp.where(bx < blocks_x - 1, block + blocks_y, from_south + by)
    west = jnp.where(by > 0, block - 1, 3 * blocks_y + bx)
    east = jnp.where(by < blocks_y - 1, block + 1, 3 * blocks_y + blocks_x + bx)
    dead = PHASES
    near_slots = jnp.concatenate([block, north, south, west, east])
    near_phase = jnp.concatenate(
        [
            jnp.zeros((nblocks,), jnp.int32),
            jnp.where(links[:, 0] & (global_row > 0), jnp.where(bx > 0, 0, 1), dead),
            jnp.where(
                links[:, 1] & (global_row < grid_rows - 1),
                jnp.where(bx < blocks_x - 1, 0, 1),
                dead,
            ),
            jnp.where(links[:, 2] & (global_col > 0), jnp.where(by > 0, 0, 1), dead),
            jnp.where(
                links[:, 3] & (global_col < grid_cols - 1),
                jnp.where(by < blocks_y - 1, 0, 1),
                dead,
            ),
        ]
    )
    from_layer = dest // peers
    steps = [
        pick(from_layer, [jnp.int32(NEAREST[z].index(origin)) for origin in range(LAYERS)])
        for z in range(LAYERS)
    ]
    far_phase = 2 + pick(layer, steps)
    far_slots = dest % peers * capacity + rank_in
    entry_block = jnp.concatenate([jnp.tile(block, 5), own_slot])
    entry_slot = jnp.concatenate([near_slots, far_slots])
    entry_phase = jnp.concatenate([near_phase, far_phase])
    count = entry_block.shape[0]
    number = jnp.arange(count, dtype=jnp.int32)
    sort_key = entry_phase * count + number
    place = jnp.sum(sort_key[None, :] < sort_key[:, None], axis=1)
    at_place = place[None, :] == number[:, None]
    sorted_block = jnp.sum(jnp.where(at_place, entry_block[None, :], 0), axis=1).astype(jnp.int32)
    sorted_slot = jnp.sum(jnp.where(at_place, entry_slot[None, :], 0), axis=1).astype(jnp.int32)
    bounds = jnp.sum(
        entry_phase[None, :] < jnp.arange(dead + 1, dtype=jnp.int32)[:, None], axis=1
    ).astype(jnp.int32)
    entries = jnp.concatenate([bounds, sorted_block, sorted_slot])

    sent, first = hand_round(0, [own], [])
    halo_rows = [
        lax.ppermute(part, "inner", steps)
        for part, steps in zip(
            lax.optimization_barrier((feats[-1], feats[0], sent))[:2], (to_next_row, to_prev_row)
        )
    ]
    place = lax.axis_index("inner")
    edge = blocks_y * BLK
    before = jnp.where(layer == 2, middle1[rows_total - edge : rows_total], end1[rows_total - edge : rows_total])
    after = jnp.where(layer == 1, middle1[:edge], end1[:edge])
    crossing = jnp.where(place == 0, after, before).reshape(blocks_y, BLK, D)
    flat, _ = lax.optimization_barrier((flat, sent))

    queries = project(flat, w_query)
    scaled = (queries * jnp.bfloat16(scale)).reshape(nblocks, BLK, D)
    keys = project(flat, w_key)
    values_t = project_transposed(flat, w_value)
    virtual_query = project(virt_emb, w_query)
    virtual_keys = project(virt_emb, w_key)
    virtual_values = project(virt_emb, w_value)

    slots_v = jnp.arange(NVIRT, dtype=jnp.int32)
    chosen = virt_ids.reshape(1, nblocks, BLK) == slots_v[:, None, None]
    virtual_score = lax.dot_general(
        per_head(virtual_keys),
        scaled.reshape(rows_total, D),
        (((1,), (1,)), ((), ())),
        preferred_element_type=jnp.float32,
    ).reshape(NVIRT, H, nblocks, BLK)
    m0 = jnp.transpose(jnp.sum(jnp.where(chosen[:, None], virtual_score, 0.0), axis=0), (1, 0, 2))
    values_wide = jnp.zeros((D, BLK), jnp.float32)
    values_wide = values_wide.at[:, :NVIRT].set(virtual_values.astype(jnp.float32).T)

    member = chosen.reshape(NVIRT, 1, rows_total)
    node_scores = lax.dot_general(
        per_head(virtual_query), keys, (((1,), (1,)), ((), ())), preferred_element_type=jnp.float32
    ).reshape(NVIRT, H, rows_total) * scale
    node_scores = jnp.where(member, node_scores, NEG_FILL)
    local_top = jnp.max(node_scores, axis=-1)
    shares = jnp.where(member, jnp.exp(node_scores - local_top[..., None]), 0.0)
    local_total = jnp.sum(shares, axis=-1)
    weighted = lax.dot_general(
        shares.reshape(NVIRT * H, rows_total),
        values_t.astype(jnp.float32),
        (((1,), (1,)), ((), ())),
        precision=lax.Precision.HIGHEST,
        preferred_element_type=jnp.float32,
    ).reshape(NVIRT, H, H, HD)
    same_head = jnp.arange(H)[:, None] == jnp.arange(H)[None, :]
    local_accum = jnp.sum(jnp.where(same_head[None, :, :, None], weighted, 0.0), axis=2)
    packed = jnp.concatenate(
        [
            local_accum.reshape(NVIRT * H, HD),
            jnp.broadcast_to(local_top.reshape(NVIRT * H, 1), (NVIRT * H, HD // 2)),
            jnp.broadcast_to(local_total.reshape(NVIRT * H, 1), (NVIRT * H, HD // 2)),
        ],
        axis=1,
    )
    planes = []
    left = packed
    for _ in range(3):
        plane = lax.reduce_precision(left, 8, 7)
        planes.append(plane.astype(jnp.bfloat16))
        left = left - plane
    planes = jnp.concatenate(planes + [jnp.zeros_like(planes[0])], axis=1)

    def merge(parts):
        tops = parts[:, :, HD : HD + 1]
        top = jnp.max(tops, axis=0)
        rescale = jnp.exp(tops - top)
        accum = jnp.sum(parts[:, :, :HD] * rescale, axis=0)
        total = jnp.sum(parts[:, :, HD + HD // 2 :] * rescale, axis=0)
        return jnp.concatenate([accum, jnp.broadcast_to(top, (NVIRT * H, HD // 2)), total], axis=1)

    w_value_t = w_value.T
    keys = keys.reshape(nblocks, BLK, D)

    def phase(number, sources, slots, state, tokens, last=None, big=False):
        return attend_phase(
            number, entries, sources, slots, w_key, w_value_t, scaled, state, tokens, last, big
        )

    slots = peers * capacity
    packed, m0, keys, values_t, scaled = lax.optimization_barrier(
        (packed, m0, keys, values_t, scaled)
    )
    sent, second = hand_round(1, [end1], [m0, packed])
    crossing, _ = lax.optimization_barrier((crossing, sent))
    halo_rows.append(lax.ppermute(crossing, "inner", [(0, inner - 1), (inner - 1, 0)]))
    state = attend_own(
        entries, scaled, keys, values_t, virt_ids.reshape(nblocks, BLK), values_wide, m0, sent
    )
    sent, third = hand_round(2, [end2, middle1], [state[1]], planes)
    state = phase(2, [first], slots, state, [sent, second, *halo_rows], big=True)
    halo_cols = [
        lax.ppermute(part, "col", steps)
        for part, steps in zip(
            lax.optimization_barrier((feats[:, -1], feats[:, 0], state[1]))[:2],
            (to_next_col, to_prev_col),
        )
    ]
    state = phase(3, [second], slots, state, [])
    sent, fourth = hand_round(3, [end3, middle2], [state[1]])
    layer_parts = third[:, capacity * BLK :, :].astype(jnp.float32)
    layer_parts = layer_parts.reshape(peers, NVIRT * H, 4, 2 * HD)
    layer_part = merge(layer_parts[:, :, 0] + layer_parts[:, :, 1] + layer_parts[:, :, 2])
    around_parts = [layer_part] + [
        lax.ppermute(layer_part, "outer", [((z + turn) % LAYERS, z) for z in range(LAYERS)])
        for turn in range(1, LAYERS)
    ]
    halo = halo_rows + halo_cols
    halo_slots = 3 * blocks_y + 2 * blocks_x
    state = phase(1, halo, halo_slots, state, [sent, third], big=True)
    state = phase(4, [third], slots, state, [*around_parts[1:]])
    node_out = phase(5, [fourth], slots, state, [], (feats.reshape(nblocks, BLK, D), w_out))
    parts = jnp.stack(
        [
            pick(layer, [around_parts[(origin - z) % LAYERS] for z in range(LAYERS)])
            for origin in range(LAYERS)
        ]
    )

    own_score = (
        jnp.sum(
            (virtual_query.astype(jnp.float32) * virtual_keys.astype(jnp.float32)).reshape(
                NVIRT, H, HD
            ),
            axis=-1,
        )
        * scale
    ).reshape(NVIRT * H)
    part_top = parts[:, :, HD]
    part_total = parts[:, :, HD + HD // 2]
    final_top = jnp.maximum(jnp.max(part_top, axis=0), own_score)
    rescale = jnp.exp(part_top - final_top)
    own_share = jnp.exp(own_score - final_top)
    total = jnp.sum(part_total * rescale, axis=0) + own_share
    accum = jnp.sum(parts[:, :, :HD] * rescale[..., None], axis=0)
    accum = accum + own_share[:, None] * virtual_values.astype(jnp.float32).reshape(NVIRT * H, HD)
    virtual_context = (accum / total[:, None]).astype(jnp.bfloat16).reshape(NVIRT, D)
    virt_out = virt_emb.astype(jnp.float32) + jnp.dot(
        virtual_context, w_out, preferred_element_type=jnp.float32
    )
    return (node_out.reshape(feats.shape), virt_out)


def solution(mesh):
    inner = mesh.shape["row"] // LAYERS
    split = Mesh(mesh.devices.reshape(LAYERS, inner, mesh.shape["col"]), AXES)
    rows = ("outer", "inner")
    return jax.shard_map(
        shards,
        mesh=split,
        in_specs=(
            P(rows, "col", None, None),
            P(),
            P(),
            P(),
            P(),
            P(),
            P(rows, "col", None),
            P(rows, "col", None),
            P(rows, "col", None),
        ),
        out_specs=(P(rows, "col", None, None), P()),
        check_vma=False,
    )
```
